32 devices in a mesh: pencil: 8 (over z, y), depth: 4 (over x, core).
Axes of the slice: x: 2, y: 2, z: 4, core: 2. Of those that a mesh axis runs over, the one named last changes fastest.
Arguments:
- currents: float32 [2, 24576], P(None, ('pencil', 'depth')), may hold values from -6 to 6
- stencil_cells: int32 [2, 24576], P(None, ('pencil', 'depth')), may hold values from 0 to 2044, as said below
- stencil_weights: float32 [16, 24576], P(None, ('pencil', 'depth')), may hold values from -3 to 3
- soil: float32 [2, 2], replicated, may hold values from 0.3 to 2
- near_pairs: int32 [3, 384], P(None, ('pencil', 'depth')), may hold values from 0 to 17, as said below
- corrections: float32 [384, 2, 128, 128], P(('pencil', 'depth')), may hold values from -0.5 to 0.5
Outputs:
- potentials: float32 [2, 24576], P(None, ('pencil', 'depth'))
The draws below stay inside these ranges and needn't reach their ends.
Inputs may be any that keep to these rules, and one draw needn't show every extreme that they name: `stencil_cells`: A segment's 16 cells form a 4 x 4 patch in one layer of its device's block: row 0 gives layer * 256 + r with r <= 252, row 1 the first column, at most 2044. `near_pairs`: row 0 holds target blocks below 6; row 1 holds source slots below 18, never naming a device beyond either end of the pencil axis; row 2 holds live flags 0 or 1, the live slots of a device come first, every device has at least one live slot, and some device has all 12 live.
All inputs are finite; a program needn't handle non-finite values.
Results may differ from the reference program's by a relative error of at most 0.00005.
Values sent between devices are 32-bit elements; how exact they have to be, the bound alone decides.
No kernel may reach another device: no remote copies, remote signals or barrier semaphores. Data moves between devices by JAX's collectives and lax.ppermute only.
A program may use at most 192 MiB of HBM per device.

```python
import math
import jax
import jax.numpy as jnp
from jax import lax

GX = 2048
GY = 2048
ZL = 8
SEG_DEV = 768
BS = 128
STEN = 16
PAIRS = 12
PENCILS = 8
DEPTHS = 4
GROUPS = 32
LAY = 2
RX = 256
NBLK = 6
SEGMENTS = 24576
ALLPAIRS = 384
N_DEPTH = 4


def draw_stencil_cells(key, part):
    total = SEG_DEV * GROUPS
    key_layer, key_row, key_column = jax.random.split(key, 3)
    layer_ids = jax.random.randint(key_layer, (total,), 0, LAY)
    row_ids = jax.random.randint(key_row, (total,), 0, RX - 3)
    column_ids = jax.random.randint(key_column, (total,), 0, GY - 3)
    local_ids = jnp.arange(total, dtype=jnp.int32) % SEG_DEV
    layer_ids = jnp.where(local_ids == 0, LAY - 1, jnp.where(local_ids == 1, 0, layer_ids))
    row_ids = jnp.where(local_ids == 0, RX - 4, jnp.where(local_ids == 1, 0, row_ids))
    column_ids = jnp.where(local_ids == 0, GY - 4, jnp.where(local_ids == 1, 0, column_ids))
    return jnp.stack([layer_ids * RX + row_ids, column_ids]).astype(jnp.int32)


def draw_near_pairs(key, part):
    total = GROUPS * PAIRS
    key_target, key_offset, key_block, key_count = jax.random.split(key, 4)
    slot_ids = jnp.arange(total, dtype=jnp.int32)
    device_ids = slot_ids // PAIRS
    pencil_ids = device_ids // DEPTHS
    local_ids = slot_ids % PAIRS
    targets = jax.random.randint(key_target, (total,), 0, NBLK)
    offsets = jax.random.randint(key_offset, (total,), 0, 3) - 1
    lowest = jnp.where(pencil_ids > 0, -1, 0)
    highest = jnp.where(pencil_ids < PENCILS - 1, 1, 0)
    offsets = jnp.clip(offsets, lowest, highest)
    source_blocks = jax.random.randint(key_block, (total,), 0, NBLK)
    at_top = (local_ids == 0) & (pencil_ids < PENCILS - 1)
    at_bottom = (local_ids == 1) & (pencil_ids > 0)
    targets = jnp.where(at_top, NBLK - 1, jnp.where(at_bottom, 0, targets))
    offsets = jnp.where(at_top, 1, jnp.where(at_bottom, -1, offsets))
    source_blocks = jnp.where(at_top, NBLK - 1, jnp.where(at_bottom, 0, source_blocks))
    sources = (offsets + 1) * NBLK + source_blocks
    counts = jax.random.randint(key_count, (GROUPS,), (PAIRS + 2) // 3, PAIRS + 1)
    counts = jnp.where(jnp.arange(GROUPS, dtype=jnp.int32) == 0, PAIRS, counts)
    live = (local_ids < counts[device_ids]).astype(jnp.int32)
    return jnp.stack([targets, sources, live]).astype(jnp.int32)


def block_levels(own_key, extent, shards, least, top_value):
    factor_of, own = 1.0, jax.random.fold_in(own_key, 6)
    for dim, shards_of in shards:
        draws = jnp.exp(jax.random.uniform(jax.random.fold_in(own, dim), (shards_of,), jnp.float32, least / len(shards), top_value / len(shards)))
        factor_of = factor_of * jnp.repeat(draws, extent[dim] // shards_of).reshape([-1 if axis == dim else 1 for axis in range(len(extent))])
    return factor_of


def centred(stream_key, extent, spread, reach, pieces=(), kind=jnp.bfloat16):
    gain = block_levels(stream_key, extent, pieces, -0.22, 0.18) if pieces else 1.0
    values = jax.random.normal(stream_key, extent, jnp.float32) * spread * gain
    return jnp.minimum(jnp.maximum(values, -reach), reach).astype(kind)


def setup_inputs(seed: int = 0) -> dict:
    arg_keys = jax.random.split(jax.random.key(seed), 7)
    currents = centred(arg_keys[0], (2, SEGMENTS), 1.0, 6.0, ((1, 32),), jnp.float32)
    stencil_cells = draw_stencil_cells(jax.random.fold_in(arg_keys[6], 71), 0)
    stencil_weights = centred(arg_keys[2], (STEN, SEGMENTS), 0.5, 3.0, ((1, 32),), jnp.float32)
    soil = jnp.clip(jax.random.uniform(arg_keys[3], (2, 2), jnp.float32, 0.3, 2.0), 0.3, 2.0)
    near_pairs = draw_near_pairs(jax.random.fold_in(arg_keys[6], 71), 0)
    corrections = centred(arg_keys[5], (ALLPAIRS, 2, BS, BS), BS ** -0.5, 0.5, ((0, 32),), jnp.float32)
    return {"currents": currents, "stencil_cells": stencil_cells, "stencil_weights": stencil_weights, "soil": soil, "near_pairs": near_pairs, "corrections": corrections}


layer_step = 1.0
screening = 0.05

def signed_freq(count, length):
    index = jnp.arange(count, dtype=jnp.int32)
    return jnp.where(index < (length - 1) // 2 + 1, index, index - length).astype(jnp.float32) / length

def reference(currents, stencil_cells, stencil_weights, soil, near_pairs, corrections):
    segment_ids = jnp.arange(SEGMENTS, dtype=jnp.int32)
    device_ids = segment_ids // SEG_DEV
    pencil_ids = device_ids // N_DEPTH
    depth_ids = device_ids % N_DEPTH
    cell_index = jnp.arange(16, dtype=jnp.int32)
    row_step = (cell_index // 4)[:, None]
    col_step = (cell_index % 4)[:, None]
    layer_ids = (stencil_cells[0] // RX)[None, :]
    row_ids = (stencil_cells[0] % RX)[None, :] + row_step
    column_ids = stencil_cells[1][None, :] + col_step
    global_ids = ((depth_ids[None, :] * LAY + layer_ids) * GX + pencil_ids[None, :] * RX + row_ids) * GY + column_ids
    flat_ids = global_ids.reshape(-1).astype(jnp.int32)
    charge_re = jax.ops.segment_sum((stencil_weights * currents[0][None, :]).reshape(-1), flat_ids, num_segments=ZL * GX * GY)
    charge_im = jax.ops.segment_sum((stencil_weights * currents[1][None, :]).reshape(-1), flat_ids, num_segments=ZL * GX * GY)
    charges = (charge_re + 1j * charge_im).reshape(ZL, GX, GY)
    spectrum = jnp.fft.fft2(charges, axes=(1, 2))
    freq_x = signed_freq(GX, GX)
    freq_y = signed_freq(GY, GY)
    kappa = 2.0 * math.pi * jnp.sqrt(freq_x[:, None] ** 2 + freq_y[None, :] ** 2)
    upper = soil[0, 0] + 1j * soil[1, 0]
    lower = soil[0, 1] + 1j * soil[1, 1]
    refl = (lower - upper) / (lower + upper)
    base = 1.0 / (kappa + screening)
    mixed_layers = []
    for layer_out in range(ZL):
        total = jnp.zeros_like(spectrum[0])
        for layer_src in range(ZL):
            rho = upper if layer_src < ZL // 2 else lower
            green = rho * (jnp.exp(-kappa * abs(layer_out - layer_src) * layer_step) + refl * jnp.exp(-kappa * (layer_out + layer_src + 1) * layer_step)) * base
            total = total + green * spectrum[layer_src]
        mixed_layers.append(total)
    grid_potential = jnp.fft.ifft2(jnp.stack(mixed_layers), axes=(1, 2)).reshape(-1)
    far = lax.optimization_barrier(jnp.sum(grid_potential[global_ids] * stencil_weights, axis=0))
    slot_ids = jnp.arange(ALLPAIRS, dtype=jnp.int32)
    owner_ids = slot_ids // PAIRS
    source_devices = owner_ids + (near_pairs[1] // NBLK - 1) * N_DEPTH
    source_blocks = source_devices * NBLK + near_pairs[1] % NBLK
    blocks = currents.reshape(2, SEGMENTS // BS, BS)
    picked_re = blocks[0][source_blocks]
    picked_im = blocks[1][source_blocks]
    out_re = jnp.einsum('pij,pj->pi', corrections[:, 0], picked_re, precision=lax.Precision.HIGHEST) - jnp.einsum('pij,pj->pi', corrections[:, 1], picked_im, precision=lax.Precision.HIGHEST)
    out_im = jnp.einsum('pij,pj->pi', corrections[:, 0], picked_im, precision=lax.Precision.HIGHEST) + jnp.einsum('pij,pj->pi', corrections[:, 1], picked_re, precision=lax.Precision.HIGHEST)
    live = near_pairs[2].astype(jnp.float32)[:, None]
    target_blocks = owner_ids * NBLK + near_pairs[0]
    near_re = jax.ops.segment_sum(out_re * live, target_blocks, num_segments=SEGMENTS // BS).reshape(-1)
    near_im = jax.ops.segment_sum(out_im * live, target_blocks, num_segments=SEGMENTS // BS).reshape(-1)
    far_re = jnp.real(far).astype(jnp.float32)
    far_im = jnp.imag(far).astype(jnp.float32)
    return jnp.stack([far_re + near_re, far_im + near_im])
```

```python
import functools
import math

import jax
import jax.numpy as jnp
import ml_dtypes
import numpy as np
from jax import lax
from jax.experimental import pallas as pl
from jax.experimental.pallas import tpu as pltpu
from jax.sharding import PartitionSpec as P

GX = 2048
GY = 2048
ZL = 8

LANES = 256
RADIX = GX // LANES
FINE = 8
SPAN = 16
COLUMNS = 64
FIELDS = 24
TILE = 16

highest = lax.Precision.HIGHEST
screening = 0.05
f32 = jnp.float32
bf16 = jnp.bfloat16


def product(form, left, right):
    return jnp.einsum(form, left, right, precision=highest)


def halves(value):
    high = value.astype(bf16)
    return high, (value - high.astype(f32)).astype(bf16)


def host_halves(value):
    value = value.astype(np.float32)
    high = value.astype(ml_dtypes.bfloat16)
    return high, (value - high.astype(np.float32)).astype(ml_dtypes.bfloat16)


def column_tables():
    ky = np.arange(GY)[:, None]

    def table(offsets):
        phase = (ky * offsets[None, :] % GY) * (2.0 * math.pi / GY)
        return np.stack([np.cos(phase), -np.sin(phase)], axis=0)

    fine_high, fine_low = host_halves(table(np.arange(SPAN)))
    coarse_high, coarse_low = host_halves(table(FINE * np.arange(GY // FINE)))
    fine = np.concatenate([fine_high, fine_high, fine_low], axis=2)
    coarse = np.concatenate([coarse_high, coarse_low], axis=2)
    return fine, coarse


def transform_tables():
    index = np.arange(LANES)
    phase = (index[:, None] * index[None, :] % LANES) * (2.0 * math.pi / LANES)
    cos, sin = np.cos(phase), np.sin(phase)
    forward = np.block([[cos, -sin], [sin, cos]])
    twist = (np.arange(RADIX)[:, None] * index[None, :]) * (2.0 * math.pi / GX)
    twists = np.stack([np.cos(twist), -np.sin(twist)]).astype(np.float32)
    return np.stack(host_halves(forward)), np.stack(host_halves(forward.T)), twists


def segment_factors(fields, fine_ref, coarse_ref):
    count = fields.shape[1]
    column = fields[19:20].astype(jnp.int32)
    coarse_index = lax.broadcasted_iota(jnp.int32, (GY // FINE, count), 0)
    pick = jnp.where(coarse_index == column // FINE, 1.0, 0.0).astype(bf16)
    coarse = jnp.dot(
        coarse_ref[...], jnp.concatenate([pick, pick], axis=0), preferred_element_type=f32
    )
    fine_index = lax.broadcasted_iota(jnp.int32, (SPAN, count), 0) - column % FINE
    at = [fine_index == offset for offset in range(4)]
    parts = []
    for a in range(4):
        spread = jnp.zeros((SPAN, count), f32)
        for b in range(4):
            spread = jnp.where(at[b], fields[4 * a + b : 4 * a + b + 1], spread)
        high, low = halves(spread)
        parts.append(jnp.concatenate([high, low, high], axis=0))
    fine = jnp.dot(fine_ref[...], jnp.concatenate(parts, axis=1), preferred_element_type=f32)
    fines = [fine[:, a * count : (a + 1) * count] for a in range(4)]
    return coarse, fines


def row_select(fields, total_rows):
    row = fields[18:19].astype(jnp.int32)
    row_index = lax.broadcasted_iota(jnp.int32, (total_rows, fields.shape[1]), 0)
    return jnp.where(row_index == row, 1.0, 0.0).astype(bf16)


def spread_kernel(fields_ref, fine_ref, coarse_ref, out_ref, *, repeats):
    fields = fields_ref[0]
    layers = out_ref.shape[0]
    coarse, fines = segment_factors(fields, fine_ref, coarse_ref)
    current_re, current_im = fields[16:17], fields[17:18]
    phase_re, phase_im = coarse[:COLUMNS], coarse[COLUMNS:]
    wave_re = phase_re * current_re - phase_im * current_im
    wave_im = phase_re * current_im + phase_im * current_re
    parts = []
    for fine in fines:
        fine_re, fine_im = fine[:COLUMNS], fine[COLUMNS:]
        parts.append(halves(wave_re * fine_re - wave_im * fine_im))
        parts.append(halves(wave_re * fine_im + wave_im * fine_re))
    select = row_select(fields, layers * LANES)
    form = (((1,), (1,)), ((), ()))
    spread = sum(
        lax.dot_general(
            jnp.concatenate([part[i] for part in parts], axis=0),
            select,
            form,
            preferred_element_type=f32,
        )
        for i in range(2)
    )
    total = spread[: 2 * COLUMNS]
    for a in range(1, 4):
        total = total + pltpu.roll(spread[2 * COLUMNS * a : 2 * COLUMNS * (a + 1)], a, 1)
    for layer in range(layers):
        piece = total[:, layer * LANES : (layer + 1) * LANES]
        if repeats == 1:
            out_ref[layer] = piece
        else:
            fresh = pl.program_id(2) == 0
            out_ref[layer] = jnp.where(fresh, 0.0, out_ref[layer]) + piece


def sample_kernel(fields_ref, field_ref, fine_ref, coarse_ref, out_ref):
    fields = fields_ref[0]
    layers = field_ref.shape[0]
    total_rows = layers * LANES
    coarse, fines = segment_factors(fields, fine_ref, coarse_ref)
    select = row_select(fields, total_rows)
    field = jnp.concatenate([field_ref[layer] for layer in range(layers)], axis=1)
    parts = [halves(field)]
    for a in range(1, 4):
        parts.append(halves(pltpu.roll(field, total_rows - a, 1)))
    sampled = sum(
        jnp.dot(
            jnp.concatenate([part[i] for part in parts], axis=0),
            select,
            preferred_element_type=f32,
        )
        for i in range(2)
    )
    sum_re, sum_im = 0.0, 0.0
    for a, fine in enumerate(fines):
        fine_re, fine_im = fine[:COLUMNS], fine[COLUMNS:]
        base = 2 * COLUMNS * a
        value_re = sampled[base : base + COLUMNS]
        value_im = sampled[base + COLUMNS : base + 2 * COLUMNS]
        sum_re = sum_re + value_re * fine_re + value_im * fine_im
        sum_im = sum_im + value_im * fine_re - value_re * fine_im
    phase_re, phase_im = coarse[:COLUMNS], coarse[COLUMNS:]
    far_re = jnp.sum(sum_re * phase_re + sum_im * phase_im, axis=0, keepdims=True)
    far_im = jnp.sum(sum_im * phase_re - sum_re * phase_im, axis=0, keepdims=True)
    out_ref[0] = jnp.concatenate([far_re, far_im], axis=0)


def turn(value, step, size, sign):
    real, imag = value
    eighth = step * (8 // size)
    if eighth == 0:
        return value
    if eighth == 2:
        return (-sign * imag, sign * real) if sign > 0 else (imag, -real)
    half = math.sqrt(0.5)
    if eighth == 1:
        if sign > 0:
            return ((real - imag) * half, (real + imag) * half)
        return ((real + imag) * half, (imag - real) * half)
    if sign > 0:
        return ((real + imag) * -half, (real - imag) * half)
    return ((imag - real) * half, (real + imag) * -half)


def butterflies(values, sign):
    size = len(values)
    if size == 1:
        return values
    even = butterflies(values[0::2], sign)
    odd = butterflies(values[1::2], sign)
    low, high = [], []
    for k in range(size // 2):
        moved = turn(odd[k], k, size, sign)
        low.append((even[k][0] + moved[0], even[k][1] + moved[1]))
        high.append((even[k][0] - moved[0], even[k][1] - moved[1]))
    return low + high


def dense(value, matrix_ref):
    high, low = halves(value)
    return (
        jnp.dot(high, matrix_ref[0], preferred_element_type=f32)
        + jnp.dot(low, matrix_ref[0], preferred_element_type=f32)
        + jnp.dot(high, matrix_ref[1], preferred_element_type=f32)
    )


def mix(spec, kappa, keep, soil_ref):
    upper = (soil_ref[0], soil_ref[1])
    lower = (soil_ref[2], soil_ref[3])
    refl_re, refl_im = soil_ref[4], soil_ref[5]
    decay = jnp.exp(-kappa)
    base = jnp.where(keep, 1.0 / (GX * GY) / (kappa + screening), 0.0)
    source = []
    for layer in range(ZL):
        rho_re, rho_im = upper if layer < ZL // 2 else lower
        re, im = spec[layer]
        source.append(((rho_re * re - rho_im * im) * base, (rho_re * im + rho_im * re) * base))
    below = [None] * ZL
    below[ZL - 1] = (jnp.zeros_like(kappa), jnp.zeros_like(kappa))
    for layer in range(ZL - 2, -1, -1):
        below[layer] = tuple(decay * (below[layer + 1][i] + source[layer + 1][i]) for i in range(2))
    surface = tuple(decay * (below[0][i] + source[0][i]) for i in range(2))
    image = (
        refl_re * surface[0] - refl_im * surface[1],
        refl_re * surface[1] + refl_im * surface[0],
    )
    above = source[0]
    mixed = []
    for layer in range(ZL):
        if layer:
            above = tuple(decay * above[i] + source[layer][i] for i in range(2))
            image = tuple(decay * image[i] for i in range(2))
        mixed.append(tuple(above[i] + below[layer][i] + image[i] for i in range(2)))
    return mixed


def mix_kernel(first_ref, soil_ref, spec_ref, forward_ref, inverse_ref, twist_ref, out_ref, *, columns):
    tile = spec_ref.shape[2]
    rows = ZL * tile
    real = spec_ref[:, 0].reshape(rows, GX)
    imag = spec_ref[:, 1].reshape(rows, GX)
    cut = [slice(n * LANES, (n + 1) * LANES) for n in range(RADIX)]
    values = butterflies([(real[:, c], imag[:, c]) for c in cut], -1.0)
    local = pl.program_id(0) * tile + lax.broadcasted_iota(jnp.int32, (tile, LANES), 0)
    keep = local < columns
    ky = first_ref[0] + local
    freq_y = jnp.where(ky < (GY - 1) // 2 + 1, ky, ky - GY).astype(f32) / GY
    inner = lax.broadcasted_iota(jnp.int32, (tile, LANES), 1)
    back = []
    for k in range(RADIX):
        twist_re, twist_im = twist_ref[0, k : k + 1], twist_ref[1, k : k + 1]
        re, im = values[k]
        turned = (re * twist_re - im * twist_im, re * twist_im + im * twist_re) if k else (re, im)
        spectrum = dense(jnp.concatenate(turned, axis=1), forward_ref)
        kx = k + RADIX * inner
        freq_x = jnp.where(kx < (GX - 1) // 2 + 1, kx, kx - GX).astype(f32) / GX
        kappa = 2.0 * math.pi * jnp.sqrt(freq_x * freq_x + freq_y * freq_y)
        spec = [
            (spectrum[s * tile : (s + 1) * tile, :LANES], spectrum[s * tile : (s + 1) * tile, LANES:])
            for s in range(ZL)
        ]
        mixed = mix(spec, kappa, keep, soil_ref)
        stacked = jnp.concatenate([jnp.concatenate(pair, axis=1) for pair in mixed], axis=0)
        field = dense(stacked, inverse_ref)
        re, im = field[:, :LANES], field[:, LANES:]
        turned = (re * twist_re + im * twist_im, im * twist_re - re * twist_im) if k else (re, im)
        back.append(turned)
    values = butterflies(back, 1.0)
    for n in range(RADIX):
        out_ref[:, 0, :, cut[n]] = values[n][0].reshape(ZL, tile, LANES)
        out_ref[:, 1, :, cut[n]] = values[n][1].reshape(ZL, tile, LANES)


def everyone(value, axis):
    count = lax.axis_size(axis)
    copies = jnp.broadcast_to(value[None], (count,) + value.shape)
    return lax.all_to_all(copies, axis, split_axis=0, concat_axis=0, tiled=True)


def near_field(beside, near_pairs, corrections):
    block_size = corrections.shape[2]
    block_count = beside.shape[2] // block_size
    slots = beside.shape[0] * block_count
    blocks = jnp.swapaxes(beside, 0, 1).reshape(2, slots, block_size)
    targets, sources, live = (near_pairs[0], near_pairs[1], near_pairs[2])
    source_select = (sources[:, None] == jnp.arange(slots, dtype=jnp.int32)[None, :]).astype(f32)
    picked = product("pk,ckj->cpj", source_select, blocks)
    piece_re = product("pij,pj->pi", corrections[:, 0], picked[0]) - product(
        "pij,pj->pi", corrections[:, 1], picked[1]
    )
    piece_im = product("pij,pj->pi", corrections[:, 0], picked[1]) + product(
        "pij,pj->pi", corrections[:, 1], picked[0]
    )
    owner = (targets[:, None] == jnp.arange(block_count, dtype=jnp.int32)[None, :]).astype(
        f32
    ) * live.astype(f32)[:, None]
    near = jnp.stack([product("pt,pi->ti", owner, piece_re), product("pt,pi->ti", owner, piece_im)])
    return near.reshape(2, block_count * block_size)


def soil_scalars(soil):
    upper_re, lower_re = (soil[0, 0], soil[0, 1])
    upper_im, lower_im = (soil[1, 0], soil[1, 1])
    denom_re, denom_im = upper_re + lower_re, upper_im + lower_im
    numer_re, numer_im = lower_re - upper_re, lower_im - upper_im
    magnitude = denom_re * denom_re + denom_im * denom_im
    refl_re = (numer_re * denom_re + numer_im * denom_im) / magnitude
    refl_im = (numer_im * denom_re - numer_re * denom_im) / magnitude
    return jnp.stack([upper_re, upper_im, lower_re, lower_im, refl_re, refl_im])


def shards(currents, stencil_cells, stencil_weights, soil, near_pairs, corrections):
    pencils = lax.axis_size("pencil")
    depths = lax.axis_size("depth")
    pencil = lax.axis_index("pencil")
    depth = lax.axis_index("depth")
    segments = currents.shape[1]
    layers = ZL // depths
    rows = GX // pencils
    repeats = LANES // rows
    groups = pencils * depths
    columns = GY // groups
    first = (pencil * depths + depth) * columns

    row = stencil_cells[0] // rows * LANES + pencil % repeats * rows + stencil_cells[0] % rows
    fields = jnp.concatenate(
        [
            stencil_weights,
            currents,
            row[None].astype(f32),
            stencil_cells[1:2].astype(f32),
            jnp.zeros((FIELDS - 20, segments), f32),
        ]
    )
    gathered = everyone(everyone(fields, "pencil"), "depth")

    fine, coarse = column_tables()
    fine = lax.dynamic_slice_in_dim(
        jnp.asarray(np.pad(fine, ((0, 0), (0, COLUMNS), (0, 0)))), first, COLUMNS, axis=1
    ).reshape(2 * COLUMNS, -1)
    coarse = lax.dynamic_slice_in_dim(
        jnp.asarray(np.pad(coarse, ((0, 0), (0, COLUMNS), (0, 0)))), first, COLUMNS, axis=1
    ).reshape(2 * COLUMNS, -1)
    forward, inverse, twists = transform_tables()

    steps = (GX // LANES, depths, repeats)
    fields_spec = pl.BlockSpec(
        (None, 1, FIELDS, segments), lambda p, d, r: (d, p * repeats + r, 0, 0)
    )
    grid_spec = pl.BlockSpec((layers, 2 * COLUMNS, LANES), lambda p, d, r: (d, 0, p))
    fine_spec = pl.BlockSpec(fine.shape, lambda p, d, r: (0, 0))
    coarse_spec = pl.BlockSpec(coarse.shape, lambda p, d, r: (0, 0))
    params = pltpu.CompilerParams(vmem_limit_bytes=48 * 1024 * 1024)
    spread = pl.pallas_call(
        functools.partial(spread_kernel, repeats=repeats),
        grid=steps,
        in_specs=[fields_spec, fine_spec, coarse_spec],
        out_specs=grid_spec,
        out_shape=jax.ShapeDtypeStruct((ZL, 2 * COLUMNS, GX), f32),
        compiler_params=params,
    )(gathered, fine, coarse)
    tile_spec = pl.BlockSpec((ZL, 2, TILE, GX), lambda t: (0, 0, t, 0))
    whole = lambda *shape: pl.BlockSpec(shape, lambda t: (0,) * len(shape))
    mixed = pl.pallas_call(
        functools.partial(mix_kernel, columns=columns),
        grid=(COLUMNS // TILE,),
        in_specs=[
            pl.BlockSpec(memory_space=pltpu.SMEM),
            pl.BlockSpec(memory_space=pltpu.SMEM),
            tile_spec,
            whole(*forward.shape),
            whole(*inverse.shape),
            whole(*twists.shape),
        ],
        out_specs=tile_spec,
        out_shape=jax.ShapeDtypeStruct((ZL, 2, COLUMNS, GX), f32),
        compiler_params=params,
    )(
        first.astype(jnp.int32).reshape(1),
        soil_scalars(soil),
        spread.reshape(ZL, 2, COLUMNS, GX),
        jnp.asarray(forward),
        jnp.asarray(inverse),
        jnp.asarray(twists),
    )
    partial = pl.pallas_call(
        sample_kernel,
        grid=steps,
        in_specs=[fields_spec, grid_spec, fine_spec, coarse_spec],
        out_specs=pl.BlockSpec(
            (1, 2, segments), lambda p, d, r: ((p * repeats + r) * depths + d, 0, 0)
        ),
        out_shape=jax.ShapeDtypeStruct((groups, 2, segments), f32),
        compiler_params=params,
    )(gathered, mixed.reshape(ZL, 2 * COLUMNS, GX), fine, coarse)
    arrived = lax.all_to_all(partial, ("pencil", "depth"), split_axis=0, concat_axis=0, tiled=True)
    far = jnp.sum(arrived, axis=0)

    own = lax.dynamic_index_in_dim(gathered, depth, axis=0, keepdims=False)
    beside = jnp.stack(
        [
            lax.dynamic_index_in_dim(
                own[:, 16:18], jnp.clip(pencil + step, 0, pencils - 1), axis=0, keepdims=False
            )
            for step in (-1, 0, 1)
        ]
    )
    return far + near_field(beside, near_pairs, corrections)


def solution(mesh):
    return jax.shard_map(
        shards,
        mesh=mesh,
        in_specs=(
            P(None, ("pencil", "depth")),
            P(None, ("pencil", "depth")),
            P(None, ("pencil", "depth")),
            P(),
            P(None, ("pencil", "depth")),
            P(("pencil", "depth"), None, None, None),
        ),
        out_specs=P(None, ("pencil", "depth")),
        check_vma=False,
    )
```

```python
import functools
import math

import jax
import jax.numpy as jnp
import ml_dtypes
import numpy as np
from jax import lax
from jax.experimental import pallas as pl
from jax.experimental.pallas import tpu as pltpu
from jax.sharding import PartitionSpec as P

GX = 2048
GY = 2048
ZL = 8

LANES = 256
INNER = 128
RADIX = GX // INNER
FINE = 8
SPAN = 16
COLUMNS = 64
FIELDS = 24
TILE = 16

highest = lax.Precision.HIGHEST
screening = 0.05
f32 = jnp.float32
bf16 = jnp.bfloat16


def product(form, left, right):
    return jnp.einsum(form, left, right, precision=highest)


def halves(value):
    high = value.astype(bf16)
    return high, (value - high.astype(f32)).astype(bf16)


def host_halves(value):
    value = value.astype(np.float32)
    high = value.astype(ml_dtypes.bfloat16)
    return high, (value - high.astype(np.float32)).astype(ml_dtypes.bfloat16)


def column_tables():
    ky = np.arange(GY)[:, None]

    def table(offsets):
        phase = (ky * offsets[None, :] % GY) * (2.0 * math.pi / GY)
        return np.stack([np.cos(phase), -np.sin(phase)], axis=0)

    fine_high, fine_low = host_halves(table(np.arange(SPAN)))
    coarse_high, coarse_low = host_halves(table(FINE * np.arange(GY // FINE)))
    fine = np.concatenate([fine_high, fine_high, fine_low], axis=2)
    coarse = np.concatenate([coarse_high, coarse_low], axis=2)
    return fine, coarse


def transform_tables():
    index = np.arange(INNER)
    phase = (index[:, None] * index[None, :] % INNER) * (2.0 * math.pi / INNER)
    cos, sin = np.cos(phase), np.sin(phase)
    forward = np.block([[cos, -sin], [sin, cos]])
    twist = (np.arange(RADIX)[:, None] * index[None, :]) * (2.0 * math.pi / GX)
    twists = np.stack([np.cos(twist), -np.sin(twist)]).astype(np.float32)
    return np.stack(host_halves(forward)), np.stack(host_halves(forward.T)), twists


def one_hot(index, size):
    candidate = lax.broadcasted_iota(jnp.int16, (size, index.shape[1]), 0)
    return jnp.where(candidate == index.astype(jnp.int16), bf16(1), bf16(0))


def segment_factors(fields, fine_ref, coarse_ref):
    count = fields.shape[1]
    column = fields[19:20].astype(jnp.int32)
    pick = one_hot(column // FINE, GY // FINE)
    coarse = jnp.dot(
        coarse_ref[...], jnp.concatenate([pick, pick], axis=0), preferred_element_type=f32
    )
    fine_index = lax.broadcasted_iota(jnp.int32, (SPAN, count), 0) - column % FINE
    at = [fine_index == offset for offset in range(4)]
    parts = []
    for a in range(4):
        spread = jnp.zeros((SPAN, count), f32)
        for b in range(4):
            spread = jnp.where(at[b], fields[4 * a + b : 4 * a + b + 1], spread)
        high, low = halves(spread)
        parts.append(jnp.concatenate([high, low, high], axis=0))
    fine = jnp.dot(fine_ref[...], jnp.concatenate(parts, axis=1), preferred_element_type=f32)
    fines = [fine[:, a * count : (a + 1) * count] for a in range(4)]
    return coarse, fines


def spread_kernel(place_ref, before_ref, fields_ref, fine_ref, coarse_ref, out_ref, *, repeats):
    fields = fields_ref[0]
    layers = out_ref.shape[0]
    coarse, fines = segment_factors(fields, fine_ref, coarse_ref)
    current_re, current_im = fields[16:17], fields[17:18]
    phase_re, phase_im = coarse[:COLUMNS], coarse[COLUMNS:]
    wave_re = phase_re * current_re - phase_im * current_im
    wave_im = phase_re * current_im + phase_im * current_re
    parts = []
    for fine in fines:
        fine_re, fine_im = fine[:COLUMNS], fine[COLUMNS:]
        parts.append(halves(wave_re * fine_re - wave_im * fine_im))
        parts.append(halves(wave_re * fine_im + wave_im * fine_re))
    factors = jnp.concatenate([part[i] for i in range(2) for part in parts], axis=0)
    select = one_hot(fields[18:19].astype(jnp.int32), layers * LANES)
    form = (((1,), (1,)), ((), ()))
    spread = lax.dot_general(factors, select, form, preferred_element_type=f32)
    spread = spread[: 8 * COLUMNS] + spread[8 * COLUMNS :]
    total = spread[: 2 * COLUMNS]
    for a in range(1, 4):
        total = total + pltpu.roll(spread[2 * COLUMNS * a : 2 * COLUMNS * (a + 1)], a, 1)
    for layer in range(layers):
        piece = total[:, layer * LANES : (layer + 1) * LANES]
        if repeats == 1:
            out_ref[layer] = piece
        else:
            fresh = pl.program_id(0) % min(repeats, pl.num_programs(0)) == 0
            out_ref[layer] = jnp.where(fresh, before_ref[layer], out_ref[layer]) + piece


def sample_kernel(place_ref, before_ref, fields_ref, field_ref, fine_ref, coarse_ref, out_ref):
    fields = fields_ref[0]
    layers = field_ref.shape[0]
    total_rows = layers * LANES
    coarse, fines = segment_factors(fields, fine_ref, coarse_ref)
    select = one_hot(fields[18:19].astype(jnp.int32), total_rows)
    field = jnp.concatenate([field_ref[layer] for layer in range(layers)], axis=1)
    parts = [halves(field)]
    for a in range(1, 4):
        parts.append(halves(pltpu.roll(field, total_rows - a, 1)))
    factors = jnp.concatenate([part[i] for i in range(2) for part in parts], axis=0)
    sampled = jnp.dot(factors, select, preferred_element_type=f32)
    sampled = sampled[: 8 * COLUMNS] + sampled[8 * COLUMNS :]
    sum_re, sum_im = 0.0, 0.0
    for a, fine in enumerate(fines):
        fine_re, fine_im = fine[:COLUMNS], fine[COLUMNS:]
        base = 2 * COLUMNS * a
        value_re = sampled[base : base + COLUMNS]
        value_im = sampled[base + COLUMNS : base + 2 * COLUMNS]
        sum_re = sum_re + value_re * fine_re + value_im * fine_im
        sum_im = sum_im + value_im * fine_re - value_re * fine_im
    phase_re, phase_im = coarse[:COLUMNS], coarse[COLUMNS:]
    far_re = jnp.sum(sum_re * phase_re + sum_im * phase_im, axis=0, keepdims=True)
    far_im = jnp.sum(sum_im * phase_re - sum_re * phase_im, axis=0, keepdims=True)
    out_ref[0] = jnp.concatenate([far_re, far_im], axis=0)


def turn(value, step, size, sign):
    real, imag = value
    if step == 0:
        return value
    if 4 * step == size:
        return (-imag, real) if sign > 0 else (imag, -real)
    half = math.sqrt(0.5)
    if 8 * step == size:
        if sign > 0:
            return ((real - imag) * half, (real + imag) * half)
        return ((real + imag) * half, (imag - real) * half)
    cos = math.cos(2.0 * math.pi * step / size)
    sin = sign * math.sin(2.0 * math.pi * step / size)
    return (real * cos - imag * sin, real * sin + imag * cos)


def butterflies(values, sign):
    size = len(values)
    if size == 1:
        return values
    even = butterflies(values[0::2], sign)
    odd = butterflies(values[1::2], sign)
    low, high = [], []
    for k in range(size // 2):
        moved = turn(odd[k], k, size, sign)
        low.append((even[k][0] + moved[0], even[k][1] + moved[1]))
        high.append((even[k][0] - moved[0], even[k][1] - moved[1]))
    return low + high


def dense(value, matrix_ref):
    high, low = halves(value)
    return (
        jnp.dot(high, matrix_ref[0], preferred_element_type=f32)
        + jnp.dot(low, matrix_ref[0], preferred_element_type=f32)
        + jnp.dot(high, matrix_ref[1], preferred_element_type=f32)
    )


def mix(spec, kappa, keep, soil_ref, reflection):
    upper = (soil_ref[0, 0], soil_ref[1, 0])
    lower = (soil_ref[0, 1], soil_ref[1, 1])
    decay = jnp.exp(-kappa)
    base = jnp.where(keep, 1.0 / (GX * GY) / (kappa + screening), 0.0)
    source = []
    for layer in range(ZL):
        rho_re, rho_im = upper if layer < ZL // 2 else lower
        re, im = spec[layer]
        source.append(((rho_re * re - rho_im * im) * base, (rho_re * im + rho_im * re) * base))
    below = [None] * ZL
    below[ZL - 1] = (jnp.zeros_like(kappa), jnp.zeros_like(kappa))
    for layer in range(ZL - 2, -1, -1):
        below[layer] = tuple(decay * (below[layer + 1][i] + source[layer + 1][i]) for i in range(2))
    surface = tuple(decay * (below[0][i] + source[0][i]) for i in range(2))
    image = (
        reflection[0] * surface[0] - reflection[1] * surface[1],
        reflection[0] * surface[1] + reflection[1] * surface[0],
    )
    above = source[0]
    mixed = []
    for layer in range(ZL):
        if layer:
            above = tuple(decay * above[i] + source[layer][i] for i in range(2))
            image = tuple(decay * image[i] for i in range(2))
        mixed.append(tuple(above[i] + below[layer][i] + image[i] for i in range(2)))
    return mixed


def reflect(soil_ref, shape):
    upper_re, lower_re = (jnp.full(shape, soil_ref[0, i], f32) for i in range(2))
    upper_im, lower_im = (jnp.full(shape, soil_ref[1, i], f32) for i in range(2))
    denom_re, denom_im = upper_re + lower_re, upper_im + lower_im
    numer_re, numer_im = lower_re - upper_re, lower_im - upper_im
    magnitude = denom_re * denom_re + denom_im * denom_im
    return (
        (numer_re * denom_re + numer_im * denom_im) / magnitude,
        (numer_im * denom_re - numer_re * denom_im) / magnitude,
    )


def mix_kernel(place_ref, soil_ref, spec_ref, forward_ref, inverse_ref, twist_ref, out_ref, *, columns):
    tile = spec_ref.shape[2]
    rows = ZL * tile
    real = spec_ref[:, 0].reshape(rows, GX)
    imag = spec_ref[:, 1].reshape(rows, GX)
    cut = [slice(n * INNER, (n + 1) * INNER) for n in range(RADIX)]
    values = butterflies([(real[:, c], imag[:, c]) for c in cut], -1.0)
    local = pl.program_id(0) * tile + lax.broadcasted_iota(jnp.int32, (tile, INNER), 0)
    keep = local < columns
    ky = place_ref[2] + local
    reflection = reflect(soil_ref, (tile, INNER))
    freq_y = jnp.where(ky < (GY - 1) // 2 + 1, ky, ky - GY).astype(f32) / GY
    inner = lax.broadcasted_iota(jnp.int32, (tile, INNER), 1)
    back = []
    for k in range(RADIX):
        twist_re, twist_im = twist_ref[0, k : k + 1], twist_ref[1, k : k + 1]
        re, im = values[k]
        turned = (re * twist_re - im * twist_im, re * twist_im + im * twist_re) if k else (re, im)
        spectrum = dense(jnp.concatenate(turned, axis=1), forward_ref)
        kx = k + RADIX * inner
        freq_x = jnp.where(kx < (GX - 1) // 2 + 1, kx, kx - GX).astype(f32) / GX
        kappa = 2.0 * math.pi * jnp.sqrt(freq_x * freq_x + freq_y * freq_y)
        spec = [
            (spectrum[s * tile : (s + 1) * tile, :INNER], spectrum[s * tile : (s + 1) * tile, INNER:])
            for s in range(ZL)
        ]
        mixed = mix(spec, kappa, keep, soil_ref, reflection)
        stacked = jnp.concatenate([jnp.concatenate(pair, axis=1) for pair in mixed], axis=0)
        field = dense(stacked, inverse_ref)
        re, im = field[:, :INNER], field[:, INNER:]
        turned = (re * twist_re + im * twist_im, im * twist_re - re * twist_im) if k else (re, im)
        back.append(turned)
    values = butterflies(back, 1.0)
    for n in range(RADIX):
        out_ref[:, 0, :, cut[n]] = values[n][0].reshape(ZL, tile, INNER)
        out_ref[:, 1, :, cut[n]] = values[n][1].reshape(ZL, tile, INNER)


def partner(value, axis, step):
    count = lax.axis_size(axis)
    return lax.ppermute(value, axis, [(i, i ^ step) for i in range(count)])


def near_field(beside, near_pairs, corrections):
    block_size = corrections.shape[2]
    block_count = beside.shape[2] // block_size
    slots = beside.shape[0] * block_count
    blocks = jnp.swapaxes(beside, 0, 1).reshape(2, slots, block_size)
    targets, sources, live = (near_pairs[0], near_pairs[1], near_pairs[2])
    source_select = (sources[:, None] == jnp.arange(slots, dtype=jnp.int32)[None, :]).astype(f32)
    picked = product("pk,ckj->cpj", source_select, blocks)
    piece_re = product("pij,pj->pi", corrections[:, 0], picked[0]) - product(
        "pij,pj->pi", corrections[:, 1], picked[1]
    )
    piece_im = product("pij,pj->pi", corrections[:, 0], picked[1]) + product(
        "pij,pj->pi", corrections[:, 1], picked[0]
    )
    owner = (targets[:, None] == jnp.arange(block_count, dtype=jnp.int32)[None, :]).astype(
        f32
    ) * live.astype(f32)[:, None]
    near = jnp.stack([product("pt,pi->ti", owner, piece_re), product("pt,pi->ti", owner, piece_im)])
    return near.reshape(2, block_count * block_size)


def shards(currents, stencil_cells, stencil_weights, soil, near_pairs, corrections):
    pencils = lax.axis_size("pencil")
    depths = lax.axis_size("depth")
    pencil = lax.axis_index("pencil")
    depth = lax.axis_index("depth")
    segments = currents.shape[1]
    layers = ZL // depths
    rows = GX // pencils
    repeats = LANES // rows
    groups = pencils * depths
    columns = GY // groups
    first = (pencil * depths + depth) * columns

    row = stencil_cells[0] // rows * LANES + pencil % repeats * rows + stencil_cells[0] % rows
    fields = jnp.concatenate(
        [
            stencil_weights,
            currents,
            row[None].astype(f32),
            stencil_cells[1:2].astype(f32),
            jnp.zeros((FIELDS - 20, segments), f32),
        ]
    )
    bits = [1 << i for i in range(pencils.bit_length() - 1)]
    if repeats == 1:
        bits = bits[::-1]
    place = jnp.stack([pencil, depth, first]).astype(jnp.int32)

    def offset(index):
        return sum((index >> j & 1) * bit for j, bit in enumerate(bits))


    fine, coarse = column_tables()
    fine = lax.dynamic_slice_in_dim(
        jnp.asarray(np.pad(fine, ((0, 0), (0, COLUMNS), (0, 0)))), first, COLUMNS, axis=1
    ).reshape(2 * COLUMNS, -1)
    coarse = lax.dynamic_slice_in_dim(
        jnp.asarray(np.pad(coarse, ((0, 0), (0, COLUMNS), (0, 0)))), first, COLUMNS, axis=1
    ).reshape(2 * COLUMNS, -1)
    forward, inverse, twists = transform_tables()
    params = pltpu.CompilerParams(vmem_limit_bytes=48 * 1024 * 1024)
    fields_spec = pl.BlockSpec((1, FIELDS, segments), lambda i, place: (i, 0, 0))

    def region(begin, step):
        return pl.BlockSpec(
            (layers, 2 * COLUMNS, LANES),
            lambda i, place: (place[1] ^ step, 0, (place[0] ^ offset(begin + i)) // repeats),
        )

    fine_spec = pl.BlockSpec(fine.shape, lambda i, place: (0, 0))
    coarse_spec = pl.BlockSpec(coarse.shape, lambda i, place: (0, 0))
    anywhere = pl.BlockSpec(memory_space=pl.ANY)

    def cost(blocks):
        return pl.CostEstimate(
            flops=blocks * 2_000_000_000, bytes_accessed=blocks * 600_000, transcendentals=0
        )

    def spread(grid, chunk, begin, step):
        fresh = grid is None
        if fresh and repeats > 1:
            grid, fresh = jnp.zeros((ZL, 2 * COLUMNS, GX), f32), False
        before = jnp.zeros((8, 128), f32) if fresh else grid
        return pl.pallas_call(
            functools.partial(spread_kernel, repeats=repeats),
            grid_spec=pltpu.PrefetchScalarGridSpec(
                num_scalar_prefetch=1,
                grid=(chunk.shape[0],),
                in_specs=[
                    anywhere if repeats == 1 else region(begin, step),
                    fields_spec,
                    fine_spec,
                    coarse_spec,
                ],
                out_specs=region(begin, step),
            ),
            out_shape=jax.ShapeDtypeStruct((ZL, 2 * COLUMNS, GX), f32),
            input_output_aliases={} if fresh else {1: 0},
            compiler_params=params,
            cost_estimate=cost(chunk.shape[0]),
        )(place, before, chunk, fine, coarse)

    ends = [(i, i + 1) for i in range(pencils - 1)]
    beside = jnp.stack(
        [
            lax.ppermute(currents, "pencil", ends),
            currents,
            lax.ppermute(currents, "pencil", [(j, i) for i, j in ends]),
        ]
    )
    own, grid = fields[None], None
    for number, bit in enumerate(bits):
        arrived = partner(own, "pencil", bit)
        own = jnp.concatenate([own, arrived])
        if number == 0:
            grid = spread(grid, own, 0, 0)
        else:
            grid = spread(grid, arrived, 1 << number, 0)
    parts = [own]
    for step in range(1, depths):
        low = step & -step
        parts.append(partner(parts[step ^ low], "depth", low))
    near = near_field(beside, near_pairs, corrections)
    near, parts[1] = lax.optimization_barrier((near, parts[1]))
    for step in range(1, depths):
        grid = spread(grid, parts[step], 0, step)

    tile_spec = pl.BlockSpec((ZL, 2, TILE, GX), lambda t: (0, 0, t, 0))
    whole = lambda *shape: pl.BlockSpec(shape, lambda t: (0,) * len(shape))
    mixed = pl.pallas_call(
        functools.partial(mix_kernel, columns=columns),
        grid=(COLUMNS // TILE,),
        in_specs=[
            pl.BlockSpec(memory_space=pltpu.SMEM),
            pl.BlockSpec(memory_space=pltpu.SMEM),
            tile_spec,
            whole(*forward.shape),
            whole(*inverse.shape),
            whole(*twists.shape),
        ],
        out_specs=tile_spec,
        out_shape=jax.ShapeDtypeStruct((ZL, 2, COLUMNS, GX), f32),
        compiler_params=params,
    )(
        place,
        soil,
        grid.reshape(ZL, 2, COLUMNS, GX),
        jnp.asarray(forward),
        jnp.asarray(inverse),
        jnp.asarray(twists),
    ).reshape(ZL, 2 * COLUMNS, GX)
    partial = None
    for step in range(depths):
        partial = pl.pallas_call(
            sample_kernel,
            grid_spec=pltpu.PrefetchScalarGridSpec(
                num_scalar_prefetch=1,
                grid=(pencils,),
                in_specs=[anywhere, fields_spec, region(0, step), fine_spec, coarse_spec],
                out_specs=pl.BlockSpec(
                    (1, 2, segments),
                    lambda i, place, step=step: (
                        (place[0] ^ offset(i)) * depths + (place[1] ^ step),
                        0,
                        0,
                    ),
                ),
            ),
            out_shape=jax.ShapeDtypeStruct((groups, 2, segments), f32),
            input_output_aliases={1: 0} if step else {},
            compiler_params=params,
            cost_estimate=cost(pencils),
        )(
            place,
            partial if step else jnp.zeros((8, 128), f32),
            parts[step],
            mixed,
            fine,
            coarse,
        )
    arrived = lax.all_to_all(partial, ("pencil", "depth"), split_axis=0, concat_axis=0, tiled=True)
    return jnp.sum(arrived, axis=0) + near


def solution(mesh):
    return jax.shard_map(
        shards,
        mesh=mesh,
        in_specs=(
            P(None, ("pencil", "depth")),
            P(None, ("pencil", "depth")),
            P(None, ("pencil", "depth")),
            P(),
            P(None, ("pencil", "depth")),
            P(("pencil", "depth"), None, None, None),
        ),
        out_specs=P(None, ("pencil", "depth")),
        check_vma=False,
    )
```

```python
import functools
import math

import jax
import jax.numpy as jnp
import ml_dtypes
import numpy as np
from jax import lax
from jax.experimental import pallas as pl
from jax.experimental.pallas import tpu as pltpu
from jax.sharding import PartitionSpec as P

GX = 2048
GY = 2048
ZL = 8

LANES = 256
INNER = 128
RADIX = GX // INNER
FINE = 8
SPAN = 16
COLUMNS = 64
FIELDS = 24
CHUNK = 256
REACH = LANES - 3
HOP = 128
TOGETHER = 2
TILE = 16

screening = 0.05
f32 = jnp.float32
bf16 = jnp.bfloat16


def halves(value):
    high = value.astype(bf16)
    return high, (value - high.astype(f32)).astype(bf16)


def host_halves(value):
    value = value.astype(np.float32)
    high = value.astype(ml_dtypes.bfloat16)
    return high, (value - high.astype(np.float32)).astype(ml_dtypes.bfloat16)


def column_tables():
    ky = np.arange(GY)[:, None]

    def table(offsets):
        phase = (ky * offsets[None, :] % GY) * (2.0 * math.pi / GY)
        return np.stack([np.cos(phase), -np.sin(phase)], axis=0)

    fine_high, fine_low = host_halves(table(np.arange(SPAN)))
    coarse_high, coarse_low = host_halves(table(FINE * np.arange(GY // FINE)))
    fine = np.concatenate([fine_high, fine_high, fine_low], axis=2)
    coarse = np.concatenate([coarse_high, coarse_low], axis=2)
    return fine, coarse


def transform_tables():
    index = np.arange(INNER)
    phase = (index[:, None] * index[None, :] % INNER) * (2.0 * math.pi / INNER)
    cos, sin = np.cos(phase), np.sin(phase)
    forward = np.block([[cos, -sin], [sin, cos]])
    twist = (np.arange(RADIX)[:, None] * index[None, :]) * (2.0 * math.pi / GX)
    twists = np.stack([np.cos(twist), -np.sin(twist)]).astype(np.float32)
    return np.stack(host_halves(forward)), np.stack(host_halves(forward.T)), twists


def one_hot(index, size):
    candidate = lax.broadcasted_iota(jnp.int16, (size, index.shape[1]), 0)
    return jnp.where(candidate == index.astype(jnp.int16), bf16(1), bf16(0))


def segment_factors(fields, fine_ref, coarse_ref):
    count = fields.shape[1]
    column = fields[19:20].astype(jnp.int32)
    pick = one_hot(column // FINE, GY // FINE)
    coarse = jnp.dot(
        coarse_ref[...], jnp.concatenate([pick, pick], axis=0), preferred_element_type=f32
    )
    fine_index = lax.broadcasted_iota(jnp.int32, (SPAN, count), 0) - column % FINE
    at = [fine_index == offset for offset in range(4)]
    parts = []
    for a in range(4):
        spread = jnp.zeros((SPAN, count), f32)
        for b in range(4):
            spread = jnp.where(at[b], fields[4 * a + b : 4 * a + b + 1], spread)
        high, low = halves(spread)
        parts.append(jnp.concatenate([high, low, high], axis=0))
    fine = jnp.dot(fine_ref[...], jnp.concatenate(parts, axis=1), preferred_element_type=f32)
    fines = [fine[:, a * count : (a + 1) * count] for a in range(4)]
    return coarse, fines


def thirds(value):
    high = value.astype(bf16)
    rest = value - high.astype(f32)
    middle = rest.astype(bf16)
    return high, middle, (rest - middle.astype(f32)).astype(bf16)


def order_kernel(place_ref, currents_ref, cells_ref, weights_ref, fields_ref, rank_ref, *, rows):
    count = currents_ref.shape[1]
    local = cells_ref[0:1]
    repeats = LANES // rows
    row = local // rows * LANES + place_ref[0] % repeats * rows + local % rows
    lane = lax.broadcasted_iota(jnp.int32, (1, count), 1)
    key = (row * count + lane).astype(f32)
    column = jnp.transpose(jnp.broadcast_to(key, (128, count)))[:, :1]
    rank = jnp.sum(jnp.where(column < key, 1.0, 0.0), axis=0, keepdims=True)
    pick = one_hot(rank.astype(jnp.int32), count)
    values = jnp.concatenate(
        [
            weights_ref[...],
            currents_ref[...],
            row.astype(f32),
            cells_ref[1:2].astype(f32),
            jnp.zeros((FIELDS - 20, count), f32),
        ],
        axis=0,
    )
    ordered = sum(
        lax.dot_general(part, pick, (((1,), (1,)), ((), ())), preferred_element_type=f32)
        for part in thirds(values)
    )
    ends = jnp.zeros((1, count), f32)
    for chunk in range(count // CHUNK):
        for side in range(2):
            at = lane == chunk * CHUNK + side * (CHUNK - 1)
            value = jnp.sum(jnp.where(at, ordered[18:19], 0.0), axis=1, keepdims=True)
            ends = ends + jnp.where(lane == 2 * chunk + side, value, 0.0)
    line = lax.broadcasted_iota(jnp.int32, (FIELDS, count), 0)
    fields_ref[...] = jnp.where(line == 20, ends, ordered)
    rank_ref[...] = rank


def finish_kernel(arrived_ref, near_ref, rank_ref, out_ref):
    far = jnp.sum(arrived_ref[...], axis=0)
    count = far.shape[1]
    pick = one_hot(rank_ref[...].astype(jnp.int32), count)
    padded = jnp.concatenate([far, jnp.zeros((14, count), f32)], axis=0)
    total = sum(jnp.dot(part, pick, preferred_element_type=f32) for part in thirds(padded))
    out_ref[...] = total[:2] + near_ref[...]


def windows(fields_ref, ends_ref, block, total_rows):
    chunks = []
    for chunk in range(fields_ref.shape[2] // CHUNK):
        low = ends_ref[block, 4, 2 * chunk].astype(jnp.int32)
        high = ends_ref[block, 4, 2 * chunk + 1].astype(jnp.int32)
        start = jnp.minimum(low // HOP * HOP, total_rows - LANES)
        more = (jnp.maximum(high + 1 - (start + REACH), 0) + HOP - 1) // HOP
        chunks.append((start, more))

    def window(chunk, number, visit):
        first = isinstance(number, int)
        row = fields_ref[block, 18:19, chunk * CHUNK : (chunk + 1) * CHUNK].astype(jnp.int32)
        begin = pl.multiple_of(chunks[chunk][0] + number * HOP, HOP)
        apart = row - begin
        inside = (apart >= (0 if first else REACH - HOP)) & (apart < REACH)
        visit(chunk, begin, one_hot(jnp.where(inside, apart, -1), LANES), first)

    def begin_all(visit):
        for chunk in range(len(chunks)):
            window(chunk, 0, visit)

    def finish_all(visit):
        @pl.when(sum(more for _, more in chunks) > 0)
        def _():
            for chunk in range(len(chunks)):

                def again(number, carry, chunk=chunk):
                    window(chunk, number, visit)
                    return carry

                lax.fori_loop(1, chunks[chunk][1] + 1, again, 0)

    return begin_all, finish_all


def spread_kernel(
    place_ref, before_ref, fields_ref, ends_ref, fine_ref, coarse_ref, out_ref, *scratch, repeats
):
    layers = out_ref.shape[0]
    half = 8 * COLUMNS
    rest = []
    for block in range(TOGETHER):
        factor_ref, total_ref = scratch[2 * block : 2 * block + 2]
        fields = fields_ref[block]
        coarse, fines = segment_factors(fields, fine_ref, coarse_ref)
        current_re, current_im = fields[16:17], fields[17:18]
        phase_re, phase_im = coarse[:COLUMNS], coarse[COLUMNS:]
        wave_re = phase_re * current_re - phase_im * current_im
        wave_im = phase_re * current_im + phase_im * current_re
        base = 0
        for fine in fines:
            fine_re, fine_im = fine[:COLUMNS], fine[COLUMNS:]
            for value in (
                wave_re * fine_re - wave_im * fine_im,
                wave_re * fine_im + wave_im * fine_re,
            ):
                high, low = halves(value)
                factor_ref[base : base + COLUMNS] = high
                factor_ref[half + base : half + base + COLUMNS] = low
                base += COLUMNS
        total_ref[...] = jnp.zeros_like(total_ref)

        def visit(chunk, begin, select, first, factor_ref=factor_ref, total_ref=total_ref):
            factors = factor_ref[:, chunk * CHUNK : (chunk + 1) * CHUNK]
            form = (((1,), (1,)), ((), ()))
            spread = lax.dot_general(factors, select, form, preferred_element_type=f32)
            spread = spread[:half] + spread[half:]
            total = spread[: 2 * COLUMNS]
            for a in range(1, 4):
                total = total + pltpu.roll(spread[2 * COLUMNS * a : 2 * COLUMNS * (a + 1)], a, 1)
            total_ref[:, pl.ds(begin, LANES)] += total

        begin_all, finish_all = windows(fields_ref, ends_ref, block, layers * LANES)
        begin_all(visit)
        rest.append((finish_all, visit))
    for finish_all, visit in rest:
        finish_all(visit)
    fresh = pl.program_id(0) * TOGETHER % min(repeats, pl.num_programs(0) * TOGETHER) == 0
    for layer in range(layers):
        pieces = [
            scratch[2 * block + 1][:, layer * LANES : (layer + 1) * LANES]
            for block in range(TOGETHER)
        ]
        if repeats == 1:
            for block, piece in enumerate(pieces):
                spot = (place_ref[0] % TOGETHER) ^ block
                out_ref[layer, :, pl.ds(pl.multiple_of(spot * LANES, LANES), LANES)] = piece
        else:
            out_ref[layer] = jnp.where(fresh, before_ref[layer], out_ref[layer]) + sum(pieces)


def sample_kernel(
    place_ref, before_ref, fields_ref, ends_ref, field_ref, fine_ref, coarse_ref, out_ref, *scratch
):
    layers = field_ref.shape[0]
    total_rows = layers * LANES
    half = 8 * COLUMNS
    rest = []
    for block in range(TOGETHER):
        factor_ref, sampled_ref = scratch[2 * block : 2 * block + 2]
        if field_ref.shape[2] == LANES:
            at = pl.ds(0, LANES)
        else:
            spot = (place_ref[0] % TOGETHER) ^ block
            at = pl.ds(pl.multiple_of(spot * LANES, LANES), LANES)
        field = jnp.concatenate([field_ref[layer, :, at] for layer in range(layers)], axis=1)
        for a in range(4):
            moved = pltpu.roll(field, total_rows - a, 1) if a else field
            high, low = halves(moved)
            base = 2 * COLUMNS * a
            factor_ref[base : base + 2 * COLUMNS] = high
            factor_ref[half + base : half + base + 2 * COLUMNS] = low

        def visit(chunk, begin, select, first, factor_ref=factor_ref, sampled_ref=sampled_ref):
            factors = factor_ref[:, pl.ds(begin, LANES)]
            sampled = jnp.dot(factors, select, preferred_element_type=f32)
            sampled = sampled[:half] + sampled[half:]
            at = slice(chunk * CHUNK, (chunk + 1) * CHUNK)
            sampled_ref[:, at] = sampled if first else sampled_ref[:, at] + sampled

        begin_all, finish_all = windows(fields_ref, ends_ref, block, total_rows)
        begin_all(visit)
        rest.append((finish_all, visit))
    for finish_all, visit in rest:
        finish_all(visit)
    for block in range(TOGETHER):
        sampled_ref = scratch[2 * block + 1]
        coarse, fines = segment_factors(fields_ref[block], fine_ref, coarse_ref)
        sum_re, sum_im = 0.0, 0.0
        for a, fine in enumerate(fines):
            fine_re, fine_im = fine[:COLUMNS], fine[COLUMNS:]
            base = 2 * COLUMNS * a
            value_re = sampled_ref[base : base + COLUMNS]
            value_im = sampled_ref[base + COLUMNS : base + 2 * COLUMNS]
            sum_re = sum_re + value_re * fine_re + value_im * fine_im
            sum_im = sum_im + value_im * fine_re - value_re * fine_im
        phase_re, phase_im = coarse[:COLUMNS], coarse[COLUMNS:]
        far_re = jnp.sum(sum_re * phase_re + sum_im * phase_im, axis=0, keepdims=True)
        far_im = jnp.sum(sum_im * phase_re - sum_re * phase_im, axis=0, keepdims=True)
        spot = (place_ref[0] % TOGETHER) ^ block
        out_ref[pl.ds(spot, 1)] = jnp.concatenate([far_re, far_im], axis=0).reshape(
            (1,) + out_ref.shape[1:]
        )


def turn(value, step, size, sign):
    real, imag = value
    if step == 0:
        return value
    if 4 * step == size:
        return (-imag, real) if sign > 0 else (imag, -real)
    half = math.sqrt(0.5)
    if 8 * step == size:
        if sign > 0:
            return ((real - imag) * half, (real + imag) * half)
        return ((real + imag) * half, (imag - real) * half)
    cos = math.cos(2.0 * math.pi * step / size)
    sin = sign * math.sin(2.0 * math.pi * step / size)
    return (real * cos - imag * sin, real * sin + imag * cos)


def butterflies(values, sign):
    size = len(values)
    if size == 1:
        return values
    even = butterflies(values[0::2], sign)
    odd = butterflies(values[1::2], sign)
    low, high = [], []
    for k in range(size // 2):
        moved = turn(odd[k], k, size, sign)
        low.append((even[k][0] + moved[0], even[k][1] + moved[1]))
        high.append((even[k][0] - moved[0], even[k][1] - moved[1]))
    return low + high


def dense(value, matrix_ref):
    high, low = halves(value)
    return (
        jnp.dot(high, matrix_ref[0], preferred_element_type=f32)
        + jnp.dot(low, matrix_ref[0], preferred_element_type=f32)
        + jnp.dot(high, matrix_ref[1], preferred_element_type=f32)
    )


def mix(spec, kappa, keep, soil_ref, reflection):
    upper = (soil_ref[0, 0], soil_ref[1, 0])
    lower = (soil_ref[0, 1], soil_ref[1, 1])
    decay = jnp.exp(-kappa)
    base = jnp.where(keep, 1.0 / (GX * GY) / (kappa + screening), 0.0)
    source = []
    for layer in range(ZL):
        rho_re, rho_im = upper if layer < ZL // 2 else lower
        re, im = spec[layer]
        source.append(((rho_re * re - rho_im * im) * base, (rho_re * im + rho_im * re) * base))
    below = [None] * ZL
    below[ZL - 1] = (jnp.zeros_like(kappa), jnp.zeros_like(kappa))
    for layer in range(ZL - 2, -1, -1):
        below[layer] = tuple(decay * (below[layer + 1][i] + source[layer + 1][i]) for i in range(2))
    surface = tuple(decay * (below[0][i] + source[0][i]) for i in range(2))
    image = (
        reflection[0] * surface[0] - reflection[1] * surface[1],
        reflection[0] * surface[1] + reflection[1] * surface[0],
    )
    above = source[0]
    mixed = []
    for layer in range(ZL):
        if layer:
            above = tuple(decay * above[i] + source[layer][i] for i in range(2))
            image = tuple(decay * image[i] for i in range(2))
        mixed.append(tuple(above[i] + below[layer][i] + image[i] for i in range(2)))
    return mixed


def reflect(soil_ref, shape):
    upper_re, lower_re = (jnp.full(shape, soil_ref[0, i], f32) for i in range(2))
    upper_im, lower_im = (jnp.full(shape, soil_ref[1, i], f32) for i in range(2))
    denom_re, denom_im = upper_re + lower_re, upper_im + lower_im
    numer_re, numer_im = lower_re - upper_re, lower_im - upper_im
    magnitude = denom_re * denom_re + denom_im * denom_im
    return (
        (numer_re * denom_re + numer_im * denom_im) / magnitude,
        (numer_im * denom_re - numer_re * denom_im) / magnitude,
    )


def mix_kernel(place_ref, soil_ref, spec_ref, forward_ref, inverse_ref, twist_ref, out_ref, *, columns):
    tile = spec_ref.shape[2]
    rows = ZL * tile
    real = spec_ref[:, 0].reshape(rows, GX)
    imag = spec_ref[:, 1].reshape(rows, GX)
    cut = [slice(n * INNER, (n + 1) * INNER) for n in range(RADIX)]
    values = butterflies([(real[:, c], imag[:, c]) for c in cut], -1.0)
    local = pl.program_id(0) * tile + lax.broadcasted_iota(jnp.int32, (tile, INNER), 0)
    keep = local < columns
    ky = place_ref[2] + local
    reflection = reflect(soil_ref, (tile, INNER))
    freq_y = jnp.where(ky < (GY - 1) // 2 + 1, ky, ky - GY).astype(f32) / GY
    inner = lax.broadcasted_iota(jnp.int32, (tile, INNER), 1)
    back = []
    for k in range(RADIX):
        twist_re, twist_im = twist_ref[0, k : k + 1], twist_ref[1, k : k + 1]
        re, im = values[k]
        turned = (re * twist_re - im * twist_im, re * twist_im + im * twist_re) if k else (re, im)
        spectrum = dense(jnp.concatenate(turned, axis=1), forward_ref)
        kx = k + RADIX * inner
        freq_x = jnp.where(kx < (GX - 1) // 2 + 1, kx, kx - GX).astype(f32) / GX
        kappa = 2.0 * math.pi * jnp.sqrt(freq_x * freq_x + freq_y * freq_y)
        spec = [
            (spectrum[s * tile : (s + 1) * tile, :INNER], spectrum[s * tile : (s + 1) * tile, INNER:])
            for s in range(ZL)
        ]
        mixed = mix(spec, kappa, keep, soil_ref, reflection)
        stacked = jnp.concatenate([jnp.concatenate(pair, axis=1) for pair in mixed], axis=0)
        field = dense(stacked, inverse_ref)
        re, im = field[:, :INNER], field[:, INNER:]
        turned = (re * twist_re + im * twist_im, im * twist_re - re * twist_im) if k else (re, im)
        back.append(turned)
    values = butterflies(back, 1.0)
    for n in range(RADIX):
        out_ref[:, 0, :, cut[n]] = values[n][0].reshape(ZL, tile, INNER)
        out_ref[:, 1, :, cut[n]] = values[n][1].reshape(ZL, tile, INNER)


def partner(value, axis, step):
    count = lax.axis_size(axis)
    return lax.ppermute(value, axis, [(i, i ^ step) for i in range(count)])


def near_kernel(pairs_ref, before_ref, own_ref, after_ref, corrections_ref, out_ref, beside_ref):
    slots, _, size, _ = corrections_ref.shape
    blocks = own_ref.shape[1] // size
    for side, ref in enumerate((before_ref, own_ref, after_ref)):
        beside_ref[side] = ref[...]
    out_ref[...] = jnp.zeros_like(out_ref)

    def add(slot, carry):
        target, source = pairs_ref[0, slot], pairs_ref[1, slot]
        live = pairs_ref[2, slot].astype(f32)
        at = pl.ds(pl.multiple_of(source % blocks * size, size), size)
        current = beside_ref[source // blocks, :, at] * live
        real, imag = corrections_ref[slot, 0], corrections_ref[slot, 1]
        piece_re = real * current[0:1] - imag * current[1:2]
        piece_im = real * current[1:2] + imag * current[0:1]
        to = pl.ds(pl.multiple_of(target * size, size), size)
        out_ref[0:1, to] += jnp.sum(jnp.transpose(piece_re), axis=0, keepdims=True)
        out_ref[1:2, to] += jnp.sum(jnp.transpose(piece_im), axis=0, keepdims=True)
        return carry

    lax.fori_loop(0, slots, add, 0)


def shards(currents, stencil_cells, stencil_weights, soil, near_pairs, corrections):
    pencils = lax.axis_size("pencil")
    depths = lax.axis_size("depth")
    pencil = lax.axis_index("pencil")
    depth = lax.axis_index("depth")
    segments = currents.shape[1]
    layers = ZL // depths
    rows = GX // pencils
    repeats = LANES // rows
    groups = pencils * depths
    columns = GY // groups
    first = (pencil * depths + depth) * columns

    bits = [1 << i for i in range(pencils.bit_length() - 1)]
    if repeats == 1:
        bits = bits[:1] + bits[:0:-1]
    place = jnp.stack([pencil, depth, first]).astype(jnp.int32)
    params = pltpu.CompilerParams(vmem_limit_bytes=48 * 1024 * 1024)
    anywhere = pl.BlockSpec(memory_space=pl.ANY)
    scalars = pl.BlockSpec(memory_space=pltpu.SMEM)
    resident = pl.BlockSpec(memory_space=pltpu.VMEM)
    fields, rank = pl.pallas_call(
        functools.partial(order_kernel, rows=rows),
        in_specs=[scalars] + [pl.BlockSpec()] * 3,
        out_specs=[pl.BlockSpec()] * 2,
        out_shape=[
            jax.ShapeDtypeStruct((FIELDS, segments), f32),
            jax.ShapeDtypeStruct((1, segments), f32),
        ],
        compiler_params=params,
    )(place, currents, stencil_cells, stencil_weights)

    def offset(index):
        return sum((index >> j & 1) * bit for j, bit in enumerate(bits))


    fine, coarse = column_tables()
    fine = lax.dynamic_slice_in_dim(
        jnp.asarray(np.pad(fine, ((0, 0), (0, COLUMNS), (0, 0)))), first, COLUMNS, axis=1
    ).reshape(2 * COLUMNS, -1)
    coarse = lax.dynamic_slice_in_dim(
        jnp.asarray(np.pad(coarse, ((0, 0), (0, COLUMNS), (0, 0)))), first, COLUMNS, axis=1
    ).reshape(2 * COLUMNS, -1)
    forward, inverse, twists = transform_tables()
    fields_spec = pl.BlockSpec((TOGETHER, FIELDS, segments), lambda i, place: (i, 0, 0))
    ends_spec = pl.BlockSpec((TOGETHER, 8, 128), lambda i, place: (i, 2, 0), memory_space=pltpu.SMEM)

    wide = TOGETHER if repeats == 1 else 1

    def region(begin, step):
        return pl.BlockSpec(
            (layers, 2 * COLUMNS, LANES * wide),
            lambda i, place: (
                place[1] ^ step,
                0,
                (place[0] ^ offset(begin + TOGETHER * i)) // (repeats * wide),
            ),
        )

    fine_spec = pl.BlockSpec(fine.shape, lambda i, place: (0, 0))
    coarse_spec = pl.BlockSpec(coarse.shape, lambda i, place: (0, 0))

    def cost(blocks):
        return pl.CostEstimate(
            flops=blocks * 2_000_000_000, bytes_accessed=blocks * 600_000, transcendentals=0
        )

    def spread(grid, chunk, begin, step):
        fresh = grid is None
        if fresh and repeats > 1:
            grid, fresh = jnp.zeros((ZL, 2 * COLUMNS, GX), f32), False
        before = jnp.zeros((8, 128), f32) if fresh else grid
        return pl.pallas_call(
            functools.partial(spread_kernel, repeats=repeats),
            grid_spec=pltpu.PrefetchScalarGridSpec(
                num_scalar_prefetch=1,
                grid=(chunk.shape[0] // TOGETHER,),
                in_specs=[
                    anywhere if repeats == 1 else region(begin, step),
                    fields_spec,
                    ends_spec,
                    fine_spec,
                    coarse_spec,
                ],
                out_specs=region(begin, step),
                scratch_shapes=[
                    pltpu.VMEM((16 * COLUMNS, segments), bf16),
                    pltpu.VMEM((2 * COLUMNS, layers * LANES), f32),
                ]
                * TOGETHER,
            ),
            out_shape=jax.ShapeDtypeStruct((ZL, 2 * COLUMNS, GX), f32),
            input_output_aliases={} if fresh else {1: 0},
            compiler_params=params,
            cost_estimate=cost(chunk.shape[0]),
        )(place, before, chunk, chunk, fine, coarse)

    own, grid = fields[None], None
    for number, bit in enumerate(bits):
        arrived = partner(own, "pencil", bit)
        own = jnp.concatenate([own, arrived])
        if number == 0:
            grid = spread(grid, own, 0, 0)
        else:
            grid = spread(grid, arrived, 1 << number, 0)
    late, own = lax.optimization_barrier((currents, own))
    parts = [own]
    for step in range(1, depths):
        low = step & -step
        parts.append(partner(parts[step ^ low], "depth", low))
    ends = [(i, i + 1) for i in range(pencils - 1)]
    near = pl.pallas_call(
        near_kernel,
        in_specs=[scalars] + [pl.BlockSpec()] * 4,
        out_specs=pl.BlockSpec(),
        out_shape=jax.ShapeDtypeStruct((2, segments), f32),
        scratch_shapes=[pltpu.VMEM((3, 2, segments), f32)],
        compiler_params=params,
        cost_estimate=cost(1),
    )(
        near_pairs,
        lax.ppermute(late, "pencil", ends),
        currents,
        lax.ppermute(late, "pencil", [(j, i) for i, j in ends]),
        corrections,
    )
    near, parts[1] = lax.optimization_barrier((near, parts[1]))
    for step in range(1, depths):
        grid = spread(grid, parts[step], 0, step)

    tile_spec = pl.BlockSpec((ZL, 2, TILE, GX), lambda t: (0, 0, t, 0))
    whole = lambda *shape: pl.BlockSpec(shape, lambda t: (0,) * len(shape))
    mixed = pl.pallas_call(
        functools.partial(mix_kernel, columns=columns),
        grid=(COLUMNS // TILE,),
        in_specs=[
            pl.BlockSpec(memory_space=pltpu.SMEM),
            pl.BlockSpec(memory_space=pltpu.SMEM),
            tile_spec,
            whole(*forward.shape),
            whole(*inverse.shape),
            whole(*twists.shape),
        ],
        out_specs=tile_spec,
        out_shape=jax.ShapeDtypeStruct((ZL, 2, COLUMNS, GX), f32),
        compiler_params=params,
    )(
        place,
        soil,
        grid.reshape(ZL, 2, COLUMNS, GX),
        jnp.asarray(forward),
        jnp.asarray(inverse),
        jnp.asarray(twists),
    ).reshape(ZL, 2 * COLUMNS, GX)
    partial = None
    for step in range(depths):
        partial = pl.pallas_call(
            sample_kernel,
            grid_spec=pltpu.PrefetchScalarGridSpec(
                num_scalar_prefetch=1,
                grid=(pencils // TOGETHER,),
                in_specs=[
                    anywhere,
                    fields_spec,
                    ends_spec,
                    region(0, step),
                    fine_spec,
                    coarse_spec,
                ],
                out_specs=pl.BlockSpec(
                    (TOGETHER, None, 2, segments),
                    lambda i, place, step=step: (
                        (place[0] ^ offset(TOGETHER * i)) // TOGETHER,
                        place[1] ^ step,
                        0,
                        0,
                    ),
                ),
                scratch_shapes=[
                    pltpu.VMEM((16 * COLUMNS, layers * LANES), bf16),
                    pltpu.VMEM((8 * COLUMNS, segments), f32),
                ]
                * TOGETHER,
            ),
            out_shape=jax.ShapeDtypeStruct((pencils, depths, 2, segments), f32),
            input_output_aliases={1: 0} if step else {},
            compiler_params=params,
            cost_estimate=cost(pencils),
        )(
            place,
            partial if step else jnp.zeros((8, 128), f32),
            parts[step],
            parts[step],
            mixed,
            fine,
            coarse,
        )
    partial = partial.reshape(groups, 2, segments)
    arrived = lax.all_to_all(partial, ("pencil", "depth"), split_axis=0, concat_axis=0, tiled=True)
    return pl.pallas_call(
        finish_kernel,
        in_specs=[resident, resident, resident],
        out_specs=resident,
        out_shape=jax.ShapeDtypeStruct((2, segments), f32),
        compiler_params=params,
    )(arrived, near, rank)


def solution(mesh):
    return jax.shard_map(
        shards,
        mesh=mesh,
        in_specs=(
            P(None, ("pencil", "depth")),
            P(None, ("pencil", "depth")),
            P(None, ("pencil", "depth")),
            P(),
            P(None, ("pencil", "depth")),
            P(("pencil", "depth"), None, None, None),
        ),
        out_specs=P(None, ("pencil", "depth")),
        check_vma=False,
    )
```

```python
import functools
import math

import jax
import jax.numpy as jnp
import ml_dtypes
import numpy as np
from jax import lax
from jax.experimental import pallas as pl
from jax.experimental.pallas import tpu as pltpu
from jax.sharding import PartitionSpec as P

GX = 2048
GY = 2048
ZL = 8

LANES = 256
INNER = 128
RADIX = GX // INNER
FINE = 8
SPAN = 16
COLUMNS = 64
FIELDS = 24
CHUNK = 256
REACH = LANES - 3
HOP = 128
TOGETHER = 4
TILE = 16

screening = 0.05
f32 = jnp.float32
bf16 = jnp.bfloat16


def halves(value):
    high = value.astype(bf16)
    return high, (value - high.astype(f32)).astype(bf16)


def host_halves(value):
    value = value.astype(np.float32)
    high = value.astype(ml_dtypes.bfloat16)
    return high, (value - high.astype(np.float32)).astype(ml_dtypes.bfloat16)


def column_tables():
    ky = np.arange(GY)[:, None]

    def table(offsets):
        phase = (ky * offsets[None, :] % GY) * (2.0 * math.pi / GY)
        return np.stack([np.cos(phase), -np.sin(phase)], axis=0)

    fine_high, fine_low = host_halves(table(np.arange(SPAN)))
    coarse_high, coarse_low = host_halves(table(FINE * np.arange(GY // FINE)))
    fine = np.concatenate([fine_high, fine_high, fine_low], axis=2)
    coarse = np.concatenate([coarse_high, coarse_low], axis=2)
    return fine, coarse


def transform_tables():
    index = np.arange(INNER)
    phase = (index[:, None] * index[None, :] % INNER) * (2.0 * math.pi / INNER)
    cos, sin = np.cos(phase), np.sin(phase)
    forward = np.block([[cos, -sin], [sin, cos]])
    twist = (np.arange(RADIX)[:, None] * index[None, :]) * (2.0 * math.pi / GX)
    twists = np.stack([np.cos(twist), -np.sin(twist)]).astype(np.float32)
    return np.stack(host_halves(forward)), np.stack(host_halves(forward.T)), twists


def one_hot(index, size):
    candidate = lax.broadcasted_iota(jnp.int16, (size, index.shape[1]), 0)
    return jnp.where(candidate == index.astype(jnp.int16), bf16(1), bf16(0))


def segment_factors(fields, fine_ref, coarse_ref):
    count = fields.shape[1]
    column = fields[19:20].astype(jnp.int32)
    pick = one_hot(column // FINE, GY // FINE)
    coarse = jnp.dot(
        coarse_ref[...], jnp.concatenate([pick, pick], axis=0), preferred_element_type=f32
    )
    fine_index = lax.broadcasted_iota(jnp.int32, (SPAN, count), 0) - column % FINE
    at = [fine_index == offset for offset in range(4)]
    parts = []
    for a in range(4):
        spread = jnp.zeros((SPAN, count), f32)
        for b in range(4):
            spread = jnp.where(at[b], fields[4 * a + b : 4 * a + b + 1], spread)
        high, low = halves(spread)
        parts.append(jnp.concatenate([high, low, high], axis=0))
    fine = jnp.dot(fine_ref[...], jnp.concatenate(parts, axis=1), preferred_element_type=f32)
    fines = [fine[:, a * count : (a + 1) * count] for a in range(4)]
    return coarse, fines


def thirds(value):
    high = value.astype(bf16)
    rest = value - high.astype(f32)
    middle = rest.astype(bf16)
    return high, middle, (rest - middle.astype(f32)).astype(bf16)


def order_kernel(place_ref, currents_ref, cells_ref, weights_ref, fields_ref, rank_ref, *, rows):
    count = currents_ref.shape[1]
    local = cells_ref[0:1]
    repeats = LANES // rows
    row = local // rows * LANES + place_ref[0] % repeats * rows + local % rows
    lane = lax.broadcasted_iota(jnp.int32, (1, count), 1)
    key = (row * count + lane).astype(f32)
    column = jnp.transpose(jnp.broadcast_to(key, (128, count)))[:, :1]
    rank = jnp.sum(jnp.where(column < key, 1.0, 0.0), axis=0, keepdims=True)
    pick = one_hot(rank.astype(jnp.int32), count)
    values = jnp.concatenate(
        [
            weights_ref[...],
            currents_ref[...],
            row.astype(f32),
            cells_ref[1:2].astype(f32),
            jnp.zeros((FIELDS - 20, count), f32),
        ],
        axis=0,
    )
    ordered = sum(
        lax.dot_general(part, pick, (((1,), (1,)), ((), ())), preferred_element_type=f32)
        for part in thirds(values)
    )
    ends = jnp.zeros((1, count), f32)
    for chunk in range(count // CHUNK):
        for side in range(2):
            at = lane == chunk * CHUNK + side * (CHUNK - 1)
            value = jnp.sum(jnp.where(at, ordered[18:19], 0.0), axis=1, keepdims=True)
            ends = ends + jnp.where(lane == 2 * chunk + side, value, 0.0)
    line = lax.broadcasted_iota(jnp.int32, (FIELDS, count), 0)
    ordered = jnp.where(line == 20, ends, ordered)
    for part in range(2):
        ordered = jnp.where(line == 21 + part, currents_ref[part : part + 1], ordered)
    fields_ref[...] = ordered
    rank_ref[...] = rank


def finish_kernel(arrived_ref, near_ref, rank_ref, out_ref):
    far = jnp.sum(arrived_ref[...], axis=0)
    count = far.shape[1]
    pick = one_hot(rank_ref[...].astype(jnp.int32), count)
    padded = jnp.concatenate([far, jnp.zeros((14, count), f32)], axis=0)
    total = sum(jnp.dot(part, pick, preferred_element_type=f32) for part in thirds(padded))
    out_ref[...] = total[:2] + near_ref[...]


def windows(fields_ref, ends, block, total_rows):
    chunks = []
    for chunk in range(fields_ref.shape[2] // CHUNK):
        low = ends(block, 2 * chunk).astype(jnp.int32)
        high = ends(block, 2 * chunk + 1).astype(jnp.int32)
        start = jnp.minimum(low // HOP * HOP, total_rows - LANES)
        more = (jnp.maximum(high + 1 - (start + REACH), 0) + HOP - 1) // HOP
        chunks.append((start, more))

    def window(chunk, number, visit):
        first = isinstance(number, int)
        row = fields_ref[block, 18:19, chunk * CHUNK : (chunk + 1) * CHUNK].astype(jnp.int32)
        begin = pl.multiple_of(chunks[chunk][0] + number * HOP, HOP)
        apart = row - begin
        inside = (apart >= (0 if first else REACH - HOP)) & (apart < REACH)
        visit(chunk, begin, one_hot(jnp.where(inside, apart, -1), LANES), first)

    def begin_all(visit):
        for chunk in range(len(chunks)):
            window(chunk, 0, visit)

    def finish_all(visit):
        @pl.when(sum(more for _, more in chunks) > 0)
        def _():
            for chunk in range(len(chunks)):

                def again(number, carry, chunk=chunk):
                    window(chunk, number, visit)
                    return carry

                lax.fori_loop(1, chunks[chunk][1] + 1, again, 0)

    return begin_all, finish_all


def spread_kernel(
    place_ref, before_ref, fields_ref, ends_ref, fine_ref, coarse_ref, out_ref, *scratch, repeats, together
):
    layers = out_ref.shape[0]
    half = 8 * COLUMNS
    rest = []
    for block in range(together):
        factor_ref, total_ref = scratch[2 * block : 2 * block + 2]
        fields = fields_ref[block]
        coarse, fines = segment_factors(fields, fine_ref, coarse_ref)
        current_re, current_im = fields[16:17], fields[17:18]
        phase_re, phase_im = coarse[:COLUMNS], coarse[COLUMNS:]
        wave_re = phase_re * current_re - phase_im * current_im
        wave_im = phase_re * current_im + phase_im * current_re
        base = 0
        for fine in fines:
            fine_re, fine_im = fine[:COLUMNS], fine[COLUMNS:]
            for value in (
                wave_re * fine_re - wave_im * fine_im,
                wave_re * fine_im + wave_im * fine_re,
            ):
                high, low = halves(value)
                factor_ref[base : base + COLUMNS] = high
                factor_ref[half + base : half + base + COLUMNS] = low
                base += COLUMNS
        total_ref[...] = jnp.zeros_like(total_ref)

        def visit(chunk, begin, select, first, factor_ref=factor_ref, total_ref=total_ref):
            factors = factor_ref[:, chunk * CHUNK : (chunk + 1) * CHUNK]
            form = (((1,), (1,)), ((), ()))
            spread = lax.dot_general(factors, select, form, preferred_element_type=f32)
            spread = spread[:half] + spread[half:]
            total = spread[: 2 * COLUMNS]
            for a in range(1, 4):
                total = total + pltpu.roll(spread[2 * COLUMNS * a : 2 * COLUMNS * (a + 1)], a, 1)
            total_ref[:, pl.ds(begin, LANES)] += total

        begin_all, finish_all = windows(
            fields_ref, lambda block, at: ends_ref[block, 4, at], block, layers * LANES
        )
        begin_all(visit)
        rest.append((finish_all, visit))
    for finish_all, visit in rest:
        finish_all(visit)
    fresh = pl.program_id(0) * together % min(repeats, pl.num_programs(0) * together) == 0
    for layer in range(layers):
        pieces = [
            scratch[2 * block + 1][:, layer * LANES : (layer + 1) * LANES]
            for block in range(together)
        ]
        if repeats == 1:
            for block, piece in enumerate(pieces):
                spot = (place_ref[0] % together) ^ block
                out_ref[layer, :, pl.ds(pl.multiple_of(spot * LANES, LANES), LANES)] = piece
        else:
            out_ref[layer] = jnp.where(fresh, before_ref[layer], out_ref[layer]) + sum(pieces)


def sample_kernel(place_ref, *refs, depths, together):
    parts, ends_refs, refs = refs[:depths], refs[depths : 2 * depths], refs[2 * depths :]
    field_ref, fine_ref, coarse_ref, out_ref, fields_ref, *scratch = refs
    turn_now = pl.program_id(0) // (pl.num_programs(0) // depths)
    for step in range(depths):

        @pl.when(turn_now == step)
        def _(step=step):
            fields_ref[...] = parts[step][...]

    def ends(block, at):
        value = ends_refs[0][block, 4, at]
        for step in range(1, depths):
            value = jnp.where(turn_now == step, ends_refs[step][block, 4, at], value)
        return value

    layers = field_ref.shape[0]
    total_rows = layers * LANES
    half = 8 * COLUMNS
    rest = []
    for block in range(together):
        factor_ref, sampled_ref = scratch[2 * block : 2 * block + 2]
        if field_ref.shape[2] == LANES:
            at = pl.ds(0, LANES)
        else:
            spot = (place_ref[0] % together) ^ block
            at = pl.ds(pl.multiple_of(spot * LANES, LANES), LANES)
        field = jnp.concatenate([field_ref[layer, :, at] for layer in range(layers)], axis=1)
        for a in range(4):
            moved = pltpu.roll(field, total_rows - a, 1) if a else field
            high, low = halves(moved)
            base = 2 * COLUMNS * a
            factor_ref[base : base + 2 * COLUMNS] = high
            factor_ref[half + base : half + base + 2 * COLUMNS] = low

        def visit(chunk, begin, select, first, factor_ref=factor_ref, sampled_ref=sampled_ref):
            factors = factor_ref[:, pl.ds(begin, LANES)]
            sampled = jnp.dot(factors, select, preferred_element_type=f32)
            sampled = sampled[:half] + sampled[half:]
            at = slice(chunk * CHUNK, (chunk + 1) * CHUNK)
            sampled_ref[:, at] = sampled if first else sampled_ref[:, at] + sampled

        begin_all, finish_all = windows(fields_ref, ends, block, total_rows)
        begin_all(visit)
        rest.append((finish_all, visit))
    for finish_all, visit in rest:
        finish_all(visit)
    for block in range(together):
        sampled_ref = scratch[2 * block + 1]
        coarse, fines = segment_factors(fields_ref[block], fine_ref, coarse_ref)
        sum_re, sum_im = 0.0, 0.0
        for a, fine in enumerate(fines):
            fine_re, fine_im = fine[:COLUMNS], fine[COLUMNS:]
            base = 2 * COLUMNS * a
            value_re = sampled_ref[base : base + COLUMNS]
            value_im = sampled_ref[base + COLUMNS : base + 2 * COLUMNS]
            sum_re = sum_re + value_re * fine_re + value_im * fine_im
            sum_im = sum_im + value_im * fine_re - value_re * fine_im
        phase_re, phase_im = coarse[:COLUMNS], coarse[COLUMNS:]
        far_re = jnp.sum(sum_re * phase_re + sum_im * phase_im, axis=0, keepdims=True)
        far_im = jnp.sum(sum_im * phase_re - sum_re * phase_im, axis=0, keepdims=True)
        spot = (place_ref[0] % together) ^ block
        out_ref[pl.ds(spot, 1)] = jnp.concatenate([far_re, far_im], axis=0).reshape(
            (1,) + out_ref.shape[1:]
        )


def turn(value, step, size, sign):
    real, imag = value
    if step == 0:
        return value
    if 4 * step == size:
        return (-imag, real) if sign > 0 else (imag, -real)
    half = math.sqrt(0.5)
    if 8 * step == size:
        if sign > 0:
            return ((real - imag) * half, (real + imag) * half)
        return ((real + imag) * half, (imag - real) * half)
    cos = math.cos(2.0 * math.pi * step / size)
    sin = sign * math.sin(2.0 * math.pi * step / size)
    return (real * cos - imag * sin, real * sin + imag * cos)


def butterflies(values, sign):
    size = len(values)
    if size == 1:
        return values
    even = butterflies(values[0::2], sign)
    odd = butterflies(values[1::2], sign)
    low, high = [], []
    for k in range(size // 2):
        moved = turn(odd[k], k, size, sign)
        low.append((even[k][0] + moved[0], even[k][1] + moved[1]))
        high.append((even[k][0] - moved[0], even[k][1] - moved[1]))
    return low + high


def dense(value, matrix_ref):
    high, low = halves(value)
    return (
        jnp.dot(high, matrix_ref[0], preferred_element_type=f32)
        + jnp.dot(low, matrix_ref[0], preferred_element_type=f32)
        + jnp.dot(high, matrix_ref[1], preferred_element_type=f32)
    )


def mix(spec, kappa, keep, soil_ref, reflection):
    upper = (soil_ref[0, 0], soil_ref[1, 0])
    lower = (soil_ref[0, 1], soil_ref[1, 1])
    decay = jnp.exp(-kappa)
    base = jnp.where(keep, 1.0 / (GX * GY) / (kappa + screening), 0.0)
    source = []
    for layer in range(ZL):
        rho_re, rho_im = upper if layer < ZL // 2 else lower
        re, im = spec[layer]
        source.append(((rho_re * re - rho_im * im) * base, (rho_re * im + rho_im * re) * base))
    below = [None] * ZL
    below[ZL - 1] = (jnp.zeros_like(kappa), jnp.zeros_like(kappa))
    for layer in range(ZL - 2, -1, -1):
        below[layer] = tuple(decay * (below[layer + 1][i] + source[layer + 1][i]) for i in range(2))
    surface = tuple(decay * (below[0][i] + source[0][i]) for i in range(2))
    image = (
        reflection[0] * surface[0] - reflection[1] * surface[1],
        reflection[0] * surface[1] + reflection[1] * surface[0],
    )
    above = source[0]
    mixed = []
    for layer in range(ZL):
        if layer:
            above = tuple(decay * above[i] + source[layer][i] for i in range(2))
            image = tuple(decay * image[i] for i in range(2))
        mixed.append(tuple(above[i] + below[layer][i] + image[i] for i in range(2)))
    return mixed


def reflect(soil_ref, shape):
    upper_re, lower_re = (jnp.full(shape, soil_ref[0, i], f32) for i in range(2))
    upper_im, lower_im = (jnp.full(shape, soil_ref[1, i], f32) for i in range(2))
    denom_re, denom_im = upper_re + lower_re, upper_im + lower_im
    numer_re, numer_im = lower_re - upper_re, lower_im - upper_im
    magnitude = denom_re * denom_re + denom_im * denom_im
    return (
        (numer_re * denom_re + numer_im * denom_im) / magnitude,
        (numer_im * denom_re - numer_re * denom_im) / magnitude,
    )


def mix_kernel(place_ref, soil_ref, spec_ref, forward_ref, inverse_ref, twist_ref, out_ref, *, columns):
    tile = spec_ref.shape[2]
    rows = ZL * tile
    real = spec_ref[:, 0].reshape(rows, GX)
    imag = spec_ref[:, 1].reshape(rows, GX)
    cut = [slice(n * INNER, (n + 1) * INNER) for n in range(RADIX)]
    values = butterflies([(real[:, c], imag[:, c]) for c in cut], -1.0)
    local = pl.program_id(0) * tile + lax.broadcasted_iota(jnp.int32, (tile, INNER), 0)
    keep = local < columns
    ky = place_ref[2] + local
    reflection = reflect(soil_ref, (tile, INNER))
    freq_y = jnp.where(ky < (GY - 1) // 2 + 1, ky, ky - GY).astype(f32) / GY
    inner = lax.broadcasted_iota(jnp.int32, (tile, INNER), 1)
    back = []
    for k in range(RADIX):
        twist_re, twist_im = twist_ref[0, k : k + 1], twist_ref[1, k : k + 1]
        re, im = values[k]
        turned = (re * twist_re - im * twist_im, re * twist_im + im * twist_re) if k else (re, im)
        spectrum = dense(jnp.concatenate(turned, axis=1), forward_ref)
        kx = k + RADIX * inner
        freq_x = jnp.where(kx < (GX - 1) // 2 + 1, kx, kx - GX).astype(f32) / GX
        kappa = 2.0 * math.pi * jnp.sqrt(freq_x * freq_x + freq_y * freq_y)
        spec = [
            (spectrum[s * tile : (s + 1) * tile, :INNER], spectrum[s * tile : (s + 1) * tile, INNER:])
            for s in range(ZL)
        ]
        mixed = mix(spec, kappa, keep, soil_ref, reflection)
        stacked = jnp.concatenate([jnp.concatenate(pair, axis=1) for pair in mixed], axis=0)
        field = dense(stacked, inverse_ref)
        re, im = field[:, :INNER], field[:, INNER:]
        turned = (re * twist_re + im * twist_im, im * twist_re - re * twist_im) if k else (re, im)
        back.append(turned)
    values = butterflies(back, 1.0)
    for n in range(RADIX):
        out_ref[:, 0, :, cut[n]] = values[n][0].reshape(ZL, tile, INNER)
        out_ref[:, 1, :, cut[n]] = values[n][1].reshape(ZL, tile, INNER)


def partner(value, axis, step):
    count = lax.axis_size(axis)
    return lax.ppermute(value, axis, [(i, i ^ step) for i in range(count)])


def near_kernel(place_ref, pairs_ref, own_ref, corrections_ref, after_ref, out_ref):
    slots, _, size, _ = corrections_ref.shape
    pencils, _, segments = own_ref.shape
    blocks = segments // size
    out_ref[...] = jnp.zeros_like(out_ref)

    def add(slot, carry):
        target, source = pairs_ref[0, slot], pairs_ref[1, slot]
        live = pairs_ref[2, slot].astype(f32)
        pencil = jnp.clip(place_ref[0] + source // blocks - 1, 0, pencils - 1)
        index = pencil ^ place_ref[0]
        at = pl.ds(pl.multiple_of(source % blocks * size, size), size)
        current = own_ref[index, 21:23, at] * live
        real, imag = corrections_ref[slot, 0], corrections_ref[slot, 1]
        piece_re = real * current[0:1] - imag * current[1:2]
        piece_im = real * current[1:2] + imag * current[0:1]
        to = pl.ds(pl.multiple_of(target * size, size), size)
        out_ref[0:1, to] += jnp.sum(jnp.transpose(piece_re), axis=0, keepdims=True)
        out_ref[1:2, to] += jnp.sum(jnp.transpose(piece_im), axis=0, keepdims=True)
        return carry

    lax.fori_loop(0, slots, add, 0)


def shards(currents, stencil_cells, stencil_weights, soil, near_pairs, corrections):
    pencils = lax.axis_size("pencil")
    depths = lax.axis_size("depth")
    pencil = lax.axis_index("pencil")
    depth = lax.axis_index("depth")
    segments = currents.shape[1]
    layers = ZL // depths
    rows = GX // pencils
    repeats = LANES // rows
    groups = pencils * depths
    columns = GY // groups
    first = (pencil * depths + depth) * columns

    bits = [1 << i for i in range(pencils.bit_length() - 1)]
    if repeats == 1:
        bits = bits[:1] + bits[:0:-1]
    place = jnp.stack([pencil, depth, first]).astype(jnp.int32)
    params = pltpu.CompilerParams(vmem_limit_bytes=48 * 1024 * 1024)
    anywhere = pl.BlockSpec(memory_space=pl.ANY)
    scalars = pl.BlockSpec(memory_space=pltpu.SMEM)
    resident = pl.BlockSpec(memory_space=pltpu.VMEM)
    fields, rank = pl.pallas_call(
        functools.partial(order_kernel, rows=rows),
        in_specs=[scalars] + [pl.BlockSpec()] * 3,
        out_specs=[pl.BlockSpec()] * 2,
        out_shape=[
            jax.ShapeDtypeStruct((FIELDS, segments), f32),
            jax.ShapeDtypeStruct((1, segments), f32),
        ],
        compiler_params=params,
    )(place, currents, stencil_cells, stencil_weights)

    params = pltpu.CompilerParams(vmem_limit_bytes=48 * 1024 * 1024)
    anywhere = pl.BlockSpec(memory_space=pl.ANY)
    scalars = pl.BlockSpec(memory_space=pltpu.SMEM)
    resident = pl.BlockSpec(memory_space=pltpu.VMEM)
    fields, rank = pl.pallas_call(
        functools.partial(order_kernel, rows=rows),
        in_specs=[scalars] + [pl.BlockSpec()] * 3,
        out_specs=[pl.BlockSpec()] * 2,
        out_shape=[
            jax.ShapeDtypeStruct((FIELDS, segments), f32),
            jax.ShapeDtypeStruct((1, segments), f32),
        ],
        compiler_params=params,
    )(place, currents, stencil_cells, stencil_weights)

    def offset(index):
        return sum((index >> j & 1) * bit for j, bit in enumerate(bits))


    fine, coarse = column_tables()
    fine = lax.dynamic_slice_in_dim(
        jnp.asarray(np.pad(fine, ((0, 0), (0, COLUMNS), (0, 0)))), first, COLUMNS, axis=1
    ).reshape(2 * COLUMNS, -1)
    coarse = lax.dynamic_slice_in_dim(
        jnp.asarray(np.pad(coarse, ((0, 0), (0, COLUMNS), (0, 0)))), first, COLUMNS, axis=1
    ).reshape(2 * COLUMNS, -1)
    forward, inverse, twists = transform_tables()
    def fields_specs(together):
        return [
            pl.BlockSpec((together, FIELDS, segments), lambda i, place: (i, 0, 0)),
            pl.BlockSpec((together, 8, 128), lambda i, place: (i, 2, 0), memory_space=pltpu.SMEM),
        ]

    def lead(offsets, together):
        firsts = offsets[::together]
        if firsts == list(range(firsts[0], firsts[0] + len(offsets), together)):
            return lambda i: firsts[0] + together * i
        return lambda i: sum(jnp.where(i == k, first, 0) for k, first in enumerate(firsts))

    def region(offsets, step, together):
        wide = together if repeats == 1 else 1
        first = lead(offsets, together)
        return pl.BlockSpec(
            (layers, 2 * COLUMNS, LANES * wide),
            lambda i, place: (place[1] ^ step, 0, (place[0] ^ first(i)) // (repeats * wide)),
        )

    fine_spec = pl.BlockSpec(fine.shape, lambda i, place: (0, 0))
    coarse_spec = pl.BlockSpec(coarse.shape, lambda i, place: (0, 0))

    def cost(blocks):
        return pl.CostEstimate(
            flops=blocks * 2_000_000_000, bytes_accessed=blocks * 600_000, transcendentals=0
        )

    def spread(grid, chunk, offsets, step, together):
        fresh = grid is None
        if fresh and repeats > 1:
            grid, fresh = jnp.zeros((ZL, 2 * COLUMNS, GX), f32), False
        before = jnp.zeros((8, 128), f32) if fresh else grid
        return pl.pallas_call(
            functools.partial(spread_kernel, repeats=repeats, together=together),
            grid_spec=pltpu.PrefetchScalarGridSpec(
                num_scalar_prefetch=1,
                grid=(chunk.shape[0] // together,),
                in_specs=[
                    anywhere if repeats == 1 else region(offsets, step, together),
                    *fields_specs(together),
                    fine_spec,
                    coarse_spec,
                ],
                out_specs=region(offsets, step, together),
                scratch_shapes=[
                    pltpu.VMEM((16 * COLUMNS, segments), bf16),
                    pltpu.VMEM((2 * COLUMNS, layers * LANES), f32),
                ]
                * together,
            ),
            out_shape=jax.ShapeDtypeStruct((ZL, 2 * COLUMNS, GX), f32),
            input_output_aliases={} if fresh else {1: 0},
            compiler_params=params,
            cost_estimate=cost(chunk.shape[0]),
        )(place, before, chunk, chunk, fine, coarse)

    own, offsets, grid = fields[None], [0], None
    for number, bit in enumerate(bits):
        arrived = partner(own, "pencil", bit)
        fresh = [offset ^ bit for offset in offsets]
        known = len(offsets)
        offsets = offsets + fresh
        pieces, order = [], list(range(2 * known))
        if number == len(bits) - 1:
            order = [int(index) for index in np.argsort(np.array(offsets))]
        while order:
            run = 1
            while run < len(order) and order[run] == order[0] + run and order[run] != known:
                run += 1
            source, at = (own, order[0]) if order[0] < known else (arrived, order[0] - known)
            pieces.append(source[at : at + run])
            order = order[run:]
        own = jnp.concatenate(pieces)
        if number == 0:
            grid = spread(grid, own, offsets, 0, 2)
        else:
            grid = spread(grid, arrived, fresh, 0, 2)
    offsets = list(range(pencils))
    together = min(TOGETHER, pencils)
    parts = {0: own}
    for step in range(1, depths):
        if step & (step - 1) == 0:
            parts[step] = partner(own, "depth", step)
    for step in range(1, depths):
        grid = spread(grid, parts[step], offsets, step, together)
        later = step + 2
        if later < depths and later not in parts:
            low = later & -later
            source, grid = lax.optimization_barrier((parts[later ^ low], grid))
            parts[later] = partner(source, "depth", low)

    tile_spec = pl.BlockSpec((ZL, 2, TILE, GX), lambda t: (0, 0, t, 0))
    whole = lambda *shape: pl.BlockSpec(shape, lambda t: (0,) * len(shape))
    mixed = pl.pallas_call(
        functools.partial(mix_kernel, columns=columns),
        grid=(COLUMNS // TILE,),
        in_specs=[
            pl.BlockSpec(memory_space=pltpu.SMEM),
            pl.BlockSpec(memory_space=pltpu.SMEM),
            tile_spec,
            whole(*forward.shape),
            whole(*inverse.shape),
            whole(*twists.shape),
        ],
        out_specs=tile_spec,
        out_shape=jax.ShapeDtypeStruct((ZL, 2, COLUMNS, GX), f32),
        compiler_params=params,
    )(
        place,
        soil,
        grid.reshape(ZL, 2, COLUMNS, GX),
        jnp.asarray(forward),
        jnp.asarray(inverse),
        jnp.asarray(twists),
    ).reshape(ZL, 2 * COLUMNS, GX)
    turns = pencils // together
    wide = together if repeats == 1 else 1

    def part_specs(block, line, step, **kinds):
        return pl.BlockSpec(
            (together,) + block,
            lambda i, place: (jnp.clip(i - step * turns, 0, turns - 1), line, 0),
            **kinds,
        )

    partial = pl.pallas_call(
        functools.partial(sample_kernel, depths=depths, together=together),
        grid_spec=pltpu.PrefetchScalarGridSpec(
            num_scalar_prefetch=1,
            grid=(depths * turns,),
            in_specs=[part_specs((FIELDS, segments), 0, step) for step in range(depths)]
            + [
                part_specs((8, 128), 2, step, memory_space=pltpu.SMEM) for step in range(depths)
            ]
            + [
                pl.BlockSpec(
                    (layers, 2 * COLUMNS, LANES * wide),
                    lambda i, place: (
                        place[1] ^ (i // turns),
                        0,
                        (place[0] ^ (together * (i % turns))) // (repeats * wide),
                    ),
                ),
                fine_spec,
                coarse_spec,
            ],
            out_specs=pl.BlockSpec(
                (together, None, 2, segments),
                lambda i, place: (
                    (place[0] ^ (together * (i % turns))) // together,
                    place[1] ^ (i // turns),
                    0,
                    0,
                ),
            ),
            scratch_shapes=[pltpu.VMEM((together, FIELDS, segments), f32)]
            + [
                pltpu.VMEM((16 * COLUMNS, layers * LANES), bf16),
                pltpu.VMEM((8 * COLUMNS, segments), f32),
            ]
            * together,
        ),
        out_shape=jax.ShapeDtypeStruct((pencils, depths, 2, segments), f32),
        compiler_params=params,
        cost_estimate=cost(groups),
    )(place, *[parts[k] for k in range(depths)], *[parts[k] for k in range(depths)], mixed, fine, coarse)
    partial = partial.reshape(groups, 2, segments)
    near = pl.pallas_call(
        near_kernel,
        in_specs=[scalars, scalars, pl.BlockSpec(), pl.BlockSpec(), anywhere],
        out_specs=pl.BlockSpec(),
        out_shape=jax.ShapeDtypeStruct((2, segments), f32),
        compiler_params=params,
        cost_estimate=cost(2),
    )(place, near_pairs, parts[0], corrections, partial)
    arrived = lax.all_to_all(partial, ("pencil", "depth"), split_axis=0, concat_axis=0, tiled=True)
    return pl.pallas_call(
        finish_kernel,
        in_specs=[resident, resident, resident],
        out_specs=resident,
        out_shape=jax.ShapeDtypeStruct((2, segments), f32),
        compiler_params=params,
    )(arrived, near, rank)


def solution(mesh):
    return jax.shard_map(
        shards,
        mesh=mesh,
        in_specs=(
            P(None, ("pencil", "depth")),
            P(None, ("pencil", "depth")),
            P(None, ("pencil", "depth")),
            P(),
            P(None, ("pencil", "depth")),
            P(("pencil", "depth"), None, None, None),
        ),
        out_specs=P(None, ("pencil", "depth")),
        check_vma=False,
    )
```

```python
import functools
import math

import jax
import jax.numpy as jnp
import ml_dtypes
import numpy as np
from jax import lax
from jax.experimental import pallas as pl
from jax.experimental.pallas import tpu as pltpu
from jax.sharding import PartitionSpec as P

GX = 2048
GY = 2048
ZL = 8

LANES = 256
INNER = 128
RADIX = GX // INNER
FINE = 16
SPAN = 32
COLUMNS = 64
FIELDS = 24
CHUNK = 256
REACH = LANES - 3
HOP = 128
TOGETHER = 4
TILE = 16

screening = 0.05
f32 = jnp.float32
bf16 = jnp.bfloat16


def halves(value):
    high = value.astype(bf16)
    return high, (value - high.astype(f32)).astype(bf16)


def host_halves(value):
    value = value.astype(np.float32)
    high = value.astype(ml_dtypes.bfloat16)
    return high, (value - high.astype(np.float32)).astype(ml_dtypes.bfloat16)


def column_tables():
    ky = np.arange(GY)[:, None]

    def table(offsets):
        phase = (ky * offsets[None, :] % GY) * (2.0 * math.pi / GY)
        return np.stack([np.cos(phase), -np.sin(phase)], axis=0)

    fine_high, fine_low = host_halves(table(np.arange(SPAN)))
    coarse_high, coarse_low = host_halves(table(FINE * np.arange(GY // FINE)))
    fine = np.concatenate([fine_high, fine_high, fine_low], axis=2)
    coarse = np.concatenate([coarse_high, coarse_low], axis=2)
    return fine, coarse


def transform_tables():
    index = np.arange(INNER)
    phase = (index[:, None] * index[None, :] % INNER) * (2.0 * math.pi / INNER)
    cos, sin = np.cos(phase), np.sin(phase)
    forward = np.block([[cos, -sin], [sin, cos]])
    twist = (np.arange(RADIX)[:, None] * index[None, :]) * (2.0 * math.pi / GX)
    twists = np.stack([np.cos(twist), -np.sin(twist)]).astype(np.float32)
    return np.stack(host_halves(forward)), np.stack(host_halves(forward.T)), twists


def one_hot(index, size):
    candidate = lax.broadcasted_iota(jnp.int16, (size, index.shape[1]), 0)
    return jnp.where(candidate == index.astype(jnp.int16), bf16(1), bf16(0))


def segment_factors(fields, fine_ref, coarse_ref):
    count = fields.shape[1]
    column = fields[19:20].astype(jnp.int32)
    pick = one_hot(column // FINE, GY // FINE)
    coarse = jnp.dot(
        coarse_ref[...], jnp.concatenate([pick, pick], axis=0), preferred_element_type=f32
    )
    fine_index = lax.broadcasted_iota(jnp.int32, (SPAN, count), 0) - column % FINE
    at = [fine_index == offset for offset in range(4)]
    parts = []
    for a in range(4):
        spread = jnp.zeros((SPAN, count), f32)
        for b in range(4):
            spread = jnp.where(at[b], fields[4 * a + b : 4 * a + b + 1], spread)
        high, low = halves(spread)
        parts.append(jnp.concatenate([high, low, high], axis=0))
    fine = jnp.dot(fine_ref[...], jnp.concatenate(parts, axis=1), preferred_element_type=f32)
    fines = [fine[:, a * count : (a + 1) * count] for a in range(4)]
    return coarse, fines


def thirds(value):
    high = value.astype(bf16)
    rest = value - high.astype(f32)
    middle = rest.astype(bf16)
    return high, middle, (rest - middle.astype(f32)).astype(bf16)


def order_kernel(place_ref, currents_ref, cells_ref, weights_ref, fields_ref, rank_ref, *, rows):
    count = currents_ref.shape[1]
    local = cells_ref[0:1]
    repeats = LANES // rows
    row = local // rows * LANES + place_ref[0] % repeats * rows + local % rows
    lane = lax.broadcasted_iota(jnp.int32, (1, count), 1)
    key = (row * count + lane).astype(f32)
    column = jnp.transpose(jnp.broadcast_to(key, (128, count)))[:, :1]
    rank = jnp.sum(jnp.where(column < key, 1.0, 0.0), axis=0, keepdims=True)
    pick = one_hot(rank.astype(jnp.int32), count)
    values = jnp.concatenate(
        [
            weights_ref[...],
            currents_ref[...],
            row.astype(f32),
            cells_ref[1:2].astype(f32),
            jnp.zeros((FIELDS - 20, count), f32),
        ],
        axis=0,
    )
    ordered = sum(
        lax.dot_general(part, pick, (((1,), (1,)), ((), ())), preferred_element_type=f32)
        for part in thirds(values)
    )
    ends = jnp.zeros((1, count), f32)
    for chunk in range(count // CHUNK):
        for side in range(2):
            at = lane == chunk * CHUNK + side * (CHUNK - 1)
            value = jnp.sum(jnp.where(at, ordered[18:19], 0.0), axis=1, keepdims=True)
            ends = ends + jnp.where(lane == 2 * chunk + side, value, 0.0)
    line = lax.broadcasted_iota(jnp.int32, (FIELDS, count), 0)
    ordered = jnp.where(line == 20, ends, ordered)
    for part in range(2):
        ordered = jnp.where(line == 21 + part, currents_ref[part : part + 1], ordered)
    fields_ref[...] = ordered
    rank_ref[...] = rank


def finish_kernel(arrived_ref, near_ref, rank_ref, out_ref):
    far = jnp.sum(arrived_ref[...], axis=0)
    count = far.shape[1]
    pick = one_hot(rank_ref[...].astype(jnp.int32), count)
    padded = jnp.concatenate([far, jnp.zeros((14, count), f32)], axis=0)
    total = sum(jnp.dot(part, pick, preferred_element_type=f32) for part in thirds(padded))
    out_ref[...] = total[:2] + near_ref[...]


def windows(fields_ref, ends, block, total_rows):
    chunks = []
    for chunk in range(fields_ref.shape[2] // CHUNK):
        low = ends(block, 2 * chunk).astype(jnp.int32)
        high = ends(block, 2 * chunk + 1).astype(jnp.int32)
        start = jnp.minimum(low // HOP * HOP, total_rows - LANES)
        more = (jnp.maximum(high + 1 - (start + REACH), 0) + HOP - 1) // HOP
        chunks.append((start, more))

    def window(chunk, number, visit):
        first = isinstance(number, int)
        row = fields_ref[block, 18:19, chunk * CHUNK : (chunk + 1) * CHUNK].astype(jnp.int32)
        begin = pl.multiple_of(chunks[chunk][0] + number * HOP, HOP)
        apart = row - begin
        inside = (apart >= (0 if first else REACH - HOP)) & (apart < REACH)
        visit(chunk, begin, one_hot(jnp.where(inside, apart, -1), LANES), first)

    def begin_all(visit):
        for chunk in range(len(chunks)):
            window(chunk, 0, visit)

    def finish_all(visit):
        @pl.when(sum(more for _, more in chunks) > 0)
        def _():
            for chunk in range(len(chunks)):

                def again(number, carry, chunk=chunk):
                    window(chunk, number, visit)
                    return carry

                lax.fori_loop(1, chunks[chunk][1] + 1, again, 0)

    return begin_all, finish_all


def spread_kernel(
    place_ref, before_ref, fields_ref, ends_ref, fine_ref, coarse_ref, out_ref, *scratch, repeats, together
):
    layers = out_ref.shape[0]
    half = 8 * COLUMNS
    rest = []
    for block in range(together):
        factor_ref, total_ref = scratch[2 * block : 2 * block + 2]
        fields = fields_ref[block]
        coarse, fines = segment_factors(fields, fine_ref, coarse_ref)
        current_re, current_im = fields[16:17], fields[17:18]
        phase_re, phase_im = coarse[:COLUMNS], coarse[COLUMNS:]
        wave_re = phase_re * current_re - phase_im * current_im
        wave_im = phase_re * current_im + phase_im * current_re
        base = 0
        for fine in fines:
            fine_re, fine_im = fine[:COLUMNS], fine[COLUMNS:]
            for value in (
                wave_re * fine_re - wave_im * fine_im,
                wave_re * fine_im + wave_im * fine_re,
            ):
                high, low = halves(value)
                factor_ref[base : base + COLUMNS] = high
                factor_ref[half + base : half + base + COLUMNS] = low
                base += COLUMNS
        total_ref[...] = jnp.zeros_like(total_ref)

        def visit(chunk, begin, select, first, factor_ref=factor_ref, total_ref=total_ref):
            factors = factor_ref[:, chunk * CHUNK : (chunk + 1) * CHUNK]
            form = (((1,), (1,)), ((), ()))
            spread = lax.dot_general(factors, select, form, preferred_element_type=f32)
            spread = spread[:half] + spread[half:]
            total = spread[: 2 * COLUMNS]
            for a in range(1, 4):
                total = total + pltpu.roll(spread[2 * COLUMNS * a : 2 * COLUMNS * (a + 1)], a, 1)
            total_ref[:, pl.ds(begin, LANES)] += total

        begin_all, finish_all = windows(
            fields_ref, lambda block, at: ends_ref[block, 4, at], block, layers * LANES
        )
        begin_all(visit)
        rest.append((finish_all, visit))
    for finish_all, visit in rest:
        finish_all(visit)
    fresh = pl.program_id(0) * together % min(repeats, pl.num_programs(0) * together) == 0
    for layer in range(layers):
        pieces = [
            scratch[2 * block + 1][:, layer * LANES : (layer + 1) * LANES]
            for block in range(together)
        ]
        if repeats == 1:
            for block, piece in enumerate(pieces):
                spot = (place_ref[0] % together) ^ block
                out_ref[layer, :, pl.ds(pl.multiple_of(spot * LANES, LANES), LANES)] = piece
        else:
            out_ref[layer] = jnp.where(fresh, before_ref[layer], out_ref[layer]) + sum(pieces)


def sample_kernel(place_ref, *refs, depths, together):
    parts, ends_refs, refs = refs[:depths], refs[depths : 2 * depths], refs[2 * depths :]
    field_ref, fine_ref, coarse_ref, out_ref, fields_ref, *scratch = refs
    turn_now = pl.program_id(0) // (pl.num_programs(0) // depths)
    for step in range(depths):

        @pl.when(turn_now == step)
        def _(step=step):
            fields_ref[...] = parts[step][...]

    def ends(block, at):
        value = ends_refs[0][block, 4, at]
        for step in range(1, depths):
            value = jnp.where(turn_now == step, ends_refs[step][block, 4, at], value)
        return value

    layers = field_ref.shape[0]
    total_rows = layers * LANES
    half = 8 * COLUMNS

    def reduced(sampled, coarse, fines):
        sum_re, sum_im = 0.0, 0.0
        for a, fine in enumerate(fines):
            fine_re, fine_im = fine[:COLUMNS], fine[COLUMNS:]
            base = 2 * COLUMNS * a
            value_re = sampled[base : base + COLUMNS]
            value_im = sampled[base + COLUMNS : base + 2 * COLUMNS]
            sum_re = sum_re + value_re * fine_re + value_im * fine_im
            sum_im = sum_im + value_im * fine_re - value_re * fine_im
        phase_re, phase_im = coarse[:COLUMNS], coarse[COLUMNS:]
        far_re = jnp.sum(sum_re * phase_re + sum_im * phase_im, axis=0, keepdims=True)
        far_im = jnp.sum(sum_im * phase_re - sum_re * phase_im, axis=0, keepdims=True)
        return jnp.concatenate([far_re, far_im], axis=0)[None]

    rest = []
    for block in range(together):
        factor_ref = scratch[block]
        spot = (place_ref[0] % together) ^ block
        if field_ref.shape[2] == LANES:
            at = pl.ds(0, LANES)
        else:
            at = pl.ds(pl.multiple_of(spot * LANES, LANES), LANES)
        field = jnp.concatenate([field_ref[layer, :, at] for layer in range(layers)], axis=1)
        for a in range(4):
            moved = pltpu.roll(field, total_rows - a, 1) if a else field
            high, low = halves(moved)
            base = 2 * COLUMNS * a
            factor_ref[base : base + 2 * COLUMNS] = high
            factor_ref[half + base : half + base + 2 * COLUMNS] = low
        coarse, fines = segment_factors(fields_ref[block], fine_ref, coarse_ref)

        def visit(
            chunk,
            begin,
            select,
            first,
            block=block,
            factor_ref=factor_ref,
            spot=spot,
            coarse=coarse,
            fines=fines,
        ):
            sampled = jnp.dot(
                factor_ref[:, pl.ds(begin, LANES)], select, preferred_element_type=f32
            )
            sampled = sampled[:half] + sampled[half:]
            cut = slice(chunk * CHUNK, (chunk + 1) * CHUNK)
            if first:
                far = reduced(sampled, coarse[:, cut], [fine[:, cut] for fine in fines])
                out_ref[pl.ds(spot, 1), :, cut] = far
            else:
                again = segment_factors(fields_ref[block, :, cut], fine_ref, coarse_ref)
                out_ref[pl.ds(spot, 1), :, cut] += reduced(sampled, *again)

        begin_all, finish_all = windows(fields_ref, ends, block, total_rows)
        begin_all(visit)
        rest.append((finish_all, visit))
    for finish_all, visit in rest:
        finish_all(visit)


def turn(value, step, size, sign):
    real, imag = value
    if step == 0:
        return value
    if 4 * step == size:
        return (-imag, real) if sign > 0 else (imag, -real)
    half = math.sqrt(0.5)
    if 8 * step == size:
        if sign > 0:
            return ((real - imag) * half, (real + imag) * half)
        return ((real + imag) * half, (imag - real) * half)
    cos = math.cos(2.0 * math.pi * step / size)
    sin = sign * math.sin(2.0 * math.pi * step / size)
    return (real * cos - imag * sin, real * sin + imag * cos)


def butterflies(values, sign):
    size = len(values)
    if size == 1:
        return values
    even = butterflies(values[0::2], sign)
    odd = butterflies(values[1::2], sign)
    low, high = [], []
    for k in range(size // 2):
        moved = turn(odd[k], k, size, sign)
        low.append((even[k][0] + moved[0], even[k][1] + moved[1]))
        high.append((even[k][0] - moved[0], even[k][1] - moved[1]))
    return low + high


def dense(value, matrix_ref):
    high, low = halves(value)
    return (
        jnp.dot(high, matrix_ref[0], preferred_element_type=f32)
        + jnp.dot(low, matrix_ref[0], preferred_element_type=f32)
        + jnp.dot(high, matrix_ref[1], preferred_element_type=f32)
    )


def mix(spec, kappa, keep, soil_ref, reflection):
    upper = (soil_ref[0, 0], soil_ref[1, 0])
    lower = (soil_ref[0, 1], soil_ref[1, 1])
    decay = jnp.exp(-kappa)
    base = jnp.where(keep, 1.0 / (GX * GY) / (kappa + screening), 0.0)
    source = []
    for layer in range(ZL):
        rho_re, rho_im = upper if layer < ZL // 2 else lower
        re, im = spec[layer]
        source.append(((rho_re * re - rho_im * im) * base, (rho_re * im + rho_im * re) * base))
    below = [None] * ZL
    below[ZL - 1] = (jnp.zeros_like(kappa), jnp.zeros_like(kappa))
    for layer in range(ZL - 2, -1, -1):
        below[layer] = tuple(decay * (below[layer + 1][i] + source[layer + 1][i]) for i in range(2))
    surface = tuple(decay * (below[0][i] + source[0][i]) for i in range(2))
    image = (
        reflection[0] * surface[0] - reflection[1] * surface[1],
        reflection[0] * surface[1] + reflection[1] * surface[0],
    )
    above = source[0]
    mixed = []
    for layer in range(ZL):
        if layer:
            above = tuple(decay * above[i] + source[layer][i] for i in range(2))
            image = tuple(decay * image[i] for i in range(2))
        mixed.append(tuple(above[i] + below[layer][i] + image[i] for i in range(2)))
    return mixed


def reflect(soil_ref, shape):
    upper_re, lower_re = (jnp.full(shape, soil_ref[0, i], f32) for i in range(2))
    upper_im, lower_im = (jnp.full(shape, soil_ref[1, i], f32) for i in range(2))
    denom_re, denom_im = upper_re + lower_re, upper_im + lower_im
    numer_re, numer_im = lower_re - upper_re, lower_im - upper_im
    magnitude = denom_re * denom_re + denom_im * denom_im
    return (
        (numer_re * denom_re + numer_im * denom_im) / magnitude,
        (numer_im * denom_re - numer_re * denom_im) / magnitude,
    )


def mix_kernel(place_ref, soil_ref, spec_ref, forward_ref, inverse_ref, twist_ref, out_ref, *, columns):
    tile = spec_ref.shape[2]
    rows = ZL * tile
    real = spec_ref[:, 0].reshape(rows, GX)
    imag = spec_ref[:, 1].reshape(rows, GX)
    cut = [slice(n * INNER, (n + 1) * INNER) for n in range(RADIX)]
    values = butterflies([(real[:, c], imag[:, c]) for c in cut], -1.0)
    local = pl.program_id(0) * tile + lax.broadcasted_iota(jnp.int32, (tile, INNER), 0)
    keep = local < columns
    ky = place_ref[2] + local
    reflection = reflect(soil_ref, (tile, INNER))
    freq_y = jnp.where(ky < (GY - 1) // 2 + 1, ky, ky - GY).astype(f32) / GY
    inner = lax.broadcasted_iota(jnp.int32, (tile, INNER), 1)
    back = []
    for k in range(RADIX):
        twist_re, twist_im = twist_ref[0, k : k + 1], twist_ref[1, k : k + 1]
        re, im = values[k]
        turned = (re * twist_re - im * twist_im, re * twist_im + im * twist_re) if k else (re, im)
        spectrum = dense(jnp.concatenate(turned, axis=1), forward_ref)
        kx = k + RADIX * inner
        freq_x = jnp.where(kx < (GX - 1) // 2 + 1, kx, kx - GX).astype(f32) / GX
        kappa = 2.0 * math.pi * jnp.sqrt(freq_x * freq_x + freq_y * freq_y)
        spec = [
            (spectrum[s * tile : (s + 1) * tile, :INNER], spectrum[s * tile : (s + 1) * tile, INNER:])
            for s in range(ZL)
        ]
        mixed = mix(spec, kappa, keep, soil_ref, reflection)
        stacked = jnp.concatenate([jnp.concatenate(pair, axis=1) for pair in mixed], axis=0)
        field = dense(stacked, inverse_ref)
        re, im = field[:, :INNER], field[:, INNER:]
        turned = (re * twist_re + im * twist_im, im * twist_re - re * twist_im) if k else (re, im)
        back.append(turned)
    values = butterflies(back, 1.0)
    for n in range(RADIX):
        out_ref[:, 0, :, cut[n]] = values[n][0].reshape(ZL, tile, INNER)
        out_ref[:, 1, :, cut[n]] = values[n][1].reshape(ZL, tile, INNER)


def partner(value, axis, step):
    count = lax.axis_size(axis)
    return lax.ppermute(value, axis, [(i, i ^ step) for i in range(count)])


def near_kernel(place_ref, pairs_ref, own_ref, corrections_ref, after_ref, out_ref):
    slots, _, size, _ = corrections_ref.shape
    pencils, _, segments = own_ref.shape
    blocks = segments // size
    out_ref[...] = jnp.zeros_like(out_ref)

    def add(slot, carry):
        target, source = pairs_ref[0, slot], pairs_ref[1, slot]
        live = pairs_ref[2, slot].astype(f32)
        pencil = jnp.clip(place_ref[0] + source // blocks - 1, 0, pencils - 1)
        index = pencil ^ place_ref[0]
        at = pl.ds(pl.multiple_of(source % blocks * size, size), size)
        current = own_ref[index, 21:23, at] * live
        real, imag = corrections_ref[slot, 0], corrections_ref[slot, 1]
        piece_re = real * current[0:1] - imag * current[1:2]
        piece_im = real * current[1:2] + imag * current[0:1]
        to = pl.ds(pl.multiple_of(target * size, size), size)
        out_ref[0:1, to] += jnp.sum(jnp.transpose(piece_re), axis=0, keepdims=True)
        out_ref[1:2, to] += jnp.sum(jnp.transpose(piece_im), axis=0, keepdims=True)
        return carry

    lax.fori_loop(0, slots, add, 0)


def shards(currents, stencil_cells, stencil_weights, soil, near_pairs, corrections):
    pencils = lax.axis_size("pencil")
    depths = lax.axis_size("depth")
    pencil = lax.axis_index("pencil")
    depth = lax.axis_index("depth")
    segments = currents.shape[1]
    layers = ZL // depths
    rows = GX // pencils
    repeats = LANES // rows
    groups = pencils * depths
    columns = GY // groups
    first = (pencil * depths + depth) * columns

    bits = [1 << i for i in range(pencils.bit_length() - 1)]
    if repeats == 1:
        bits = bits[:1] + bits[:0:-1]
    place = jnp.stack([pencil, depth, first]).astype(jnp.int32)
    params = pltpu.CompilerParams(vmem_limit_bytes=48 * 1024 * 1024)
    anywhere = pl.BlockSpec(memory_space=pl.ANY)
    scalars = pl.BlockSpec(memory_space=pltpu.SMEM)
    resident = pl.BlockSpec(memory_space=pltpu.VMEM)
    fields, rank = pl.pallas_call(
        functools.partial(order_kernel, rows=rows),
        in_specs=[scalars] + [pl.BlockSpec()] * 3,
        out_specs=[pl.BlockSpec()] * 2,
        out_shape=[
            jax.ShapeDtypeStruct((FIELDS, segments), f32),
            jax.ShapeDtypeStruct((1, segments), f32),
        ],
        compiler_params=params,
    )(place, currents, stencil_cells, stencil_weights)

    params = pltpu.CompilerParams(vmem_limit_bytes=48 * 1024 * 1024)
    anywhere = pl.BlockSpec(memory_space=pl.ANY)
    scalars = pl.BlockSpec(memory_space=pltpu.SMEM)
    resident = pl.BlockSpec(memory_space=pltpu.VMEM)
    fields, rank = pl.pallas_call(
        functools.partial(order_kernel, rows=rows),
        in_specs=[scalars] + [pl.BlockSpec()] * 3,
        out_specs=[pl.BlockSpec()] * 2,
        out_shape=[
            jax.ShapeDtypeStruct((FIELDS, segments), f32),
            jax.ShapeDtypeStruct((1, segments), f32),
        ],
        compiler_params=params,
    )(place, currents, stencil_cells, stencil_weights)

    def offset(index):
        return sum((index >> j & 1) * bit for j, bit in enumerate(bits))


    fine, coarse = column_tables()
    fine = lax.dynamic_slice_in_dim(
        jnp.asarray(np.pad(fine, ((0, 0), (0, COLUMNS), (0, 0)))), first, COLUMNS, axis=1
    ).reshape(2 * COLUMNS, -1)
    coarse = lax.dynamic_slice_in_dim(
        jnp.asarray(np.pad(coarse, ((0, 0), (0, COLUMNS), (0, 0)))), first, COLUMNS, axis=1
    ).reshape(2 * COLUMNS, -1)
    forward, inverse, twists = transform_tables()
    def fields_specs(together):
        return [
            pl.BlockSpec((together, FIELDS, segments), lambda i, place: (i, 0, 0)),
            pl.BlockSpec((together, 8, 128), lambda i, place: (i, 2, 0), memory_space=pltpu.SMEM),
        ]

    def lead(offsets, together):
        firsts = offsets[::together]
        if firsts == list(range(firsts[0], firsts[0] + len(offsets), together)):
            return lambda i: firsts[0] + together * i
        return lambda i: sum(jnp.where(i == k, first, 0) for k, first in enumerate(firsts))

    def region(offsets, step, together):
        wide = together if repeats == 1 else 1
        first = lead(offsets, together)
        return pl.BlockSpec(
            (layers, 2 * COLUMNS, LANES * wide),
            lambda i, place: (place[1] ^ step, 0, (place[0] ^ first(i)) // (repeats * wide)),
        )

    fine_spec = pl.BlockSpec(fine.shape, lambda i, place: (0, 0))
    coarse_spec = pl.BlockSpec(coarse.shape, lambda i, place: (0, 0))

    def cost(blocks):
        return pl.CostEstimate(
            flops=blocks * 2_000_000_000, bytes_accessed=blocks * 600_000, transcendentals=0
        )

    def spread(grid, chunk, offsets, step, together):
        fresh = grid is None
        if fresh and repeats > 1:
            grid, fresh = jnp.zeros((ZL, 2 * COLUMNS, GX), f32), False
        before = jnp.zeros((8, 128), f32) if fresh else grid
        return pl.pallas_call(
            functools.partial(spread_kernel, repeats=repeats, together=together),
            grid_spec=pltpu.PrefetchScalarGridSpec(
                num_scalar_prefetch=1,
                grid=(chunk.shape[0] // together,),
                in_specs=[
                    anywhere if repeats == 1 else region(offsets, step, together),
                    *fields_specs(together),
                    fine_spec,
                    coarse_spec,
                ],
                out_specs=region(offsets, step, together),
                scratch_shapes=[
                    pltpu.VMEM((16 * COLUMNS, segments), bf16),
                    pltpu.VMEM((2 * COLUMNS, layers * LANES), f32),
                ]
                * together,
            ),
            out_shape=jax.ShapeDtypeStruct((ZL, 2 * COLUMNS, GX), f32),
            input_output_aliases={} if fresh else {1: 0},
            compiler_params=params,
            cost_estimate=cost(chunk.shape[0]),
        )(place, before, chunk, chunk, fine, coarse)

    own, offsets, grid = fields[None], [0], None
    for number, bit in enumerate(bits):
        arrived = partner(own, "pencil", bit)
        fresh = [offset ^ bit for offset in offsets]
        known = len(offsets)
        offsets = offsets + fresh
        pieces, order = [], list(range(2 * known))
        if number == len(bits) - 1:
            order = [int(index) for index in np.argsort(np.array(offsets))]
        while order:
            run = 1
            while run < len(order) and order[run] == order[0] + run and order[run] != known:
                run += 1
            source, at = (own, order[0]) if order[0] < known else (arrived, order[0] - known)
            pieces.append(source[at : at + run])
            order = order[run:]
        own = jnp.concatenate(pieces)
        if number == 0:
            grid = spread(grid, own, offsets, 0, 2)
        else:
            grid = spread(grid, arrived, fresh, 0, 2)
    offsets = list(range(pencils))
    together = min(TOGETHER, pencils)
    parts = {0: own}
    for step in range(1, depths):
        if step & (step - 1) == 0:
            parts[step] = partner(own, "depth", step)
    for step in range(1, depths):
        grid = spread(grid, parts[step], offsets, step, together)
        later = step + 2
        if later < depths and later not in parts:
            low = later & -later
            source, grid = lax.optimization_barrier((parts[later ^ low], grid))
            parts[later] = partner(source, "depth", low)

    tile_spec = pl.BlockSpec((ZL, 2, TILE, GX), lambda t: (0, 0, t, 0))
    whole = lambda *shape: pl.BlockSpec(shape, lambda t: (0,) * len(shape))
    mixed = pl.pallas_call(
        functools.partial(mix_kernel, columns=columns),
        grid=(COLUMNS // TILE,),
        in_specs=[
            pl.BlockSpec(memory_space=pltpu.SMEM),
            pl.BlockSpec(memory_space=pltpu.SMEM),
            tile_spec,
            whole(*forward.shape),
            whole(*inverse.shape),
            whole(*twists.shape),
        ],
        out_specs=tile_spec,
        out_shape=jax.ShapeDtypeStruct((ZL, 2, COLUMNS, GX), f32),
        compiler_params=params,
    )(
        place,
        soil,
        grid.reshape(ZL, 2, COLUMNS, GX),
        jnp.asarray(forward),
        jnp.asarray(inverse),
        jnp.asarray(twists),
    ).reshape(ZL, 2 * COLUMNS, GX)
    turns = pencils // together
    wide = together if repeats == 1 else 1

    def part_specs(block, line, step, **kinds):
        return pl.BlockSpec(
            (together,) + block,
            lambda i, place: (jnp.clip(i - step * turns, 0, turns - 1), line, 0),
            **kinds,
        )

    partial = pl.pallas_call(
        functools.partial(sample_kernel, depths=depths, together=together),
        grid_spec=pltpu.PrefetchScalarGridSpec(
            num_scalar_prefetch=1,
            grid=(depths * turns,),
            in_specs=[part_specs((FIELDS, segments), 0, step) for step in range(depths)]
            + [
                part_specs((8, 128), 2, step, memory_space=pltpu.SMEM) for step in range(depths)
            ]
            + [
                pl.BlockSpec(
                    (layers, 2 * COLUMNS, LANES * wide),
                    lambda i, place: (
                        place[1] ^ (i // turns),
                        0,
                        (place[0] ^ (together * (i % turns))) // (repeats * wide),
                    ),
                ),
                fine_spec,
                coarse_spec,
            ],
            out_specs=pl.BlockSpec(
                (together, None, 2, segments),
                lambda i, place: (
                    (place[0] ^ (together * (i % turns))) // together,
                    place[1] ^ (i // turns),
                    0,
                    0,
                ),
            ),
            scratch_shapes=[pltpu.VMEM((together, FIELDS, segments), f32)]
            + [pltpu.VMEM((16 * COLUMNS, layers * LANES), bf16)] * together,
        ),
        out_shape=jax.ShapeDtypeStruct((pencils, depths, 2, segments), f32),
        compiler_params=params,
        cost_estimate=cost(groups),
    )(place, *[parts[k] for k in range(depths)], *[parts[k] for k in range(depths)], mixed, fine, coarse)
    partial = partial.reshape(groups, 2, segments)
    near = pl.pallas_call(
        near_kernel,
        in_specs=[scalars, scalars, pl.BlockSpec(), pl.BlockSpec(), anywhere],
        out_specs=pl.BlockSpec(),
        out_shape=jax.ShapeDtypeStruct((2, segments), f32),
        compiler_params=params,
        cost_estimate=cost(2),
    )(place, near_pairs, parts[0], corrections, partial)
    arrived = lax.all_to_all(partial, ("pencil", "depth"), split_axis=0, concat_axis=0, tiled=True)
    return pl.pallas_call(
        finish_kernel,
        in_specs=[resident, resident, resident],
        out_specs=resident,
        out_shape=jax.ShapeDtypeStruct((2, segments), f32),
        compiler_params=params,
    )(arrived, near, rank)


def solution(mesh):
    return jax.shard_map(
        shards,
        mesh=mesh,
        in_specs=(
            P(None, ("pencil", "depth")),
            P(None, ("pencil", "depth")),
            P(None, ("pencil", "depth")),
            P(),
            P(None, ("pencil", "depth")),
            P(("pencil", "depth"), None, None, None),
        ),
        out_specs=P(None, ("pencil", "depth")),
        check_vma=False,
    )
```

```python
import functools
import math

import jax
import jax.numpy as jnp
import ml_dtypes
import numpy as np
from jax import lax
from jax.experimental import pallas as pl
from jax.experimental.pallas import tpu as pltpu
from jax.sharding import PartitionSpec as P

GX = 2048
GY = 2048
ZL = 8

LANES = 256
INNER = 128
RADIX = GX // INNER
FINE = 16
SPAN = 24
COLUMNS = 64
FIELDS = 24
CHUNK = 256
REACH = LANES - 3
HOP = 128
TOGETHER = 4
TILE = 16

screening = 0.05
f32 = jnp.float32
bf16 = jnp.bfloat16


def halves(value):
    high = value.astype(bf16)
    return high, (value - high.astype(f32)).astype(bf16)


def host_halves(value):
    value = value.astype(np.float32)
    high = value.astype(ml_dtypes.bfloat16)
    return high, (value - high.astype(np.float32)).astype(ml_dtypes.bfloat16)


def column_tables():
    ky = np.arange(GY)[:, None]

    def table(offsets):
        phase = (ky * offsets[None, :] % GY) * (2.0 * math.pi / GY)
        return np.stack([np.cos(phase), -np.sin(phase)], axis=0)

    fine_high, fine_low = host_halves(table(np.arange(SPAN)))
    coarse_high, coarse_low = host_halves(table(FINE * np.arange(GY // FINE)))
    fine = np.concatenate([fine_high, fine_high, fine_low], axis=2)
    coarse = np.concatenate([coarse_high, coarse_low], axis=2)
    return fine, coarse


def transform_tables():
    index = np.arange(INNER)
    phase = (index[:, None] * index[None, :] % INNER) * (2.0 * math.pi / INNER)
    cos, sin = np.cos(phase), np.sin(phase)
    forward = np.block([[cos, -sin], [sin, cos]])
    twist = (np.arange(RADIX)[:, None] * index[None, :]) * (2.0 * math.pi / GX)
    twists = np.stack([np.cos(twist), -np.sin(twist)]).astype(np.float32)
    return np.stack(host_halves(forward)), np.stack(host_halves(forward.T)), twists


def one_hot(index, size):
    candidate = lax.broadcasted_iota(jnp.int16, (size, index.shape[1]), 0)
    return jnp.where(candidate == index.astype(jnp.int16), bf16(1), bf16(0))


def segment_factors(fields, fine_ref, coarse_ref):
    count = fields.shape[1]
    column = fields[19:20].astype(jnp.int32)
    pick = one_hot(column // FINE, GY // FINE)
    coarse = jnp.dot(
        coarse_ref[...], jnp.concatenate([pick, pick], axis=0), preferred_element_type=f32
    )
    fine_index = lax.broadcasted_iota(jnp.int32, (SPAN, count), 0) - column % FINE
    at = [fine_index == offset for offset in range(4)]
    parts = []
    for a in range(4):
        spread = jnp.zeros((SPAN, count), f32)
        for b in range(4):
            spread = jnp.where(at[b], fields[4 * a + b : 4 * a + b + 1], spread)
        high = spread.astype(bf16).astype(f32)
        parts.append(jnp.concatenate([high, spread - high, high], axis=0).astype(bf16))
    fine = jnp.dot(fine_ref[...], jnp.concatenate(parts, axis=1), preferred_element_type=f32)
    fines = [fine[:, a * count : (a + 1) * count] for a in range(4)]
    return coarse, fines


def thirds(value):
    high = value.astype(bf16)
    rest = value - high.astype(f32)
    middle = rest.astype(bf16)
    return high, middle, (rest - middle.astype(f32)).astype(bf16)


def order_kernel(place_ref, currents_ref, cells_ref, weights_ref, fields_ref, rank_ref, *, rows):
    count = currents_ref.shape[1]
    local = cells_ref[0:1]
    repeats = LANES // rows
    row = local // rows * LANES + place_ref[0] % repeats * rows + local % rows
    lane = lax.broadcasted_iota(jnp.int32, (1, count), 1)
    key = (row * count + lane).astype(f32)
    column = jnp.transpose(jnp.broadcast_to(key, (128, count)))[:, :1]
    rank = jnp.sum(jnp.where(column < key, 1.0, 0.0), axis=0, keepdims=True)
    pick = one_hot(rank.astype(jnp.int32), count)
    values = jnp.concatenate(
        [
            weights_ref[...],
            currents_ref[...],
            row.astype(f32),
            cells_ref[1:2].astype(f32),
            jnp.zeros((FIELDS - 20, count), f32),
        ],
        axis=0,
    )
    ordered = sum(
        lax.dot_general(part, pick, (((1,), (1,)), ((), ())), preferred_element_type=f32)
        for part in thirds(values)
    )
    ends = jnp.zeros((1, count), f32)
    for chunk in range(count // CHUNK):
        for side in range(2):
            at = lane == chunk * CHUNK + side * (CHUNK - 1)
            value = jnp.sum(jnp.where(at, ordered[18:19], 0.0), axis=1, keepdims=True)
            ends = ends + jnp.where(lane == 2 * chunk + side, value, 0.0)
    line = lax.broadcasted_iota(jnp.int32, (FIELDS, count), 0)
    ordered = jnp.where(line == 20, ends, ordered)
    for part in range(2):
        ordered = jnp.where(line == 21 + part, currents_ref[part : part + 1], ordered)
    fields_ref[...] = ordered
    rank_ref[...] = rank


def finish_kernel(arrived_ref, near_ref, rank_ref, out_ref):
    far = jnp.sum(arrived_ref[...], axis=0)
    count = far.shape[1]
    pick = one_hot(rank_ref[...].astype(jnp.int32), count)
    padded = jnp.concatenate([far, jnp.zeros((14, count), f32)], axis=0)
    total = sum(jnp.dot(part, pick, preferred_element_type=f32) for part in thirds(padded))
    out_ref[...] = total[:2] + near_ref[...]


def windows(fields_ref, ends, block, total_rows):
    chunks = []
    for chunk in range(fields_ref.shape[2] // CHUNK):
        low = ends(block, 2 * chunk).astype(jnp.int32)
        high = ends(block, 2 * chunk + 1).astype(jnp.int32)
        start = jnp.minimum(low // HOP * HOP, total_rows - LANES)
        more = (jnp.maximum(high + 1 - (start + REACH), 0) + HOP - 1) // HOP
        chunks.append((start, more))

    def window(chunk, number, visit):
        first = isinstance(number, int)
        row = fields_ref[block, 18:19, chunk * CHUNK : (chunk + 1) * CHUNK].astype(jnp.int32)
        begin = pl.multiple_of(chunks[chunk][0] + number * HOP, HOP)
        apart = row - begin
        inside = (apart >= (0 if first else REACH - HOP)) & (apart < REACH)
        visit(chunk, begin, one_hot(jnp.where(inside, apart, -1), LANES), first)

    def begin_all(visit):
        for chunk in range(len(chunks)):
            window(chunk, 0, visit)

    def finish_all(visit):
        @pl.when(sum(more for _, more in chunks) > 0)
        def _():
            for chunk in range(len(chunks)):

                def again(number, carry, chunk=chunk):
                    window(chunk, number, visit)
                    return carry

                lax.fori_loop(1, chunks[chunk][1] + 1, again, 0)

    return begin_all, finish_all


def spread_kernel(
    place_ref, before_ref, fields_ref, ends_ref, fine_ref, coarse_ref, out_ref, *scratch, repeats, together
):
    layers = out_ref.shape[0]
    half = 8 * COLUMNS
    rest = []
    for block in range(together):
        factor_ref, total_ref = scratch[2 * block : 2 * block + 2]
        fields = fields_ref[block]
        coarse, fines = segment_factors(fields, fine_ref, coarse_ref)
        current_re, current_im = fields[16:17], fields[17:18]
        phase_re, phase_im = coarse[:COLUMNS], coarse[COLUMNS:]
        wave_re = phase_re * current_re - phase_im * current_im
        wave_im = phase_re * current_im + phase_im * current_re
        base = 0
        for fine in fines:
            fine_re, fine_im = fine[:COLUMNS], fine[COLUMNS:]
            for value in (
                wave_re * fine_re - wave_im * fine_im,
                wave_re * fine_im + wave_im * fine_re,
            ):
                high, low = halves(value)
                factor_ref[base : base + COLUMNS] = high
                factor_ref[half + base : half + base + COLUMNS] = low
                base += COLUMNS
        total_ref[...] = jnp.zeros_like(total_ref)

        def visit(chunk, begin, select, first, factor_ref=factor_ref, total_ref=total_ref):
            factors = factor_ref[:, chunk * CHUNK : (chunk + 1) * CHUNK]
            form = (((1,), (1,)), ((), ()))
            spread = lax.dot_general(factors, select, form, preferred_element_type=f32)
            spread = spread[:half] + spread[half:]
            total = spread[: 2 * COLUMNS]
            for a in range(1, 4):
                total = total + pltpu.roll(spread[2 * COLUMNS * a : 2 * COLUMNS * (a + 1)], a, 1)
            total_ref[:, pl.ds(begin, LANES)] += total

        begin_all, finish_all = windows(
            fields_ref, lambda block, at: ends_ref[block, 4, at], block, layers * LANES
        )
        begin_all(visit)
        rest.append((finish_all, visit))
    for finish_all, visit in rest:
        finish_all(visit)
    fresh = pl.program_id(0) * together % min(repeats, pl.num_programs(0) * together) == 0
    for layer in range(layers):
        pieces = [
            scratch[2 * block + 1][:, layer * LANES : (layer + 1) * LANES]
            for block in range(together)
        ]
        if repeats == 1:
            for block, piece in enumerate(pieces):
                spot = (place_ref[0] % together) ^ block
                out_ref[layer, :, pl.ds(pl.multiple_of(spot * LANES, LANES), LANES)] = piece
        else:
            out_ref[layer] = jnp.where(fresh, before_ref[layer], out_ref[layer]) + sum(pieces)


def sample_kernel(place_ref, *refs, depths, together):
    parts, ends_refs, refs = refs[:depths], refs[depths : 2 * depths], refs[2 * depths :]
    field_ref, fine_ref, coarse_ref, out_ref, fields_ref, *scratch = refs
    turn_now = pl.program_id(0) // (pl.num_programs(0) // depths)
    for step in range(depths):

        @pl.when(turn_now == step)
        def _(step=step):
            fields_ref[...] = parts[step][...]

    def ends(block, at):
        value = ends_refs[0][block, 4, at]
        for step in range(1, depths):
            value = jnp.where(turn_now == step, ends_refs[step][block, 4, at], value)
        return value

    layers = field_ref.shape[0]
    total_rows = layers * LANES
    half = 8 * COLUMNS

    def reduced(sampled, coarse, fines):
        sum_re, sum_im = 0.0, 0.0
        for a, fine in enumerate(fines):
            fine_re, fine_im = fine[:COLUMNS], fine[COLUMNS:]
            base = 2 * COLUMNS * a
            value_re = sampled[base : base + COLUMNS]
            value_im = sampled[base + COLUMNS : base + 2 * COLUMNS]
            sum_re = sum_re + value_re * fine_re + value_im * fine_im
            sum_im = sum_im + value_im * fine_re - value_re * fine_im
        phase_re, phase_im = coarse[:COLUMNS], coarse[COLUMNS:]
        far_re = jnp.sum(sum_re * phase_re + sum_im * phase_im, axis=0, keepdims=True)
        far_im = jnp.sum(sum_im * phase_re - sum_re * phase_im, axis=0, keepdims=True)
        return jnp.concatenate([far_re, far_im], axis=0)[None]

    rest = []
    for block in range(together):
        factor_ref = scratch[block]
        spot = (place_ref[0] % together) ^ block
        if field_ref.shape[2] == LANES:
            at = pl.ds(0, LANES)
        else:
            at = pl.ds(pl.multiple_of(spot * LANES, LANES), LANES)
        field = jnp.concatenate([field_ref[layer, :, at] for layer in range(layers)], axis=1)
        for a in range(4):
            moved = pltpu.roll(field, total_rows - a, 1) if a else field
            high, low = halves(moved)
            base = 2 * COLUMNS * a
            factor_ref[base : base + 2 * COLUMNS] = high
            factor_ref[half + base : half + base + 2 * COLUMNS] = low
        coarse, fines = segment_factors(fields_ref[block], fine_ref, coarse_ref)

        def visit(
            chunk,
            begin,
            select,
            first,
            block=block,
            factor_ref=factor_ref,
            spot=spot,
            coarse=coarse,
            fines=fines,
        ):
            sampled = jnp.dot(
                factor_ref[:, pl.ds(begin, LANES)], select, preferred_element_type=f32
            )
            sampled = sampled[:half] + sampled[half:]
            cut = slice(chunk * CHUNK, (chunk + 1) * CHUNK)
            if first:
                far = reduced(sampled, coarse[:, cut], [fine[:, cut] for fine in fines])
                out_ref[pl.ds(spot, 1), :, cut] = far
            else:
                again = segment_factors(fields_ref[block, :, cut], fine_ref, coarse_ref)
                out_ref[pl.ds(spot, 1), :, cut] += reduced(sampled, *again)

        begin_all, finish_all = windows(fields_ref, ends, block, total_rows)
        begin_all(visit)
        rest.append((finish_all, visit))
    for finish_all, visit in rest:
        finish_all(visit)


def turn(value, step, size, sign):
    real, imag = value
    if step == 0:
        return value
    if 4 * step == size:
        return (-imag, real) if sign > 0 else (imag, -real)
    half = math.sqrt(0.5)
    if 8 * step == size:
        if sign > 0:
            return ((real - imag) * half, (real + imag) * half)
        return ((real + imag) * half, (imag - real) * half)
    cos = math.cos(2.0 * math.pi * step / size)
    sin = sign * math.sin(2.0 * math.pi * step / size)
    return (real * cos - imag * sin, real * sin + imag * cos)


def butterflies(values, sign):
    size = len(values)
    if size == 1:
        return values
    even = butterflies(values[0::2], sign)
    odd = butterflies(values[1::2], sign)
    low, high = [], []
    for k in range(size // 2):
        moved = turn(odd[k], k, size, sign)
        low.append((even[k][0] + moved[0], even[k][1] + moved[1]))
        high.append((even[k][0] - moved[0], even[k][1] - moved[1]))
    return low + high


def dense(value, matrix_ref):
    high, low = halves(value)
    return (
        jnp.dot(high, matrix_ref[0], preferred_element_type=f32)
        + jnp.dot(low, matrix_ref[0], preferred_element_type=f32)
        + jnp.dot(high, matrix_ref[1], preferred_element_type=f32)
    )


def mix(spec, kappa, keep, soil_ref, reflection):
    upper = (soil_ref[0, 0], soil_ref[1, 0])
    lower = (soil_ref[0, 1], soil_ref[1, 1])
    decay = jnp.exp(-kappa)
    base = jnp.where(keep, 1.0 / (GX * GY) / (kappa + screening), 0.0)
    source = []
    for layer in range(ZL):
        rho_re, rho_im = upper if layer < ZL // 2 else lower
        re, im = spec[layer]
        source.append(((rho_re * re - rho_im * im) * base, (rho_re * im + rho_im * re) * base))
    below = [None] * ZL
    below[ZL - 1] = (jnp.zeros_like(kappa), jnp.zeros_like(kappa))
    for layer in range(ZL - 2, -1, -1):
        below[layer] = tuple(decay * (below[layer + 1][i] + source[layer + 1][i]) for i in range(2))
    surface = tuple(decay * (below[0][i] + source[0][i]) for i in range(2))
    image = (
        reflection[0] * surface[0] - reflection[1] * surface[1],
        reflection[0] * surface[1] + reflection[1] * surface[0],
    )
    above = source[0]
    mixed = []
    for layer in range(ZL):
        if layer:
            above = tuple(decay * above[i] + source[layer][i] for i in range(2))
            image = tuple(decay * image[i] for i in range(2))
        mixed.append(tuple(above[i] + below[layer][i] + image[i] for i in range(2)))
    return mixed


def reflect(soil_ref, shape):
    upper_re, lower_re = (jnp.full(shape, soil_ref[0, i], f32) for i in range(2))
    upper_im, lower_im = (jnp.full(shape, soil_ref[1, i], f32) for i in range(2))
    denom_re, denom_im = upper_re + lower_re, upper_im + lower_im
    numer_re, numer_im = lower_re - upper_re, lower_im - upper_im
    magnitude = denom_re * denom_re + denom_im * denom_im
    return (
        (numer_re * denom_re + numer_im * denom_im) / magnitude,
        (numer_im * denom_re - numer_re * denom_im) / magnitude,
    )


def mix_kernel(place_ref, soil_ref, spec_ref, forward_ref, inverse_ref, twist_ref, out_ref, *, columns):
    tile = spec_ref.shape[2]
    rows = ZL * tile
    real = spec_ref[:, 0].reshape(rows, GX)
    imag = spec_ref[:, 1].reshape(rows, GX)
    cut = [slice(n * INNER, (n + 1) * INNER) for n in range(RADIX)]
    values = butterflies([(real[:, c], imag[:, c]) for c in cut], -1.0)
    local = pl.program_id(0) * tile + lax.broadcasted_iota(jnp.int32, (tile, INNER), 0)
    keep = local < columns
    ky = place_ref[2] + local
    reflection = reflect(soil_ref, (tile, INNER))
    freq_y = jnp.where(ky < (GY - 1) // 2 + 1, ky, ky - GY).astype(f32) / GY
    inner = lax.broadcasted_iota(jnp.int32, (tile, INNER), 1)
    back = []
    for k in range(RADIX):
        twist_re, twist_im = twist_ref[0, k : k + 1], twist_ref[1, k : k + 1]
        re, im = values[k]
        turned = (re * twist_re - im * twist_im, re * twist_im + im * twist_re) if k else (re, im)
        spectrum = dense(jnp.concatenate(turned, axis=1), forward_ref)
        kx = k + RADIX * inner
        freq_x = jnp.where(kx < (GX - 1) // 2 + 1, kx, kx - GX).astype(f32) / GX
        kappa = 2.0 * math.pi * jnp.sqrt(freq_x * freq_x + freq_y * freq_y)
        spec = [
            (spectrum[s * tile : (s + 1) * tile, :INNER], spectrum[s * tile : (s + 1) * tile, INNER:])
            for s in range(ZL)
        ]
        mixed = mix(spec, kappa, keep, soil_ref, reflection)
        stacked = jnp.concatenate([jnp.concatenate(pair, axis=1) for pair in mixed], axis=0)
        field = dense(stacked, inverse_ref)
        re, im = field[:, :INNER], field[:, INNER:]
        turned = (re * twist_re + im * twist_im, im * twist_re - re * twist_im) if k else (re, im)
        back.append(turned)
    values = butterflies(back, 1.0)
    for n in range(RADIX):
        out_ref[:, 0, :, cut[n]] = values[n][0].reshape(ZL, tile, INNER)
        out_ref[:, 1, :, cut[n]] = values[n][1].reshape(ZL, tile, INNER)


def partner(value, axis, step):
    count = lax.axis_size(axis)
    return lax.ppermute(value, axis, [(i, i ^ step) for i in range(count)])


def near_kernel(place_ref, pairs_ref, own_ref, corrections_ref, after_ref, out_ref):
    slots, _, size, _ = corrections_ref.shape
    pencils, _, segments = own_ref.shape
    blocks = segments // size
    out_ref[...] = jnp.zeros_like(out_ref)

    def add(slot, carry):
        target, source = pairs_ref[0, slot], pairs_ref[1, slot]
        live = pairs_ref[2, slot].astype(f32)
        pencil = jnp.clip(place_ref[0] + source // blocks - 1, 0, pencils - 1)
        index = pencil ^ place_ref[0]
        at = pl.ds(pl.multiple_of(source % blocks * size, size), size)
        current = own_ref[index, 21:23, at] * live
        real, imag = corrections_ref[slot, 0], corrections_ref[slot, 1]
        piece_re = real * current[0:1] - imag * current[1:2]
        piece_im = real * current[1:2] + imag * current[0:1]
        to = pl.ds(pl.multiple_of(target * size, size), size)
        out_ref[0:1, to] += jnp.sum(jnp.transpose(piece_re), axis=0, keepdims=True)
        out_ref[1:2, to] += jnp.sum(jnp.transpose(piece_im), axis=0, keepdims=True)
        return carry

    lax.fori_loop(0, slots, add, 0)


def shards(currents, stencil_cells, stencil_weights, soil, near_pairs, corrections):
    pencils = lax.axis_size("pencil")
    depths = lax.axis_size("depth")
    pencil = lax.axis_index("pencil")
    depth = lax.axis_index("depth")
    segments = currents.shape[1]
    layers = ZL // depths
    rows = GX // pencils
    repeats = LANES // rows
    groups = pencils * depths
    columns = GY // groups
    first = (pencil * depths + depth) * columns

    bits = [1 << i for i in range(pencils.bit_length() - 1)]
    if repeats == 1:
        bits = bits[:1] + bits[:0:-1]
    place = jnp.stack([pencil, depth, first]).astype(jnp.int32)
    params = pltpu.CompilerParams(vmem_limit_bytes=48 * 1024 * 1024)
    anywhere = pl.BlockSpec(memory_space=pl.ANY)
    scalars = pl.BlockSpec(memory_space=pltpu.SMEM)
    resident = pl.BlockSpec(memory_space=pltpu.VMEM)
    fields, rank = pl.pallas_call(
        functools.partial(order_kernel, rows=rows),
        in_specs=[scalars] + [pl.BlockSpec()] * 3,
        out_specs=[pl.BlockSpec()] * 2,
        out_shape=[
            jax.ShapeDtypeStruct((FIELDS, segments), f32),
            jax.ShapeDtypeStruct((1, segments), f32),
        ],
        compiler_params=pltpu.CompilerParams(vmem_limit_bytes=62 * 1024 * 1024),
    )(place, currents, stencil_cells, stencil_weights)


    def offset(index):
        return sum((index >> j & 1) * bit for j, bit in enumerate(bits))


    fine, coarse = column_tables()
    fine = lax.dynamic_slice_in_dim(
        jnp.asarray(np.pad(fine, ((0, 0), (0, COLUMNS), (0, 0)))), first, COLUMNS, axis=1
    ).reshape(2 * COLUMNS, -1)
    coarse = lax.dynamic_slice_in_dim(
        jnp.asarray(np.pad(coarse, ((0, 0), (0, COLUMNS), (0, 0)))), first, COLUMNS, axis=1
    ).reshape(2 * COLUMNS, -1)
    forward, inverse, twists = transform_tables()
    def fields_specs(together):
        return [
            pl.BlockSpec((together, FIELDS, segments), lambda i, place: (i, 0, 0)),
            pl.BlockSpec((together, 8, 128), lambda i, place: (i, 2, 0), memory_space=pltpu.SMEM),
        ]

    def lead(offsets, together):
        firsts = offsets[::together]
        if firsts == list(range(firsts[0], firsts[0] + len(offsets), together)):
            return lambda i: firsts[0] + together * i
        return lambda i: sum(jnp.where(i == k, first, 0) for k, first in enumerate(firsts))

    def region(offsets, step, together):
        wide = together if repeats == 1 else 1
        first = lead(offsets, together)
        return pl.BlockSpec(
            (layers, 2 * COLUMNS, LANES * wide),
            lambda i, place: (place[1] ^ step, 0, (place[0] ^ first(i)) // (repeats * wide)),
        )

    fine_spec = pl.BlockSpec(fine.shape, lambda i, place: (0, 0))
    coarse_spec = pl.BlockSpec(coarse.shape, lambda i, place: (0, 0))

    def cost(blocks):
        return pl.CostEstimate(
            flops=blocks * 2_000_000_000, bytes_accessed=blocks * 600_000, transcendentals=0
        )

    def spread(grid, chunk, offsets, step, together):
        fresh = grid is None
        if fresh and repeats > 1:
            grid, fresh = jnp.zeros((ZL, 2 * COLUMNS, GX), f32), False
        before = jnp.zeros((8, 128), f32) if fresh else grid
        return pl.pallas_call(
            functools.partial(spread_kernel, repeats=repeats, together=together),
            grid_spec=pltpu.PrefetchScalarGridSpec(
                num_scalar_prefetch=1,
                grid=(chunk.shape[0] // together,),
                in_specs=[
                    anywhere if repeats == 1 else region(offsets, step, together),
                    *fields_specs(together),
                    fine_spec,
                    coarse_spec,
                ],
                out_specs=region(offsets, step, together),
                scratch_shapes=[
                    pltpu.VMEM((16 * COLUMNS, segments), bf16),
                    pltpu.VMEM((2 * COLUMNS, layers * LANES), f32),
                ]
                * together,
            ),
            out_shape=jax.ShapeDtypeStruct((ZL, 2 * COLUMNS, GX), f32),
            input_output_aliases={} if fresh else {1: 0},
            compiler_params=params,
            cost_estimate=cost(chunk.shape[0]),
        )(place, before, chunk, chunk, fine, coarse)

    own, offsets, grid = fields[None], [0], None
    for number, bit in enumerate(bits):
        arrived = partner(own, "pencil", bit)
        fresh = [offset ^ bit for offset in offsets]
        known = len(offsets)
        offsets = offsets + fresh
        pieces, order = [], list(range(2 * known))
        if number == len(bits) - 1:
            order = [int(index) for index in np.argsort(np.array(offsets))]
        while order:
            run = 1
            while run < len(order) and order[run] == order[0] + run and order[run] != known:
                run += 1
            source, at = (own, order[0]) if order[0] < known else (arrived, order[0] - known)
            pieces.append(source[at : at + run])
            order = order[run:]
        own = jnp.concatenate(pieces)
        if number == 0:
            grid = spread(grid, own, offsets, 0, 2)
        else:
            grid = spread(grid, arrived, fresh, 0, 2)
    offsets = list(range(pencils))
    together = min(TOGETHER, pencils)
    parts = {0: own}
    for step in range(1, depths):
        if step & (step - 1) == 0:
            parts[step] = partner(own, "depth", step)
    for step in range(1, depths):
        grid = spread(grid, parts[step], offsets, step, together)
        later = step + 2
        if later < depths and later not in parts:
            low = later & -later
            source, grid = lax.optimization_barrier((parts[later ^ low], grid))
            parts[later] = partner(source, "depth", low)

    tile_spec = pl.BlockSpec((ZL, 2, TILE, GX), lambda t: (0, 0, t, 0))
    whole = lambda *shape: pl.BlockSpec(shape, lambda t: (0,) * len(shape))
    mixed = pl.pallas_call(
        functools.partial(mix_kernel, columns=columns),
        grid=(COLUMNS // TILE,),
        in_specs=[
            pl.BlockSpec(memory_space=pltpu.SMEM),
            pl.BlockSpec(memory_space=pltpu.SMEM),
            tile_spec,
            whole(*forward.shape),
            whole(*inverse.shape),
            whole(*twists.shape),
        ],
        out_specs=tile_spec,
        out_shape=jax.ShapeDtypeStruct((ZL, 2, COLUMNS, GX), f32),
        compiler_params=params,
    )(
        place,
        soil,
        grid.reshape(ZL, 2, COLUMNS, GX),
        jnp.asarray(forward),
        jnp.asarray(inverse),
        jnp.asarray(twists),
    ).reshape(ZL, 2 * COLUMNS, GX)
    turns = pencils // together
    wide = together if repeats == 1 else 1

    def part_specs(block, line, step, **kinds):
        return pl.BlockSpec(
            (together,) + block,
            lambda i, place: (jnp.clip(i - step * turns, 0, turns - 1), line, 0),
            **kinds,
        )

    partial = pl.pallas_call(
        functools.partial(sample_kernel, depths=depths, together=together),
        grid_spec=pltpu.PrefetchScalarGridSpec(
            num_scalar_prefetch=1,
            grid=(depths * turns,),
            in_specs=[part_specs((FIELDS, segments), 0, step) for step in range(depths)]
            + [
                part_specs((8, 128), 2, step, memory_space=pltpu.SMEM) for step in range(depths)
            ]
            + [
                pl.BlockSpec(
                    (layers, 2 * COLUMNS, LANES * wide),
                    lambda i, place: (
                        place[1] ^ (i // turns),
                        0,
                        (place[0] ^ (together * (i % turns))) // (repeats * wide),
                    ),
                ),
                fine_spec,
                coarse_spec,
            ],
            out_specs=pl.BlockSpec(
                (together, None, 2, segments),
                lambda i, place: (
                    (place[0] ^ (together * (i % turns))) // together,
                    place[1] ^ (i // turns),
                    0,
                    0,
                ),
            ),
            scratch_shapes=[pltpu.VMEM((together, FIELDS, segments), f32)]
            + [pltpu.VMEM((16 * COLUMNS, layers * LANES), bf16)] * together,
        ),
        out_shape=jax.ShapeDtypeStruct((pencils, depths, 2, segments), f32),
        compiler_params=params,
        cost_estimate=cost(groups),
    )(place, *[parts[k] for k in range(depths)], *[parts[k] for k in range(depths)], mixed, fine, coarse)
    partial = partial.reshape(groups, 2, segments)
    near = pl.pallas_call(
        near_kernel,
        in_specs=[scalars, scalars, pl.BlockSpec(), pl.BlockSpec(), anywhere],
        out_specs=pl.BlockSpec(),
        out_shape=jax.ShapeDtypeStruct((2, segments), f32),
        compiler_params=params,
        cost_estimate=cost(2),
    )(place, near_pairs, parts[0], corrections, partial)
    arrived = lax.all_to_all(partial, ("pencil", "depth"), split_axis=0, concat_axis=0, tiled=True)
    return pl.pallas_call(
        finish_kernel,
        in_specs=[resident, resident, resident],
        out_specs=resident,
        out_shape=jax.ShapeDtypeStruct((2, segments), f32),
        compiler_params=params,
    )(arrived, near, rank)


def solution(mesh):
    return jax.shard_map(
        shards,
        mesh=mesh,
        in_specs=(
            P(None, ("pencil", "depth")),
            P(None, ("pencil", "depth")),
            P(None, ("pencil", "depth")),
            P(),
            P(None, ("pencil", "depth")),
            P(("pencil", "depth"), None, None, None),
        ),
        out_specs=P(None, ("pencil", "depth")),
        check_vma=False,
    )
```

```python
import functools
import math

import jax
import jax.numpy as jnp
import ml_dtypes
import numpy as np
from jax import lax
from jax.experimental import pallas as pl
from jax.experimental.pallas import tpu as pltpu
from jax.sharding import PartitionSpec as P

GX = 2048
GY = 2048
ZL = 8

LANES = 256
INNER = 128
RADIX = GX // INNER
FINE = 16
SPAN = 24
COLUMNS = 64
FIELDS = 24
CHUNK = 256
REACH = LANES - 3
HOP = 128
TOGETHER = 4
TILE = 16

screening = 0.05
f32 = jnp.float32
bf16 = jnp.bfloat16


def halves(value):
    high = value.astype(bf16)
    return high, (value - high.astype(f32)).astype(bf16)


def host_halves(value):
    value = value.astype(np.float32)
    high = value.astype(ml_dtypes.bfloat16)
    return high, (value - high.astype(np.float32)).astype(ml_dtypes.bfloat16)


def column_tables():
    ky = np.arange(GY)[:, None]

    def table(offsets):
        phase = (ky * offsets[None, :] % GY) * (2.0 * math.pi / GY)
        return np.stack([np.cos(phase), -np.sin(phase)], axis=0)

    fine_high, fine_low = host_halves(table(np.arange(SPAN)))
    coarse_high, coarse_low = host_halves(table(FINE * np.arange(GY // FINE)))
    fine = np.concatenate([fine_high, fine_high, fine_low], axis=2)
    coarse = np.concatenate([coarse_high, coarse_low], axis=2)
    return fine, coarse


def transform_tables():
    index = np.arange(INNER)
    phase = (index[:, None] * index[None, :] % INNER) * (2.0 * math.pi / INNER)
    cos, sin = np.cos(phase), np.sin(phase)
    forward = np.block([[cos, -sin], [sin, cos]])
    twist = (np.arange(RADIX)[:, None] * index[None, :]) * (2.0 * math.pi / GX)
    twists = np.stack([np.cos(twist), -np.sin(twist)]).astype(np.float32)
    return np.stack(host_halves(forward)), np.stack(host_halves(forward.T)), twists


def one_hot(index, size):
    candidate = lax.broadcasted_iota(jnp.int16, (size, index.shape[1]), 0)
    return jnp.where(candidate == index.astype(jnp.int16), bf16(1), bf16(0))


def segment_factors(fields, fine_ref, coarse_ref):
    count = fields.shape[1]
    column = fields[19:20].astype(jnp.int32)
    pick = one_hot(column // FINE, GY // FINE)
    coarse = jnp.dot(
        coarse_ref[...], jnp.concatenate([pick, pick], axis=0), preferred_element_type=f32
    )
    fine_index = lax.broadcasted_iota(jnp.int32, (SPAN, count), 0) - column % FINE
    at = [fine_index == offset for offset in range(4)]
    parts = []
    for a in range(4):
        spread = jnp.zeros((SPAN, count), f32)
        for b in range(4):
            spread = jnp.where(at[b], fields[4 * a + b : 4 * a + b + 1], spread)
        high = spread.astype(bf16).astype(f32)
        parts.append(jnp.concatenate([high, spread - high, high], axis=0).astype(bf16))
    fine = jnp.dot(fine_ref[...], jnp.concatenate(parts, axis=1), preferred_element_type=f32)
    fines = [fine[:, a * count : (a + 1) * count] for a in range(4)]
    return coarse, fines


def moved(value, pick, form):
    rows = value.shape[0]
    high = value.astype(bf16).astype(f32)
    middle = (value - high).astype(bf16).astype(f32)
    pieces = jnp.concatenate([high, middle, value - high - middle], axis=0).astype(bf16)
    out = lax.dot_general(pieces, pick, (form, ((), ())), preferred_element_type=f32)
    return out[:rows] + out[rows : 2 * rows] + out[2 * rows :]


def order_kernel(place_ref, currents_ref, cells_ref, weights_ref, fields_ref, rank_ref, *, rows):
    count = currents_ref.shape[1]
    local = cells_ref[0:1]
    repeats = LANES // rows
    row = local // rows * LANES + place_ref[0] % repeats * rows + local % rows
    lane = lax.broadcasted_iota(jnp.int32, (1, count), 1)
    key = (row * count + lane).astype(f32)
    column = jnp.transpose(jnp.broadcast_to(key, (128, count)))[:, :1]
    rank = jnp.sum(jnp.where(column < key, 1.0, 0.0), axis=0, keepdims=True)
    pick = one_hot(rank.astype(jnp.int32), count)
    values = jnp.concatenate(
        [
            weights_ref[...],
            currents_ref[...],
            row.astype(f32),
            cells_ref[1:2].astype(f32),
            jnp.zeros((FIELDS - 20, count), f32),
        ],
        axis=0,
    )
    ordered = moved(values, pick, ((1,), (1,)))
    ends = jnp.zeros((1, count), f32)
    for chunk in range(count // CHUNK):
        for side in range(2):
            at = lane == chunk * CHUNK + side * (CHUNK - 1)
            value = jnp.sum(jnp.where(at, ordered[18:19], 0.0), axis=1, keepdims=True)
            ends = ends + jnp.where(lane == 2 * chunk + side, value, 0.0)
    line = lax.broadcasted_iota(jnp.int32, (FIELDS, count), 0)
    ordered = jnp.where(line == 20, ends, ordered)
    for part in range(2):
        ordered = jnp.where(line == 21 + part, currents_ref[part : part + 1], ordered)
    fields_ref[...] = ordered
    rank_ref[...] = rank


def finish_kernel(arrived_ref, near_ref, rank_ref, out_ref):
    far = jnp.sum(arrived_ref[...], axis=0)
    count = far.shape[1]
    pick = one_hot(rank_ref[...].astype(jnp.int32), count)
    padded = jnp.concatenate([far, jnp.zeros((6, count), f32)], axis=0)
    total = moved(padded, pick, ((1,), (0,)))
    out_ref[...] = total[:2] + near_ref[...]


def windows(fields_ref, ends, block, total_rows):
    chunks = []
    for chunk in range(fields_ref.shape[2] // CHUNK):
        low = ends(block, 2 * chunk).astype(jnp.int32)
        high = ends(block, 2 * chunk + 1).astype(jnp.int32)
        start = jnp.minimum(low // HOP * HOP, total_rows - LANES)
        more = (jnp.maximum(high + 1 - (start + REACH), 0) + HOP - 1) // HOP
        chunks.append((start, more))

    def window(chunk, number, visit):
        first = isinstance(number, int)
        row = fields_ref[block, 18:19, chunk * CHUNK : (chunk + 1) * CHUNK].astype(jnp.int32)
        begin = pl.multiple_of(chunks[chunk][0] + number * HOP, HOP)
        apart = row - begin
        inside = (apart >= (0 if first else REACH - HOP)) & (apart < REACH)
        visit(chunk, begin, one_hot(jnp.where(inside, apart, -1), LANES), first)

    def begin_all(visit):
        for chunk in range(len(chunks)):
            window(chunk, 0, visit)

    def finish_all(visit):
        @pl.when(sum(more for _, more in chunks) > 0)
        def _():
            for chunk in range(len(chunks)):

                def again(number, carry, chunk=chunk):
                    window(chunk, number, visit)
                    return carry

                lax.fori_loop(1, chunks[chunk][1] + 1, again, 0)

    return begin_all, finish_all


def spread_kernel(
    place_ref, before_ref, fields_ref, ends_ref, fine_ref, coarse_ref, out_ref, *scratch, repeats, together
):
    layers = out_ref.shape[0]
    half = 8 * COLUMNS
    rest = []
    for block in range(together):
        factor_ref, total_ref = scratch[2 * block : 2 * block + 2]
        fields = fields_ref[block]
        coarse, fines = segment_factors(fields, fine_ref, coarse_ref)
        current_re, current_im = fields[16:17], fields[17:18]
        phase_re, phase_im = coarse[:COLUMNS], coarse[COLUMNS:]
        wave_re = phase_re * current_re - phase_im * current_im
        wave_im = phase_re * current_im + phase_im * current_re
        base = 0
        for fine in fines:
            fine_re, fine_im = fine[:COLUMNS], fine[COLUMNS:]
            for value in (
                wave_re * fine_re - wave_im * fine_im,
                wave_re * fine_im + wave_im * fine_re,
            ):
                high, low = halves(value)
                factor_ref[base : base + COLUMNS] = high
                factor_ref[half + base : half + base + COLUMNS] = low
                base += COLUMNS
        total_ref[...] = jnp.zeros_like(total_ref)

        def visit(chunk, begin, select, first, factor_ref=factor_ref, total_ref=total_ref):
            factors = factor_ref[:, chunk * CHUNK : (chunk + 1) * CHUNK]
            form = (((1,), (1,)), ((), ()))
            spread = lax.dot_general(factors, select, form, preferred_element_type=f32)
            spread = spread[:half] + spread[half:]
            total = spread[: 2 * COLUMNS]
            for a in range(1, 4):
                total = total + pltpu.roll(spread[2 * COLUMNS * a : 2 * COLUMNS * (a + 1)], a, 1)
            total_ref[:, pl.ds(begin, LANES)] += total

        begin_all, finish_all = windows(
            fields_ref, lambda block, at: ends_ref[block, 4, at], block, layers * LANES
        )
        begin_all(visit)
        rest.append((finish_all, visit))
    for finish_all, visit in rest:
        finish_all(visit)
    fresh = pl.program_id(0) * together % min(repeats, pl.num_programs(0) * together) == 0
    for layer in range(layers):
        pieces = [
            scratch[2 * block + 1][:, layer * LANES : (layer + 1) * LANES]
            for block in range(together)
        ]
        if repeats == 1:
            for block, piece in enumerate(pieces):
                spot = (place_ref[0] % together) ^ block
                out_ref[layer, :, pl.ds(pl.multiple_of(spot * LANES, LANES), LANES)] = piece
        else:
            out_ref[layer] = jnp.where(fresh, before_ref[layer], out_ref[layer]) + sum(pieces)


def sample_kernel(place_ref, *refs, depths, together):
    parts, ends_refs, refs = refs[:depths], refs[depths : 2 * depths], refs[2 * depths :]
    field_ref, fine_ref, coarse_ref, out_ref, fields_ref, *scratch = refs
    turn_now = pl.program_id(0) // (pl.num_programs(0) // depths)
    for step in range(depths):

        @pl.when(turn_now == step)
        def _(step=step):
            fields_ref[...] = parts[step][...]

    def ends(block, at):
        value = ends_refs[0][block, 4, at]
        for step in range(1, depths):
            value = jnp.where(turn_now == step, ends_refs[step][block, 4, at], value)
        return value

    layers = field_ref.shape[0]
    total_rows = layers * LANES
    half = 8 * COLUMNS

    def reduced(sampled, coarse, fines):
        sum_re, sum_im = 0.0, 0.0
        for a, fine in enumerate(fines):
            fine_re, fine_im = fine[:COLUMNS], fine[COLUMNS:]
            base = 2 * COLUMNS * a
            value_re = sampled[base : base + COLUMNS]
            value_im = sampled[base + COLUMNS : base + 2 * COLUMNS]
            sum_re = sum_re + value_re * fine_re + value_im * fine_im
            sum_im = sum_im + value_im * fine_re - value_re * fine_im
        phase_re, phase_im = coarse[:COLUMNS], coarse[COLUMNS:]
        far_re = jnp.sum(sum_re * phase_re + sum_im * phase_im, axis=0, keepdims=True)
        far_im = jnp.sum(sum_im * phase_re - sum_re * phase_im, axis=0, keepdims=True)
        return jnp.concatenate([far_re, far_im], axis=0)[None]

    rest = []
    for block in range(together):
        factor_ref = scratch[block]
        spot = (place_ref[0] % together) ^ block
        if field_ref.shape[2] == LANES:
            at = pl.ds(0, LANES)
        else:
            at = pl.ds(pl.multiple_of(spot * LANES, LANES), LANES)
        field = jnp.concatenate([field_ref[layer, :, at] for layer in range(layers)], axis=1)
        for a in range(4):
            shifted = pltpu.roll(field, total_rows - a, 1) if a else field
            high, low = halves(shifted)
            base = 2 * COLUMNS * a
            factor_ref[base : base + 2 * COLUMNS] = high
            factor_ref[half + base : half + base + 2 * COLUMNS] = low
        coarse, fines = segment_factors(fields_ref[block], fine_ref, coarse_ref)

        def visit(
            chunk,
            begin,
            select,
            first,
            block=block,
            factor_ref=factor_ref,
            spot=spot,
            coarse=coarse,
            fines=fines,
        ):
            sampled = jnp.dot(
                factor_ref[:, pl.ds(begin, LANES)], select, preferred_element_type=f32
            )
            sampled = sampled[:half] + sampled[half:]
            cut = slice(chunk * CHUNK, (chunk + 1) * CHUNK)
            if first:
                far = reduced(sampled, coarse[:, cut], [fine[:, cut] for fine in fines])
                out_ref[pl.ds(spot, 1), :, cut] = far
            else:
                again = segment_factors(fields_ref[block, :, cut], fine_ref, coarse_ref)
                out_ref[pl.ds(spot, 1), :, cut] += reduced(sampled, *again)

        begin_all, finish_all = windows(fields_ref, ends, block, total_rows)
        begin_all(visit)
        rest.append((finish_all, visit))
    for finish_all, visit in rest:
        finish_all(visit)


def turn(value, step, size, sign):
    real, imag = value
    if step == 0:
        return value
    if 4 * step == size:
        return (-imag, real) if sign > 0 else (imag, -real)
    half = math.sqrt(0.5)
    if 8 * step == size:
        if sign > 0:
            return ((real - imag) * half, (real + imag) * half)
        return ((real + imag) * half, (imag - real) * half)
    cos = math.cos(2.0 * math.pi * step / size)
    sin = sign * math.sin(2.0 * math.pi * step / size)
    return (real * cos - imag * sin, real * sin + imag * cos)


def butterflies(values, sign):
    size = len(values)
    if size == 1:
        return values
    even = butterflies(values[0::2], sign)
    odd = butterflies(values[1::2], sign)
    low, high = [], []
    for k in range(size // 2):
        turned = turn(odd[k], k, size, sign)
        low.append((even[k][0] + turned[0], even[k][1] + turned[1]))
        high.append((even[k][0] - turned[0], even[k][1] - turned[1]))
    return low + high


def dense(value, matrix_ref):
    high, low = halves(value)
    return (
        jnp.dot(high, matrix_ref[0], preferred_element_type=f32)
        + jnp.dot(low, matrix_ref[0], preferred_element_type=f32)
        + jnp.dot(high, matrix_ref[1], preferred_element_type=f32)
    )


def mix(spec, kappa, keep, soil_ref, reflection):
    upper = (soil_ref[0, 0], soil_ref[1, 0])
    lower = (soil_ref[0, 1], soil_ref[1, 1])
    decay = jnp.exp(-kappa)
    base = jnp.where(keep, 1.0 / (GX * GY) / (kappa + screening), 0.0)
    source = []
    for layer in range(ZL):
        rho_re, rho_im = upper if layer < ZL // 2 else lower
        re, im = spec[layer]
        source.append(((rho_re * re - rho_im * im) * base, (rho_re * im + rho_im * re) * base))
    below = [None] * ZL
    below[ZL - 1] = (jnp.zeros_like(kappa), jnp.zeros_like(kappa))
    for layer in range(ZL - 2, -1, -1):
        below[layer] = tuple(decay * (below[layer + 1][i] + source[layer + 1][i]) for i in range(2))
    surface = tuple(decay * (below[0][i] + source[0][i]) for i in range(2))
    image = (
        reflection[0] * surface[0] - reflection[1] * surface[1],
        reflection[0] * surface[1] + reflection[1] * surface[0],
    )
    above = source[0]
    mixed = []
    for layer in range(ZL):
        if layer:
            above = tuple(decay * above[i] + source[layer][i] for i in range(2))
            image = tuple(decay * image[i] for i in range(2))
        mixed.append(tuple(above[i] + below[layer][i] + image[i] for i in range(2)))
    return mixed


def reflect(soil_ref, shape):
    upper_re, lower_re = (jnp.full(shape, soil_ref[0, i], f32) for i in range(2))
    upper_im, lower_im = (jnp.full(shape, soil_ref[1, i], f32) for i in range(2))
    denom_re, denom_im = upper_re + lower_re, upper_im + lower_im
    numer_re, numer_im = lower_re - upper_re, lower_im - upper_im
    magnitude = denom_re * denom_re + denom_im * denom_im
    return (
        (numer_re * denom_re + numer_im * denom_im) / magnitude,
        (numer_im * denom_re - numer_re * denom_im) / magnitude,
    )


def mix_kernel(place_ref, soil_ref, spec_ref, forward_ref, inverse_ref, twist_ref, out_ref, *, columns):
    tile = spec_ref.shape[2]
    rows = ZL * tile
    real = spec_ref[:, 0].reshape(rows, GX)
    imag = spec_ref[:, 1].reshape(rows, GX)
    cut = [slice(n * INNER, (n + 1) * INNER) for n in range(RADIX)]
    values = butterflies([(real[:, c], imag[:, c]) for c in cut], -1.0)
    local = pl.program_id(0) * tile + lax.broadcasted_iota(jnp.int32, (tile, INNER), 0)
    keep = local < columns
    ky = place_ref[2] + local
    reflection = reflect(soil_ref, (tile, INNER))
    freq_y = jnp.where(ky < (GY - 1) // 2 + 1, ky, ky - GY).astype(f32) / GY
    inner = lax.broadcasted_iota(jnp.int32, (tile, INNER), 1)
    back = []
    for k in range(RADIX):
        twist_re, twist_im = twist_ref[0, k : k + 1], twist_ref[1, k : k + 1]
        re, im = values[k]
        turned = (re * twist_re - im * twist_im, re * twist_im + im * twist_re) if k else (re, im)
        spectrum = dense(jnp.concatenate(turned, axis=1), forward_ref)
        kx = k + RADIX * inner
        freq_x = jnp.where(kx < (GX - 1) // 2 + 1, kx, kx - GX).astype(f32) / GX
        kappa = 2.0 * math.pi * jnp.sqrt(freq_x * freq_x + freq_y * freq_y)
        spec = [
            (spectrum[s * tile : (s + 1) * tile, :INNER], spectrum[s * tile : (s + 1) * tile, INNER:])
            for s in range(ZL)
        ]
        mixed = mix(spec, kappa, keep, soil_ref, reflection)
        stacked = jnp.concatenate([jnp.concatenate(pair, axis=1) for pair in mixed], axis=0)
        field = dense(stacked, inverse_ref)
        re, im = field[:, :INNER], field[:, INNER:]
        turned = (re * twist_re + im * twist_im, im * twist_re - re * twist_im) if k else (re, im)
        back.append(turned)
    values = butterflies(back, 1.0)
    for n in range(RADIX):
        out_ref[:, 0, :, cut[n]] = values[n][0].reshape(ZL, tile, INNER)
        out_ref[:, 1, :, cut[n]] = values[n][1].reshape(ZL, tile, INNER)


def partner(value, axis, step):
    count = lax.axis_size(axis)
    return lax.ppermute(value, axis, [(i, i ^ step) for i in range(count)])


def near_kernel(place_ref, pairs_ref, own_ref, corrections_ref, after_ref, out_ref):
    slots, _, size, _ = corrections_ref.shape
    pencils, _, segments = own_ref.shape
    blocks = segments // size
    out_ref[...] = jnp.zeros_like(out_ref)

    def add(slot, carry):
        target, source = pairs_ref[0, slot], pairs_ref[1, slot]
        live = pairs_ref[2, slot].astype(f32)
        pencil = jnp.clip(place_ref[0] + source // blocks - 1, 0, pencils - 1)
        index = pencil ^ place_ref[0]
        at = pl.ds(pl.multiple_of(source % blocks * size, size), size)
        current = own_ref[index, 21:23, at] * live
        real, imag = corrections_ref[slot, 0], corrections_ref[slot, 1]
        piece_re = real * current[0:1] - imag * current[1:2]
        piece_im = real * current[1:2] + imag * current[0:1]
        to = pl.ds(pl.multiple_of(target * size, size), size)
        out_ref[0:1, to] += jnp.sum(jnp.transpose(piece_re), axis=0, keepdims=True)
        out_ref[1:2, to] += jnp.sum(jnp.transpose(piece_im), axis=0, keepdims=True)
        return carry

    lax.fori_loop(0, slots, add, 0)


def shards(currents, stencil_cells, stencil_weights, soil, near_pairs, corrections):
    pencils = lax.axis_size("pencil")
    depths = lax.axis_size("depth")
    pencil = lax.axis_index("pencil")
    depth = lax.axis_index("depth")
    segments = currents.shape[1]
    layers = ZL // depths
    rows = GX // pencils
    repeats = LANES // rows
    groups = pencils * depths
    columns = GY // groups
    first = (pencil * depths + depth) * columns

    bits = [1 << i for i in range(pencils.bit_length() - 1)]
    if repeats == 1:
        bits = bits[:1] + bits[:0:-1]
    place = jnp.stack([pencil, depth, first]).astype(jnp.int32)
    params = pltpu.CompilerParams(vmem_limit_bytes=48 * 1024 * 1024)
    anywhere = pl.BlockSpec(memory_space=pl.ANY)
    scalars = pl.BlockSpec(memory_space=pltpu.SMEM)
    resident = pl.BlockSpec(memory_space=pltpu.VMEM)
    fields, rank = pl.pallas_call(
        functools.partial(order_kernel, rows=rows),
        in_specs=[scalars] + [pl.BlockSpec()] * 3,
        out_specs=[pl.BlockSpec()] * 2,
        out_shape=[
            jax.ShapeDtypeStruct((FIELDS, segments), f32),
            jax.ShapeDtypeStruct((1, segments), f32),
        ],
        compiler_params=pltpu.CompilerParams(vmem_limit_bytes=62 * 1024 * 1024),
    )(place, currents, stencil_cells, stencil_weights)


    def offset(index):
        return sum((index >> j & 1) * bit for j, bit in enumerate(bits))


    fine, coarse = column_tables()
    fine = lax.dynamic_slice_in_dim(
        jnp.asarray(np.pad(fine, ((0, 0), (0, COLUMNS), (0, 0)))), first, COLUMNS, axis=1
    ).reshape(2 * COLUMNS, -1)
    coarse = lax.dynamic_slice_in_dim(
        jnp.asarray(np.pad(coarse, ((0, 0), (0, COLUMNS), (0, 0)))), first, COLUMNS, axis=1
    ).reshape(2 * COLUMNS, -1)
    forward, inverse, twists = transform_tables()
    def fields_specs(together):
        return [
            pl.BlockSpec((together, FIELDS, segments), lambda i, place: (i, 0, 0)),
            pl.BlockSpec((together, 8, 128), lambda i, place: (i, 2, 0), memory_space=pltpu.SMEM),
        ]

    def lead(offsets, together):
        firsts = offsets[::together]
        if firsts == list(range(firsts[0], firsts[0] + len(offsets), together)):
            return lambda i: firsts[0] + together * i
        return lambda i: sum(jnp.where(i == k, first, 0) for k, first in enumerate(firsts))

    def region(offsets, step, together):
        wide = together if repeats == 1 else 1
        first = lead(offsets, together)
        return pl.BlockSpec(
            (layers, 2 * COLUMNS, LANES * wide),
            lambda i, place: (place[1] ^ step, 0, (place[0] ^ first(i)) // (repeats * wide)),
        )

    fine_spec = pl.BlockSpec(fine.shape, lambda i, place: (0, 0))
    coarse_spec = pl.BlockSpec(coarse.shape, lambda i, place: (0, 0))

    def cost(blocks):
        return pl.CostEstimate(
            flops=blocks * 2_000_000_000, bytes_accessed=blocks * 600_000, transcendentals=0
        )

    def spread(grid, chunk, offsets, step, together):
        fresh = grid is None
        if fresh and repeats > 1:
            grid, fresh = jnp.zeros((ZL, 2 * COLUMNS, GX), f32), False
        before = jnp.zeros((8, 128), f32) if fresh else grid
        return pl.pallas_call(
            functools.partial(spread_kernel, repeats=repeats, together=together),
            grid_spec=pltpu.PrefetchScalarGridSpec(
                num_scalar_prefetch=1,
                grid=(chunk.shape[0] // together,),
                in_specs=[
                    anywhere if repeats == 1 else region(offsets, step, together),
                    *fields_specs(together),
                    fine_spec,
                    coarse_spec,
                ],
                out_specs=region(offsets, step, together),
                scratch_shapes=[
                    pltpu.VMEM((16 * COLUMNS, segments), bf16),
                    pltpu.VMEM((2 * COLUMNS, layers * LANES), f32),
                ]
                * together,
            ),
            out_shape=jax.ShapeDtypeStruct((ZL, 2 * COLUMNS, GX), f32),
            input_output_aliases={} if fresh else {1: 0},
            compiler_params=params,
            cost_estimate=cost(chunk.shape[0]),
        )(place, before, chunk, chunk, fine, coarse)

    own, offsets, grid = fields[None], [0], None
    for number, bit in enumerate(bits):
        arrived = partner(own, "pencil", bit)
        fresh = [offset ^ bit for offset in offsets]
        known = len(offsets)
        offsets = offsets + fresh
        pieces, order = [], list(range(2 * known))
        if number == len(bits) - 1:
            order = [int(index) for index in np.argsort(np.array(offsets))]
        while order:
            run = 1
            while run < len(order) and order[run] == order[0] + run and order[run] != known:
                run += 1
            source, at = (own, order[0]) if order[0] < known else (arrived, order[0] - known)
            pieces.append(source[at : at + run])
            order = order[run:]
        own = jnp.concatenate(pieces)
        if number == 0:
            grid = spread(grid, own, offsets, 0, 2)
        else:
            grid = spread(grid, arrived, fresh, 0, 2)
    offsets = list(range(pencils))
    together = min(TOGETHER, pencils)
    parts = {0: own}
    for step in range(1, depths):
        if step & (step - 1) == 0:
            parts[step] = partner(own, "depth", step)
    for step in range(1, depths):
        grid = spread(grid, parts[step], offsets, step, together)
        later = step + 2
        if later < depths and later not in parts:
            low = later & -later
            source, grid = lax.optimization_barrier((parts[later ^ low], grid))
            parts[later] = partner(source, "depth", low)

    tile_spec = pl.BlockSpec((ZL, 2, TILE, GX), lambda t: (0, 0, t, 0))
    whole = lambda *shape: pl.BlockSpec(shape, lambda t: (0,) * len(shape))
    mixed = pl.pallas_call(
        functools.partial(mix_kernel, columns=columns),
        grid=(COLUMNS // TILE,),
        in_specs=[
            pl.BlockSpec(memory_space=pltpu.SMEM),
            pl.BlockSpec(memory_space=pltpu.SMEM),
            tile_spec,
            whole(*forward.shape),
            whole(*inverse.shape),
            whole(*twists.shape),
        ],
        out_specs=tile_spec,
        out_shape=jax.ShapeDtypeStruct((ZL, 2, COLUMNS, GX), f32),
        compiler_params=params,
    )(
        place,
        soil,
        grid.reshape(ZL, 2, COLUMNS, GX),
        jnp.asarray(forward),
        jnp.asarray(inverse),
        jnp.asarray(twists),
    ).reshape(ZL, 2 * COLUMNS, GX)
    turns = pencils // together
    wide = together if repeats == 1 else 1

    def part_specs(block, line, step, **kinds):
        return pl.BlockSpec(
            (together,) + block,
            lambda i, place: (jnp.clip(i - step * turns, 0, turns - 1), line, 0),
            **kinds,
        )

    partial = pl.pallas_call(
        functools.partial(sample_kernel, depths=depths, together=together),
        grid_spec=pltpu.PrefetchScalarGridSpec(
            num_scalar_prefetch=1,
            grid=(depths * turns,),
            in_specs=[part_specs((FIELDS, segments), 0, step) for step in range(depths)]
            + [
                part_specs((8, 128), 2, step, memory_space=pltpu.SMEM) for step in range(depths)
            ]
            + [
                pl.BlockSpec(
                    (layers, 2 * COLUMNS, LANES * wide),
                    lambda i, place: (
                        place[1] ^ (i // turns),
                        0,
                        (place[0] ^ (together * (i % turns))) // (repeats * wide),
                    ),
                ),
                fine_spec,
                coarse_spec,
            ],
            out_specs=pl.BlockSpec(
                (together, None, 2, segments),
                lambda i, place: (
                    (place[0] ^ (together * (i % turns))) // together,
                    place[1] ^ (i // turns),
                    0,
                    0,
                ),
            ),
            scratch_shapes=[pltpu.VMEM((together, FIELDS, segments), f32)]
            + [pltpu.VMEM((16 * COLUMNS, layers * LANES), bf16)] * together,
        ),
        out_shape=jax.ShapeDtypeStruct((pencils, depths, 2, segments), f32),
        compiler_params=params,
        cost_estimate=cost(groups),
    )(place, *[parts[k] for k in range(depths)], *[parts[k] for k in range(depths)], mixed, fine, coarse)
    partial = partial.reshape(groups, 2, segments)
    near = pl.pallas_call(
        near_kernel,
        in_specs=[scalars, scalars, pl.BlockSpec(), pl.BlockSpec(), anywhere],
        out_specs=pl.BlockSpec(),
        out_shape=jax.ShapeDtypeStruct((2, segments), f32),
        compiler_params=params,
        cost_estimate=cost(2),
    )(place, near_pairs, parts[0], corrections, partial)
    arrived = lax.all_to_all(partial, ("pencil", "depth"), split_axis=0, concat_axis=0, tiled=True)
    return pl.pallas_call(
        finish_kernel,
        in_specs=[resident, resident, resident],
        out_specs=resident,
        out_shape=jax.ShapeDtypeStruct((2, segments), f32),
        compiler_params=params,
    )(arrived, near, rank)


def solution(mesh):
    return jax.shard_map(
        shards,
        mesh=mesh,
        in_specs=(
            P(None, ("pencil", "depth")),
            P(None, ("pencil", "depth")),
            P(None, ("pencil", "depth")),
            P(),
            P(None, ("pencil", "depth")),
            P(("pencil", "depth"), None, None, None),
        ),
        out_specs=P(None, ("pencil", "depth")),
        check_vma=False,
    )
```

```python
import functools
import math

import jax
import jax.numpy as jnp
import ml_dtypes
import numpy as np
from jax import lax
from jax.experimental import pallas as pl
from jax.experimental.pallas import tpu as pltpu
from jax.sharding import PartitionSpec as P

GX = 2048
GY = 2048
ZL = 8

LANES = 256
INNER = 128
RADIX = GX // INNER
FINE = 16
SPAN = 24
COLUMNS = 64
FIELDS = 24
CHUNK = 256
REACH = LANES - 3
HOP = 128
TOGETHER = 4
TILE = 16

screening = 0.05
f32 = jnp.float32
bf16 = jnp.bfloat16


def halves(value):
    high = value.astype(bf16)
    return high, (value - high.astype(f32)).astype(bf16)


def host_halves(value):
    value = value.astype(np.float32)
    high = value.astype(ml_dtypes.bfloat16)
    return high, (value - high.astype(np.float32)).astype(ml_dtypes.bfloat16)


def column_tables():
    ky = np.arange(GY)[:, None]

    def table(offsets):
        phase = (ky * offsets[None, :] % GY) * (2.0 * math.pi / GY)
        return np.stack([np.cos(phase), -np.sin(phase)], axis=0)

    fine_high, fine_low = host_halves(table(np.arange(SPAN)))
    coarse_high, coarse_low = host_halves(table(FINE * np.arange(GY // FINE)))
    fine = np.concatenate([fine_high, fine_high, fine_low], axis=2)
    coarse = np.concatenate([coarse_high, coarse_low], axis=2)
    return fine, coarse


def transform_tables():
    index = np.arange(INNER)
    phase = (index[:, None] * index[None, :] % INNER) * (2.0 * math.pi / INNER)
    cos, sin = np.cos(phase), np.sin(phase)
    forward = np.block([[cos, -sin], [sin, cos]])
    twist = (np.arange(RADIX)[:, None] * index[None, :]) * (2.0 * math.pi / GX)
    twists = np.stack([np.cos(twist), -np.sin(twist)]).astype(np.float32)
    return np.stack(host_halves(forward)), np.stack(host_halves(forward.T)), twists


def one_hot(index, size):
    candidate = lax.broadcasted_iota(jnp.int16, (size, index.shape[1]), 0)
    return jnp.where(candidate == index.astype(jnp.int16), bf16(1), bf16(0))


def segment_factors(fields, fine_ref, coarse_ref):
    count = fields.shape[1]
    column = fields[19:20].astype(jnp.int32)
    pick = one_hot(column // FINE, GY // FINE)
    coarse = jnp.dot(
        coarse_ref[...], jnp.concatenate([pick, pick], axis=0), preferred_element_type=f32
    )
    fine_index = lax.broadcasted_iota(jnp.int32, (SPAN, count), 0) - column % FINE
    at = [fine_index == offset for offset in range(4)]
    parts = []
    for a in range(4):
        spread = jnp.zeros((SPAN, count), f32)
        for b in range(4):
            spread = jnp.where(at[b], fields[4 * a + b : 4 * a + b + 1], spread)
        high = spread.astype(bf16).astype(f32)
        parts.append(jnp.concatenate([high, spread - high, high], axis=0).astype(bf16))
    fine = jnp.dot(fine_ref[...], jnp.concatenate(parts, axis=1), preferred_element_type=f32)
    fines = [fine[:, a * count : (a + 1) * count] for a in range(4)]
    return coarse, fines


def moved(value, pick, form):
    rows = value.shape[0]
    high = value.astype(bf16).astype(f32)
    middle = (value - high).astype(bf16).astype(f32)
    pieces = jnp.concatenate([high, middle, value - high - middle], axis=0).astype(bf16)
    out = lax.dot_general(pieces, pick, (form, ((), ())), preferred_element_type=f32)
    return out[:rows] + out[rows : 2 * rows] + out[2 * rows :]


def order_kernel(place_ref, currents_ref, cells_ref, weights_ref, fields_ref, rank_ref, *, rows):
    count = currents_ref.shape[1]
    local = cells_ref[0:1]
    repeats = LANES // rows
    row = local // rows * LANES + place_ref[0] % repeats * rows + local % rows
    lane = lax.broadcasted_iota(jnp.int32, (1, count), 1)
    key = (row * count + lane).astype(f32)
    column = jnp.transpose(jnp.broadcast_to(key, (8, count)))[:, :1]
    rank = jnp.sum(jnp.where(column < key, 1.0, 0.0), axis=0, keepdims=True)
    pick = one_hot(rank.astype(jnp.int32), count)
    values = jnp.concatenate(
        [
            weights_ref[...],
            currents_ref[...],
            row.astype(f32),
            cells_ref[1:2].astype(f32),
            jnp.zeros((FIELDS - 20, count), f32),
        ],
        axis=0,
    )
    ordered = moved(values, pick, ((1,), (1,)))
    ends = jnp.zeros((1, count), f32)
    for chunk in range(count // CHUNK):
        for side in range(2):
            at = lane == chunk * CHUNK + side * (CHUNK - 1)
            value = jnp.sum(jnp.where(at, ordered[18:19], 0.0), axis=1, keepdims=True)
            ends = ends + jnp.where(lane == 2 * chunk + side, value, 0.0)
    line = lax.broadcasted_iota(jnp.int32, (FIELDS, count), 0)
    ordered = jnp.where(line == 20, ends, ordered)
    for part in range(2):
        ordered = jnp.where(line == 21 + part, currents_ref[part : part + 1], ordered)
    fields_ref[...] = ordered
    rank_ref[...] = rank


def finish_kernel(arrived_ref, near_ref, rank_ref, out_ref):
    far = jnp.sum(arrived_ref[...], axis=0)
    count = far.shape[1]
    pick = one_hot(rank_ref[...].astype(jnp.int32), count)
    padded = jnp.concatenate([far, jnp.zeros((6, count), f32)], axis=0)
    total = moved(padded, pick, ((1,), (0,)))
    out_ref[...] = total[:2] + near_ref[...]


def windows(fields_ref, ends, block, total_rows):
    chunks = []
    for chunk in range(fields_ref.shape[2] // CHUNK):
        low = ends(block, 2 * chunk).astype(jnp.int32)
        high = ends(block, 2 * chunk + 1).astype(jnp.int32)
        start = jnp.minimum(low // HOP * HOP, total_rows - LANES)
        more = (jnp.maximum(high + 1 - (start + REACH), 0) + HOP - 1) // HOP
        chunks.append((start, more))

    def window(chunk, number, visit):
        first = isinstance(number, int)
        row = fields_ref[block, 18:19, chunk * CHUNK : (chunk + 1) * CHUNK].astype(jnp.int32)
        begin = pl.multiple_of(chunks[chunk][0] + number * HOP, HOP)
        apart = row - begin
        inside = (apart >= (0 if first else REACH - HOP)) & (apart < REACH)
        visit(chunk, begin, one_hot(jnp.where(inside, apart, -1), LANES), first)

    def begin_all(visit):
        for chunk in range(len(chunks)):
            window(chunk, 0, visit)

    def finish_all(visit):
        @pl.when(sum(more for _, more in chunks) > 0)
        def _():
            for chunk in range(len(chunks)):

                def again(number, carry, chunk=chunk):
                    window(chunk, number, visit)
                    return carry

                lax.fori_loop(1, chunks[chunk][1] + 1, again, 0)

    return begin_all, finish_all


def spread_kernel(
    place_ref, before_ref, fields_ref, ends_ref, fine_ref, coarse_ref, out_ref, *scratch, repeats, together
):
    layers = out_ref.shape[0]
    half = 8 * COLUMNS
    rest = []
    for block in range(together):
        factor_ref, total_ref = scratch[2 * block : 2 * block + 2]
        fields = fields_ref[block]
        coarse, fines = segment_factors(fields, fine_ref, coarse_ref)
        current_re, current_im = fields[16:17], fields[17:18]
        phase_re, phase_im = coarse[:COLUMNS], coarse[COLUMNS:]
        wave_re = phase_re * current_re - phase_im * current_im
        wave_im = phase_re * current_im + phase_im * current_re
        base = 0
        for fine in fines:
            fine_re, fine_im = fine[:COLUMNS], fine[COLUMNS:]
            for value in (
                wave_re * fine_re - wave_im * fine_im,
                wave_re * fine_im + wave_im * fine_re,
            ):
                high, low = halves(value)
                factor_ref[base : base + COLUMNS] = high
                factor_ref[half + base : half + base + COLUMNS] = low
                base += COLUMNS
        total_ref[...] = jnp.zeros_like(total_ref)

        def visit(chunk, begin, select, first, factor_ref=factor_ref, total_ref=total_ref):
            factors = factor_ref[:, chunk * CHUNK : (chunk + 1) * CHUNK]
            form = (((1,), (1,)), ((), ()))
            spread = lax.dot_general(factors, select, form, preferred_element_type=f32)
            spread = spread[:half] + spread[half:]
            total = spread[: 2 * COLUMNS]
            for a in range(1, 4):
                total = total + pltpu.roll(spread[2 * COLUMNS * a : 2 * COLUMNS * (a + 1)], a, 1)
            total_ref[:, pl.ds(begin, LANES)] += total

        begin_all, finish_all = windows(
            fields_ref, lambda block, at: ends_ref[block, 4, at], block, layers * LANES
        )
        begin_all(visit)
        rest.append((finish_all, visit))
    for finish_all, visit in rest:
        finish_all(visit)
    fresh = pl.program_id(0) * together % min(repeats, pl.num_programs(0) * together) == 0
    for layer in range(layers):
        pieces = [
            scratch[2 * block + 1][:, layer * LANES : (layer + 1) * LANES]
            for block in range(together)
        ]
        if repeats == 1:
            for block, piece in enumerate(pieces):
                spot = (place_ref[0] % together) ^ block
                out_ref[layer, :, pl.ds(pl.multiple_of(spot * LANES, LANES), LANES)] = piece
        else:
            out_ref[layer] = jnp.where(fresh, before_ref[layer], out_ref[layer]) + sum(pieces)


def sample_kernel(place_ref, *refs, depths, together):
    parts, ends_refs, refs = refs[:depths], refs[depths : 2 * depths], refs[2 * depths :]
    field_ref, fine_ref, coarse_ref, out_ref, fields_ref, *scratch = refs
    turn_now = pl.program_id(0) // (pl.num_programs(0) // depths)
    for step in range(depths):

        @pl.when(turn_now == step)
        def _(step=step):
            fields_ref[...] = parts[step][...]

    def ends(block, at):
        value = ends_refs[0][block, 4, at]
        for step in range(1, depths):
            value = jnp.where(turn_now == step, ends_refs[step][block, 4, at], value)
        return value

    layers = field_ref.shape[0]
    total_rows = layers * LANES
    half = 8 * COLUMNS

    def reduced(sampled, coarse, fines):
        sum_re, sum_im = 0.0, 0.0
        for a, fine in enumerate(fines):
            fine_re, fine_im = fine[:COLUMNS], fine[COLUMNS:]
            base = 2 * COLUMNS * a
            value_re = sampled[base : base + COLUMNS]
            value_im = sampled[base + COLUMNS : base + 2 * COLUMNS]
            sum_re = sum_re + value_re * fine_re + value_im * fine_im
            sum_im = sum_im + value_im * fine_re - value_re * fine_im
        phase_re, phase_im = coarse[:COLUMNS], coarse[COLUMNS:]
        far_re = jnp.sum(sum_re * phase_re + sum_im * phase_im, axis=0, keepdims=True)
        far_im = jnp.sum(sum_im * phase_re - sum_re * phase_im, axis=0, keepdims=True)
        return jnp.concatenate([far_re, far_im], axis=0)[None]

    rest = []
    for block in range(together):
        factor_ref = scratch[block]
        spot = (place_ref[0] % together) ^ block
        if field_ref.shape[2] == LANES:
            at = pl.ds(0, LANES)
        else:
            at = pl.ds(pl.multiple_of(spot * LANES, LANES), LANES)
        field = jnp.concatenate([field_ref[layer, :, at] for layer in range(layers)], axis=1)
        for a in range(4):
            shifted = pltpu.roll(field, total_rows - a, 1) if a else field
            high, low = halves(shifted)
            base = 2 * COLUMNS * a
            factor_ref[base : base + 2 * COLUMNS] = high
            factor_ref[half + base : half + base + 2 * COLUMNS] = low
        coarse, fines = segment_factors(fields_ref[block], fine_ref, coarse_ref)

        def visit(
            chunk,
            begin,
            select,
            first,
            block=block,
            factor_ref=factor_ref,
            spot=spot,
            coarse=coarse,
            fines=fines,
        ):
            sampled = jnp.dot(
                factor_ref[:, pl.ds(begin, LANES)], select, preferred_element_type=f32
            )
            sampled = sampled[:half] + sampled[half:]
            cut = slice(chunk * CHUNK, (chunk + 1) * CHUNK)
            if first:
                far = reduced(sampled, coarse[:, cut], [fine[:, cut] for fine in fines])
                out_ref[pl.ds(spot, 1), :, cut] = far
            else:
                again = segment_factors(fields_ref[block, :, cut], fine_ref, coarse_ref)
                out_ref[pl.ds(spot, 1), :, cut] += reduced(sampled, *again)

        begin_all, finish_all = windows(fields_ref, ends, block, total_rows)
        begin_all(visit)
        rest.append((finish_all, visit))
    for finish_all, visit in rest:
        finish_all(visit)


def turn(value, step, size, sign):
    real, imag = value
    if step == 0:
        return value
    if 4 * step == size:
        return (-imag, real) if sign > 0 else (imag, -real)
    half = math.sqrt(0.5)
    if 8 * step == size:
        if sign > 0:
            return ((real - imag) * half, (real + imag) * half)
        return ((real + imag) * half, (imag - real) * half)
    cos = math.cos(2.0 * math.pi * step / size)
    sin = sign * math.sin(2.0 * math.pi * step / size)
    return (real * cos - imag * sin, real * sin + imag * cos)


def butterflies(values, sign):
    size = len(values)
    if size == 1:
        return values
    even = butterflies(values[0::2], sign)
    odd = butterflies(values[1::2], sign)
    low, high = [], []
    for k in range(size // 2):
        turned = turn(odd[k], k, size, sign)
        low.append((even[k][0] + turned[0], even[k][1] + turned[1]))
        high.append((even[k][0] - turned[0], even[k][1] - turned[1]))
    return low + high


def dense(value, matrix_ref):
    high, low = halves(value)
    return (
        jnp.dot(high, matrix_ref[0], preferred_element_type=f32)
        + jnp.dot(low, matrix_ref[0], preferred_element_type=f32)
        + jnp.dot(high, matrix_ref[1], preferred_element_type=f32)
    )


def mix(spec, kappa, keep, soil_ref, reflection):
    upper = (soil_ref[0, 0], soil_ref[1, 0])
    lower = (soil_ref[0, 1], soil_ref[1, 1])
    decay = jnp.exp(-kappa)
    base = jnp.where(keep, 1.0 / (GX * GY) / (kappa + screening), 0.0)
    source = []
    for layer in range(ZL):
        rho_re, rho_im = upper if layer < ZL // 2 else lower
        re, im = spec[layer]
        source.append(((rho_re * re - rho_im * im) * base, (rho_re * im + rho_im * re) * base))
    below = [None] * ZL
    below[ZL - 1] = (jnp.zeros_like(kappa), jnp.zeros_like(kappa))
    for layer in range(ZL - 2, -1, -1):
        below[layer] = tuple(decay * (below[layer + 1][i] + source[layer + 1][i]) for i in range(2))
    surface = tuple(decay * (below[0][i] + source[0][i]) for i in range(2))
    image = (
        reflection[0] * surface[0] - reflection[1] * surface[1],
        reflection[0] * surface[1] + reflection[1] * surface[0],
    )
    above = source[0]
    mixed = []
    for layer in range(ZL):
        if layer:
            above = tuple(decay * above[i] + source[layer][i] for i in range(2))
            image = tuple(decay * image[i] for i in range(2))
        mixed.append(tuple(above[i] + below[layer][i] + image[i] for i in range(2)))
    return mixed


def reflect(soil_ref, shape):
    upper_re, lower_re = (jnp.full(shape, soil_ref[0, i], f32) for i in range(2))
    upper_im, lower_im = (jnp.full(shape, soil_ref[1, i], f32) for i in range(2))
    denom_re, denom_im = upper_re + lower_re, upper_im + lower_im
    numer_re, numer_im = lower_re - upper_re, lower_im - upper_im
    magnitude = denom_re * denom_re + denom_im * denom_im
    return (
        (numer_re * denom_re + numer_im * denom_im) / magnitude,
        (numer_im * denom_re - numer_re * denom_im) / magnitude,
    )


def mix_kernel(place_ref, soil_ref, spec_ref, forward_ref, inverse_ref, twist_ref, out_ref, *, columns):
    tile = spec_ref.shape[2]
    rows = ZL * tile
    real = spec_ref[:, 0].reshape(rows, GX)
    imag = spec_ref[:, 1].reshape(rows, GX)
    cut = [slice(n * INNER, (n + 1) * INNER) for n in range(RADIX)]
    values = butterflies([(real[:, c], imag[:, c]) for c in cut], -1.0)
    local = pl.program_id(0) * tile + lax.broadcasted_iota(jnp.int32, (tile, INNER), 0)
    keep = local < columns
    ky = place_ref[2] + local
    reflection = reflect(soil_ref, (tile, INNER))
    freq_y = jnp.where(ky < (GY - 1) // 2 + 1, ky, ky - GY).astype(f32) / GY
    inner = lax.broadcasted_iota(jnp.int32, (tile, INNER), 1)
    back = []
    for k in range(RADIX):
        twist_re, twist_im = twist_ref[0, k : k + 1], twist_ref[1, k : k + 1]
        re, im = values[k]
        turned = (re * twist_re - im * twist_im, re * twist_im + im * twist_re) if k else (re, im)
        spectrum = dense(jnp.concatenate(turned, axis=1), forward_ref)
        kx = k + RADIX * inner
        freq_x = jnp.where(kx < (GX - 1) // 2 + 1, kx, kx - GX).astype(f32) / GX
        kappa = 2.0 * math.pi * jnp.sqrt(freq_x * freq_x + freq_y * freq_y)
        spec = [
            (spectrum[s * tile : (s + 1) * tile, :INNER], spectrum[s * tile : (s + 1) * tile, INNER:])
            for s in range(ZL)
        ]
        mixed = mix(spec, kappa, keep, soil_ref, reflection)
        stacked = jnp.concatenate([jnp.concatenate(pair, axis=1) for pair in mixed], axis=0)
        field = dense(stacked, inverse_ref)
        re, im = field[:, :INNER], field[:, INNER:]
        turned = (re * twist_re + im * twist_im, im * twist_re - re * twist_im) if k else (re, im)
        back.append(turned)
    values = butterflies(back, 1.0)
    for n in range(RADIX):
        out_ref[:, 0, :, cut[n]] = values[n][0].reshape(ZL, tile, INNER)
        out_ref[:, 1, :, cut[n]] = values[n][1].reshape(ZL, tile, INNER)


def partner(value, axis, step):
    count = lax.axis_size(axis)
    return lax.ppermute(value, axis, [(i, i ^ step) for i in range(count)])


def near_kernel(place_ref, pairs_ref, own_ref, corrections_ref, after_ref, out_ref):
    slots, _, size, _ = corrections_ref.shape
    pencils, _, segments = own_ref.shape
    blocks = segments // size
    out_ref[...] = jnp.zeros_like(out_ref)

    def add(slot, carry):
        target, source = pairs_ref[0, slot], pairs_ref[1, slot]
        live = pairs_ref[2, slot].astype(f32)
        pencil = jnp.clip(place_ref[0] + source // blocks - 1, 0, pencils - 1)
        index = pencil ^ place_ref[0]
        at = pl.ds(pl.multiple_of(source % blocks * size, size), size)
        current = own_ref[index, 21:23, at] * live
        real, imag = corrections_ref[slot, 0], corrections_ref[slot, 1]
        piece_re = real * current[0:1] - imag * current[1:2]
        piece_im = real * current[1:2] + imag * current[0:1]
        to = pl.ds(pl.multiple_of(target * size, size), size)
        out_ref[0:1, to] += jnp.sum(jnp.transpose(piece_re), axis=0, keepdims=True)
        out_ref[1:2, to] += jnp.sum(jnp.transpose(piece_im), axis=0, keepdims=True)
        return carry

    lax.fori_loop(0, slots, add, 0)


def shards(currents, stencil_cells, stencil_weights, soil, near_pairs, corrections):
    pencils = lax.axis_size("pencil")
    depths = lax.axis_size("depth")
    pencil = lax.axis_index("pencil")
    depth = lax.axis_index("depth")
    segments = currents.shape[1]
    layers = ZL // depths
    rows = GX // pencils
    repeats = LANES // rows
    groups = pencils * depths
    columns = GY // groups
    first = (pencil * depths + depth) * columns

    bits = [1 << i for i in range(pencils.bit_length() - 1)]
    if repeats == 1:
        bits = bits[:1] + bits[:0:-1]
    place = jnp.stack([pencil, depth, first]).astype(jnp.int32)
    params = pltpu.CompilerParams(vmem_limit_bytes=48 * 1024 * 1024)
    anywhere = pl.BlockSpec(memory_space=pl.ANY)
    scalars = pl.BlockSpec(memory_space=pltpu.SMEM)
    resident = pl.BlockSpec(memory_space=pltpu.VMEM)
    fields, rank = pl.pallas_call(
        functools.partial(order_kernel, rows=rows),
        in_specs=[scalars] + [pl.BlockSpec()] * 3,
        out_specs=[pl.BlockSpec()] * 2,
        out_shape=[
            jax.ShapeDtypeStruct((FIELDS, segments), f32),
            jax.ShapeDtypeStruct((1, segments), f32),
        ],
        compiler_params=pltpu.CompilerParams(vmem_limit_bytes=62 * 1024 * 1024),
    )(place, currents, stencil_cells, stencil_weights)


    def offset(index):
        return sum((index >> j & 1) * bit for j, bit in enumerate(bits))


    fine, coarse = column_tables()
    fine = lax.dynamic_slice_in_dim(
        jnp.asarray(np.pad(fine, ((0, 0), (0, COLUMNS), (0, 0)))), first, COLUMNS, axis=1
    ).reshape(2 * COLUMNS, -1)
    coarse = lax.dynamic_slice_in_dim(
        jnp.asarray(np.pad(coarse, ((0, 0), (0, COLUMNS), (0, 0)))), first, COLUMNS, axis=1
    ).reshape(2 * COLUMNS, -1)
    forward, inverse, twists = transform_tables()
    def fields_specs(together):
        return [
            pl.BlockSpec((together, FIELDS, segments), lambda i, place: (i, 0, 0)),
            pl.BlockSpec((together, 8, 128), lambda i, place: (i, 2, 0), memory_space=pltpu.SMEM),
        ]

    def lead(offsets, together):
        firsts = offsets[::together]
        if firsts == list(range(firsts[0], firsts[0] + len(offsets), together)):
            return lambda i: firsts[0] + together * i
        return lambda i: sum(jnp.where(i == k, first, 0) for k, first in enumerate(firsts))

    def region(offsets, step, together):
        wide = together if repeats == 1 else 1
        first = lead(offsets, together)
        return pl.BlockSpec(
            (layers, 2 * COLUMNS, LANES * wide),
            lambda i, place: (place[1] ^ step, 0, (place[0] ^ first(i)) // (repeats * wide)),
        )

    fine_spec = pl.BlockSpec(fine.shape, lambda i, place: (0, 0))
    coarse_spec = pl.BlockSpec(coarse.shape, lambda i, place: (0, 0))

    def cost(blocks):
        return pl.CostEstimate(
            flops=blocks * 2_000_000_000, bytes_accessed=blocks * 600_000, transcendentals=0
        )

    def spread(grid, chunk, offsets, step, together):
        fresh = grid is None
        if fresh and repeats > 1:
            grid, fresh = jnp.zeros((ZL, 2 * COLUMNS, GX), f32), False
        before = jnp.zeros((8, 128), f32) if fresh else grid
        return pl.pallas_call(
            functools.partial(spread_kernel, repeats=repeats, together=together),
            grid_spec=pltpu.PrefetchScalarGridSpec(
                num_scalar_prefetch=1,
                grid=(chunk.shape[0] // together,),
                in_specs=[
                    anywhere if repeats == 1 else region(offsets, step, together),
                    *fields_specs(together),
                    fine_spec,
                    coarse_spec,
                ],
                out_specs=region(offsets, step, together),
                scratch_shapes=[
                    pltpu.VMEM((16 * COLUMNS, segments), bf16),
                    pltpu.VMEM((2 * COLUMNS, layers * LANES), f32),
                ]
                * together,
            ),
            out_shape=jax.ShapeDtypeStruct((ZL, 2 * COLUMNS, GX), f32),
            input_output_aliases={} if fresh else {1: 0},
            compiler_params=params,
            cost_estimate=cost(chunk.shape[0]),
        )(place, before, chunk, chunk, fine, coarse)

    own, offsets, grid = fields[None], [0], None
    for number, bit in enumerate(bits):
        arrived = partner(own, "pencil", bit)
        fresh = [offset ^ bit for offset in offsets]
        known = len(offsets)
        offsets = offsets + fresh
        pieces, order = [], list(range(2 * known))
        if number == len(bits) - 1:
            order = [int(index) for index in np.argsort(np.array(offsets))]
        while order:
            run = 1
            while run < len(order) and order[run] == order[0] + run and order[run] != known:
                run += 1
            source, at = (own, order[0]) if order[0] < known else (arrived, order[0] - known)
            pieces.append(source[at : at + run])
            order = order[run:]
        own = jnp.concatenate(pieces)
        if number == 0:
            grid = spread(grid, own, offsets, 0, 2)
        else:
            grid = spread(grid, arrived, fresh, 0, 2)
    offsets = list(range(pencils))
    together = min(TOGETHER, pencils)
    parts = {0: own}
    for step in range(1, depths):
        if step & (step - 1) == 0:
            parts[step] = partner(own, "depth", step)
    for step in range(1, depths):
        grid = spread(grid, parts[step], offsets, step, together)
        later = step + 2
        if later < depths and later not in parts:
            low = later & -later
            source, grid = lax.optimization_barrier((parts[later ^ low], grid))
            parts[later] = partner(source, "depth", low)

    tile_spec = pl.BlockSpec((ZL, 2, TILE, GX), lambda t: (0, 0, t, 0))
    whole = lambda *shape: pl.BlockSpec(shape, lambda t: (0,) * len(shape))
    mixed = pl.pallas_call(
        functools.partial(mix_kernel, columns=columns),
        grid=(COLUMNS // TILE,),
        in_specs=[
            pl.BlockSpec(memory_space=pltpu.SMEM),
            pl.BlockSpec(memory_space=pltpu.SMEM),
            tile_spec,
            whole(*forward.shape),
            whole(*inverse.shape),
            whole(*twists.shape),
        ],
        out_specs=tile_spec,
        out_shape=jax.ShapeDtypeStruct((ZL, 2, COLUMNS, GX), f32),
        compiler_params=params,
    )(
        place,
        soil,
        grid.reshape(ZL, 2, COLUMNS, GX),
        jnp.asarray(forward),
        jnp.asarray(inverse),
        jnp.asarray(twists),
    ).reshape(ZL, 2 * COLUMNS, GX)
    turns = pencils // together
    wide = together if repeats == 1 else 1

    def part_specs(block, line, step, **kinds):
        return pl.BlockSpec(
            (together,) + block,
            lambda i, place: (jnp.clip(i - step * turns, 0, turns - 1), line, 0),
            **kinds,
        )

    partial = pl.pallas_call(
        functools.partial(sample_kernel, depths=depths, together=together),
        grid_spec=pltpu.PrefetchScalarGridSpec(
            num_scalar_prefetch=1,
            grid=(depths * turns,),
            in_specs=[part_specs((FIELDS, segments), 0, step) for step in range(depths)]
            + [
                part_specs((8, 128), 2, step, memory_space=pltpu.SMEM) for step in range(depths)
            ]
            + [
                pl.BlockSpec(
                    (layers, 2 * COLUMNS, LANES * wide),
                    lambda i, place: (
                        place[1] ^ (i // turns),
                        0,
                        (place[0] ^ (together * (i % turns))) // (repeats * wide),
                    ),
                ),
                fine_spec,
                coarse_spec,
            ],
            out_specs=pl.BlockSpec(
                (together, None, 2, segments),
                lambda i, place: (
                    (place[0] ^ (together * (i % turns))) // together,
                    place[1] ^ (i // turns),
                    0,
                    0,
                ),
            ),
            scratch_shapes=[pltpu.VMEM((together, FIELDS, segments), f32)]
            + [pltpu.VMEM((16 * COLUMNS, layers * LANES), bf16)] * together,
        ),
        out_shape=jax.ShapeDtypeStruct((pencils, depths, 2, segments), f32),
        compiler_params=params,
        cost_estimate=cost(groups),
    )(place, *[parts[k] for k in range(depths)], *[parts[k] for k in range(depths)], mixed, fine, coarse)
    partial = partial.reshape(groups, 2, segments)
    near = pl.pallas_call(
        near_kernel,
        in_specs=[scalars, scalars, pl.BlockSpec(), pl.BlockSpec(), anywhere],
        out_specs=pl.BlockSpec(),
        out_shape=jax.ShapeDtypeStruct((2, segments), f32),
        compiler_params=params,
        cost_estimate=cost(2),
    )(place, near_pairs, parts[0], corrections, partial)
    arrived = lax.all_to_all(partial, ("pencil", "depth"), split_axis=0, concat_axis=0, tiled=True)
    return pl.pallas_call(
        finish_kernel,
        in_specs=[resident, resident, resident],
        out_specs=resident,
        out_shape=jax.ShapeDtypeStruct((2, segments), f32),
        compiler_params=params,
    )(arrived, near, rank)


def solution(mesh):
    return jax.shard_map(
        shards,
        mesh=mesh,
        in_specs=(
            P(None, ("pencil", "depth")),
            P(None, ("pencil", "depth")),
            P(None, ("pencil", "depth")),
            P(),
            P(None, ("pencil", "depth")),
            P(("pencil", "depth"), None, None, None),
        ),
        out_specs=P(None, ("pencil", "depth")),
        check_vma=False,
    )
```
